32 devices in a mesh: seq: 4 (over x, core), dp: 8 (over z, y).
Axes of the slice: x: 2, y: 2, z: 4, core: 2. Of those that a mesh axis runs over, the one named last changes fastest.
Arguments:
- tokens: bfloat16 [8, 2048, 640], P('dp', 'seq'), may hold values from -6 to 6
- cotangent: bfloat16 [8, 2048, 640], P('dp', 'seq'), may hold values from -6 to 6
- quarters: int32 [8, 4], P('dp'), may hold values from 1 to 256, 512 in all within a row
- qkv_weight: bfloat16 [640, 1920], P(None, 'seq'), may hold values from -0.3125 to 0.3125
- qkv_bias: bfloat16 [1920], P('seq'), may hold values from -3 to 3
- out_weight: bfloat16 [640, 640], P(None, 'seq'), may hold values from -1 to 1
- out_bias: bfloat16 [640], P('seq'), may hold values from -3 to 3
- attn_gain: bfloat16 [640], P('seq'), may hold values from 0.5 to 1.5
- attn_shift: bfloat16 [640], P('seq'), may hold values from -3 to 3
- ffn_gain: bfloat16 [640], P('seq'), may hold values from 0.5 to 1.5
- ffn_shift: bfloat16 [640], P('seq'), may hold values from -3 to 3
- up_weight: bfloat16 [640, 2560], P(None, 'seq'), may hold values from -0.25 to 0.25
- up_bias: bfloat16 [2560], P('seq'), may hold values from -3 to 3
- down_weight: bfloat16 [2560, 640], P('seq'), may hold values from -0.125 to 0.125
- down_bias: bfloat16 [640], P('seq'), may hold values from -3 to 3
Outputs:
- out_tokens: bfloat16 [8, 2048, 640], P('dp', 'seq')
- grad_tokens: float32 [8, 2048, 640], P('dp', 'seq')
- qkv_weight_grad: float32 [640, 1920], P(None, 'seq')
- qkv_bias_grad: float32 [1920], P('seq')
- out_weight_grad: float32 [640, 640], P(None, 'seq')
- out_bias_grad: float32 [640], P('seq')
- attn_gain_grad: float32 [640], P('seq')
- attn_shift_grad: float32 [640], P('seq')
- ffn_gain_grad: float32 [640], P('seq')
- ffn_shift_grad: float32 [640], P('seq')
- up_weight_grad: float32 [640, 2560], P(None, 'seq')
- up_bias_grad: float32 [2560], P('seq')
- down_weight_grad: float32 [2560, 640], P('seq')
- down_bias_grad: float32 [640], P('seq')
The draws below stay inside these ranges and needn't reach their ends.
Inputs may be any that keep to these rules, and one draw needn't show every extreme that they name: `quarters`: each row sums to 512; in every group one crop has exactly 256 rows on each device.
All inputs are finite; a program needn't handle non-finite values.
Results may differ from the reference program's by a relative error of at most 0.018.
The reference program's roundings to bfloat16 on the way count: a program that leaves them out, or rounds other values in their place, can miss the bound.
Values may be sent and summed in bfloat16 or wider, within the bound.
No kernel may reach another device: no remote copies, remote signals or barrier semaphores. Data moves between devices by JAX's collectives and lax.ppermute only.
A program may use at most 192 MiB of HBM per device.

```python
import math
import jax
import jax.numpy as jnp
import numpy as np
from jax import lax

D = 640
HEADS = 20
HEAD_DIM = 32
FF = 2560
TOK_DEV = 512
CROPS = 4
MAX_Q = 256
GROUPS = 8
GROUP_TOK = 2048
N_SEQ = 4


def shard_levels(stream_key, dims, split, low, top_value):
    def one(dim, blocks):
        steps = jax.random.uniform(jax.random.fold_in(jax.random.fold_in(stream_key, 6), dim), (blocks,), jnp.float32, low / len(split), top_value / len(split))
        return jnp.repeat(jnp.exp(steps), dims[dim] // blocks).reshape((-1,) + (1,) * (len(dims) - dim - 1))

    level = one(*split[0])
    for cut in split[1:]:
        level = level * one(*cut)
    return level


def length_profile(count, total, most, skew):
    weights = [(1 << 20) // math.isqrt(grade ** skew) + 1 for grade in range(2, count + 1)]
    surplus, holding = total - most - (count - 1), [1] * (count - 1)
    while surplus > 0:
        candidates = [i for i in range(count - 1) if holding[i] < most]
        mass, budget = sum([weights[i] for i in candidates]), surplus
        for i in candidates:
            more = min(most - holding[i], max(1, budget * weights[i] // mass), surplus)
            holding[i] = holding[i] + more
            surplus = surplus - more
    return np.array([most] + holding)


def ragged_sizes(rng, amount, total, reach, lean):
    if amount == 2:
        one = jax.random.randint(rng, (), max(1, total - reach), min(reach, total - 1) + 1)
        return jnp.stack([one, total - one])
    sizes = jnp.asarray(length_profile(amount, total, reach, lean), jnp.int32)
    pairs = (amount - 1) // 2
    donor, taker = sizes[1:1 + 2 * pairs:2], sizes[2:2 + 2 * pairs:2]
    margin = jnp.minimum(donor - 1, reach - taker)
    moved = jax.random.randint(jax.random.fold_in(rng, 1), (pairs,), 0, 1 << 20) % (margin + 1)
    sizes = sizes.at[1:1 + 2 * pairs:2].set(donor - moved).at[2:2 + 2 * pairs:2].set(taker + moved)
    return sizes[jax.random.permutation(jax.random.fold_in(rng, 2), amount)]


def scatter_about(rng, extent, deviation, most, cuts=(), kind=jnp.bfloat16):
    values = deviation * jax.random.normal(rng, extent, jnp.float32)
    if cuts:
        values = values * shard_levels(rng, extent, cuts, -0.22, 0.18)
    return jnp.clip(values, -most, most).astype(kind)


def setup_inputs(seed: int = 0) -> dict:
    key_of = jax.random.split(jax.random.key(seed), 16)
    return {
        "tokens": scatter_about(key_of[0], (GROUPS, GROUP_TOK, D), 1.0, 6.0, ((0, 8), (1, 4))),
        "cotangent": scatter_about(key_of[1], (GROUPS, GROUP_TOK, D), 1.0, 6.0, ((0, 8), (1, 4))),
        "quarters": jax.vmap(lambda own: ragged_sizes(own, CROPS, TOK_DEV, MAX_Q, 2))(jax.random.split(key_of[2], GROUPS)).reshape((GROUPS, CROPS)).astype(jnp.int32),
        "qkv_weight": scatter_about(key_of[3], (D, 3 * D), (D // 2) ** -0.5, 0.3125, ((1, 4),)),
        "qkv_bias": scatter_about(key_of[4], (3 * D,), 0.3, 3.0, ((0, 4),)),
        "out_weight": scatter_about(key_of[5], (D, D), (D // 16) ** -0.5, 1.0, ((1, 4),)),
        "out_bias": scatter_about(key_of[6], (D,), 0.3, 3.0, ((0, 4),)),
        "attn_gain": jnp.clip(1.0 + 0.1 * jax.random.normal(key_of[7], (D,), jnp.float32), 0.5, 1.5).astype(jnp.bfloat16),
        "attn_shift": scatter_about(key_of[8], (D,), 0.3, 3.0, ((0, 4),)),
        "ffn_gain": jnp.clip(1.0 + 0.1 * jax.random.normal(key_of[9], (D,), jnp.float32), 0.5, 1.5).astype(jnp.bfloat16),
        "ffn_shift": scatter_about(key_of[10], (D,), 0.3, 3.0, ((0, 4),)),
        "up_weight": scatter_about(key_of[11], (D, FF), D ** -0.5, 0.25, ((1, 4),)),
        "up_bias": scatter_about(key_of[12], (FF,), 0.3, 3.0, ((0, 4),)),
        "down_weight": scatter_about(key_of[13], (FF, D), FF ** -0.5, 0.125, ((0, 4),)),
        "down_bias": scatter_about(key_of[14], (D,), 0.3, 3.0, ((0, 4),)),
    }


@jax.custom_vjp
def low(v):
    return lax.optimization_barrier(v.astype(jnp.bfloat16)).astype(jnp.float32)

@jax.custom_vjp
def low_back(v):
    return v

def low_keep(v):
    return (low(v), None)

def low_pass(kept, grad):
    return (grad,)

def back_keep(v):
    return (v, None)

def back_low(kept, grad):
    return (low(grad),)
low.defvjp(low_keep, low_pass)
low_back.defvjp(back_keep, back_low)

def layer_norm(value, gain, shift):
    center = value - lax.optimization_barrier(jnp.mean(value, axis=-1, keepdims=True))
    spread = lax.optimization_barrier(jnp.mean(center * center, axis=-1, keepdims=True))
    return center * lax.rsqrt(spread + 1e-05) * gain + shift

def rotate(value, angles):
    half = value.shape[-1] // 2
    cosine = jnp.cos(angles)[:, None, :]
    sine = jnp.sin(angles)[:, None, :]
    first = value[..., :half]
    second = value[..., half:]
    return jnp.concatenate([first * cosine - second * sine, second * cosine + first * sine], axis=-1)

def crop_table(quarter, local_rows):
    ends = jnp.cumsum(quarter).astype(jnp.int32)
    starts = (ends - quarter).astype(jnp.int32)
    after = local_rows[:, None] >= ends[None, :]
    inside = jnp.logical_and(local_rows[:, None] >= starts[None, :], jnp.logical_not(after))
    crop = lax.optimization_barrier(jnp.sum(after.astype(jnp.int32), axis=1)).astype(jnp.int32)
    offset = lax.optimization_barrier(jnp.sum(jnp.where(inside, starts[None, :], 0), axis=1)).astype(jnp.int32)
    length = lax.optimization_barrier(jnp.sum(jnp.where(inside, quarter[None, :], 0), axis=1)).astype(jnp.int32)
    return (crop, offset, length)

def matmul(left, right):
    return jnp.dot(left, right, precision=lax.Precision.HIGHEST)

def attend(queries, keys, values, crop):
    group_rows = queries.shape[0]
    block_rows = 512 if group_rows % 512 == 0 else group_rows
    blocks = group_rows // block_rows
    scale = 1.0 / math.sqrt(HEAD_DIM)

    def one_block(inputs):
        query_blk, crop_blk = inputs
        scores = jnp.einsum('qhd,khd->hqk', query_blk, keys, precision=lax.Precision.HIGHEST) * scale
        scores = low_back(scores)
        allowed = (crop_blk[:, None] == crop[None, :])[None]
        masked = jnp.where(allowed, scores, -1e+30)
        highest = lax.optimization_barrier(jnp.max(masked, axis=-1, keepdims=True))
        weights = jnp.where(allowed, jnp.exp(masked - highest), 0.0)
        probs = weights / lax.optimization_barrier(jnp.sum(weights, axis=-1, keepdims=True))
        return jnp.einsum('hqk,khd->qhd', low(probs), values, precision=lax.Precision.HIGHEST)
    result = lax.map(jax.checkpoint(one_block), (queries.reshape(blocks, block_rows, HEADS, HEAD_DIM), crop.reshape(blocks, block_rows)))
    return result.reshape(group_rows, HEADS, HEAD_DIM)

def forward(tokens, qkv_weight, qkv_bias, out_weight, out_bias, attn_gain, attn_shift, ffn_gain, ffn_shift, up_weight, up_bias, down_weight, down_bias, crop, angles):
    group_rows = tokens.shape[0]
    normed = low(layer_norm(tokens, attn_gain, attn_shift))
    qkv = low_back(matmul(normed, qkv_weight) + qkv_bias)
    queries = qkv[:, :D].reshape(group_rows, HEADS, HEAD_DIM)
    keys = qkv[:, D:2 * D].reshape(group_rows, HEADS, HEAD_DIM)
    values = qkv[:, 2 * D:].reshape(group_rows, HEADS, HEAD_DIM)
    queries = low(rotate(queries, angles))
    keys = low(rotate(keys, angles))
    values = low(values)
    context = attend(queries, keys, values, crop).reshape(group_rows, D)
    context = low(low_back(context))
    middle = tokens + low_back(matmul(context, out_weight) + out_bias)
    normed2 = low(layer_norm(middle, ffn_gain, ffn_shift))
    hidden_pre = low_back(matmul(normed2, up_weight) + up_bias)
    activated = low(jax.nn.gelu(hidden_pre, approximate=False))
    return middle + low_back(matmul(activated, down_weight) + down_bias)

def reference(tokens, cotangent, quarters, qkv_weight, qkv_bias, out_weight, out_bias, attn_gain, attn_shift, ffn_gain, ffn_shift, up_weight, up_bias, down_weight, down_bias):
    params = tuple((p.astype(jnp.float32) for p in (qkv_weight, qkv_bias, out_weight, out_bias, attn_gain, attn_shift, ffn_gain, ffn_shift, up_weight, up_bias, down_weight, down_bias)))
    group_rows = N_SEQ * TOK_DEV
    freqs = 10000.0 ** (-jnp.arange(0, HEAD_DIM, 2).astype(jnp.float32) / HEAD_DIM)

    def one_group(totals, inputs):
        token_grp, cot_grp, quarter = inputs
        rows = jnp.arange(group_rows, dtype=jnp.int32)
        local_rows = (rows % TOK_DEV).astype(jnp.int32)
        shard_of = (rows // TOK_DEV).astype(jnp.int32)
        crop, offset, length = crop_table(quarter, local_rows)
        position = (shard_of * length + local_rows - offset).astype(jnp.float32)
        angles = position[:, None] * freqs[None, :]

        def layer(value, *weights):
            return forward(value, *weights, crop, angles)
        output, pullback = jax.vjp(layer, token_grp.astype(jnp.float32), *params)
        grads = pullback(cot_grp.astype(jnp.float32))
        totals = tuple((a + b for a, b in zip(totals, grads[1:])))
        return (totals, (output.astype(jnp.bfloat16), grads[0]))
    zeros = tuple((jnp.zeros(p.shape, jnp.float32) for p in params))
    totals, (out_tokens, grad_tokens) = lax.scan(one_group, zeros, (tokens, cotangent, quarters))
    return (out_tokens, grad_tokens, totals[0], totals[1], totals[2], totals[3], totals[4], totals[5], totals[6], totals[7], totals[8], totals[9], totals[10], totals[11])
```

```python
import functools
import math

import jax
import jax.numpy as jnp
from jax import lax
from jax.experimental import pallas as pl
from jax.experimental.pallas import tpu as pltpu
from jax.sharding import PartitionSpec as P

HEADS = 20
HEAD_DIM = 32
HALF = 16
D = 640
FF = 2560
ROWS = 512
SEG = 256
QW = 480
OW = 160
EPS = 1e-05
SCALE = 1.0 / math.sqrt(HEAD_DIM)
SCALE2 = SCALE * math.log2(math.e)

bf16 = jnp.bfloat16
f32 = jnp.float32

NN = (((1,), (0,)), ((), ()))
NT = (((1,), (1,)), ((), ()))
TN = (((0,), (0,)), ((), ()))
TT = (((0,), (1,)), ((), ()))

VMEM = pl.BlockSpec(memory_space=pltpu.VMEM)
SMEM = pl.BlockSpec(memory_space=pltpu.SMEM)
ANY = pl.BlockSpec(memory_space=pl.ANY)
BIG = pltpu.CompilerParams(vmem_limit_bytes=60 * 2**20)


def dot(a, b, dims):
    return lax.dot_general(a, b, dims, preferred_element_type=f32)


def normalize(x):
    center = x - jnp.mean(x, axis=-1, keepdims=True)
    spread = jnp.mean(center * center, axis=-1, keepdims=True)
    rstd = lax.rsqrt(spread + EPS)
    return center * rstd, rstd


def rolled(ref, start):
    return pltpu.roll(ref[...].astype(f32), ROWS - start, 0)


def project_kernel(
    sc, tok_a, tok_b, w0, w1, w2, w3, bias, gain, shift, cos, sin, *rest, with_q
):
    if with_q:
        q_out, k_out, v_out, n_out, wt = rest
        pos = sc[0]
        for p, w in enumerate((w0, w1, w2, w3)):
            wt[pl.ds(QW * (pos ^ p), QW), :] = w[...].T
    else:
        k_out, v_out, n_out = rest
        wt = w0
    start = sc[1]
    column = bias[...].T[:, 0:1]
    for p, tok in enumerate((tok_a, tok_b)):
        xhat, _ = normalize(rolled(tok, start))
        normed = (xhat * gain[...] + shift[...]).astype(bf16)
        n_out[p] = normed
        for part in range(0 if with_q and p == 0 else 1, 3):
            rows = slice(D * part, D * part + D)
            y = dot(wt[rows, :], normed, NT) + column[rows]
            if part == 2:
                v_out[p] = y.astype(bf16)
                continue
            c, s = cos[p], sin[p]
            for h in range(HEADS):
                a = y[32 * h : 32 * h + 16]
                b = y[32 * h + 16 : 32 * h + 32]
                r = jnp.concatenate([a * c - b * s, b * c + a * s], axis=0).astype(bf16)
                if part == 0:
                    q_out[32 * h : 32 * h + 32, :] = r
                else:
                    k_out[p, 32 * h : 32 * h + 32, :] = r


def project(scalars, tok_a, tok_b, weights, bias, gain, shift, cos, sin, with_q):
    kv = jax.ShapeDtypeStruct((2, D, ROWS), bf16)
    outs = [kv, kv, jax.ShapeDtypeStruct((2, ROWS, D), bf16)]
    if with_q:
        outs = [jax.ShapeDtypeStruct((D, ROWS), bf16)] + outs
        outs.append(jax.ShapeDtypeStruct((3 * D, D), bf16))
    else:
        dummy = jnp.zeros((8, 128), bf16)
        weights = (weights, dummy, dummy, dummy)
    return pl.pallas_call(
        functools.partial(project_kernel, with_q=with_q),
        in_specs=[SMEM] + [VMEM] * 11,
        out_specs=[VMEM] * len(outs),
        out_shape=outs,
        compiler_params=BIG,
        cost_estimate=pl.CostEstimate(
            flops=2 * 2 * ROWS * D * 2 * D, bytes_accessed=8 * 2**20, transcendentals=0
        ),
    )(scalars, tok_a, tok_b, *weights, bias, gain, shift, cos, sin)


def attend_kernel(q_ref, ka_ref, kb_ref, va_ref, vb_ref, mask_ref, o_ref, l_ref, *, heads):
    for h in range(heads):
        hs = slice(32 * h, 32 * h + 32)
        for seg in range(2):
            cs = slice(SEG * seg, SEG * seg + SEG)
            q = q_ref[hs, cs]
            scores = []
            for k_ref in (ka_ref, kb_ref):
                for p in range(2):
                    s = dot(k_ref[p, hs, cs], q, TN)
                    if seg == 1:
                        s = s + mask_ref[...]
                    scores.append(s)
            top = scores[0].max(0, keepdims=True)
            for s in scores[1:]:
                top = jnp.maximum(top, s.max(0, keepdims=True))
            acc = jnp.zeros((HEAD_DIM, SEG), f32)
            total = jnp.zeros((1, SEG), f32)
            for p in range(4):
                v_ref = (va_ref, vb_ref)[p // 2]
                e = jnp.exp2((scores[p] - top) * SCALE2)
                total = total + e.sum(0, keepdims=True)
                acc = acc + dot(v_ref[p % 2, hs, cs], e.astype(bf16), NN)
            o_ref[hs, cs] = acc / total
            l_ref[h, :, cs] = top * SCALE2 + jnp.log2(total)


def attend(q, ka, kb, va, vb, mask):
    heads = 2
    row = pl.BlockSpec((32 * heads, ROWS), lambda h: (h, 0))
    pair = pl.BlockSpec((2, 32 * heads, ROWS), lambda h: (0, h, 0))
    return pl.pallas_call(
        functools.partial(attend_kernel, heads=heads),
        grid=(HEADS // heads,),
        in_specs=[row, pair, pair, pair, pair, pl.BlockSpec((SEG, SEG), lambda h: (0, 0))],
        out_specs=[row, pl.BlockSpec((heads, 1, ROWS), lambda h: (h, 0, 0))],
        out_shape=[
            jax.ShapeDtypeStruct((D, ROWS), f32),
            jax.ShapeDtypeStruct((HEADS, 1, ROWS), f32),
        ],
        compiler_params=BIG,
        cost_estimate=pl.CostEstimate(
            flops=8 * 2**30, bytes_accessed=8 * 2**20, transcendentals=HEADS * ROWS * 1024
        ),
    )(q, ka, kb, va, vb, mask)


def middle_kernel(
    sc, ctx_ref, tok, cot, wo0, wo1, wo2, wo3, vec, upb,
    up0, up1, up2, up3, dn0, dn1, dn2, dn3,
    out_ref, dmid_ref, dctx_ref, delta_ref, vecg_ref, upbg_ref, ga_up, gb_up, ga_dn, gb_dn, ga_o, gb_o,
    up_s, dn_s, mid_t, mid_s, n2_s, n2t_s, cot_s, acc_s, dn2_s, gup_s, gdn_s, go_s, sems,
):
    pos, start = sc[0], sc[1]
    copies = []
    for p, (u, d) in enumerate(((up0, dn0), (up1, dn1), (up2, dn2), (up3, dn3))):
        copies.append(pltpu.make_async_copy(u, up_s.at[p], sems.at[2 * p]))
        copies.append(pltpu.make_async_copy(d, dn_s.at[p], sems.at[2 * p + 1]))
    for c in copies:
        c.start()
    wos = (wo0, wo1, wo2, wo3)
    ctx_low = ctx_ref[...].astype(bf16)
    for p in range(4):
        mid_t[pl.ds(OW * (pos ^ p), OW), :] = dot(wos[p][...], ctx_low, TN)
    out_bias, gain, shift, down_bias = (vec[i : i + 1, :] for i in range(4))
    mid = rolled(tok, start) + mid_t[...].T + out_bias
    mid_s[...] = mid
    xhat, rstd = normalize(mid)
    normed2 = (xhat * gain + shift).astype(bf16)
    n2_s[...] = normed2
    n2t_s[...] = normed2.T
    cot_s[...] = rolled(cot, start).astype(bf16)
    acc_s[...] = mid + down_bias
    dn2_s[...] = jnp.zeros_like(dn2_s)
    for c in copies:
        c.wait()

    def piece(p, carry):
        pre = dot(n2_s[...], up_s[p], NN) + upb[pl.ds(p, 1), :]
        d_act = dot(cot_s[...], dn_s[p], NT)
        cdf = 0.5 + 0.5 * lax.erf(pre * (1.0 / math.sqrt(2.0)))
        pdf = jnp.exp(-0.5 * pre * pre) * (1.0 / math.sqrt(2.0 * math.pi))
        act = (pre * cdf).astype(bf16)
        d_pre = (d_act * (cdf + pre * pdf)).astype(bf16)
        acc_s[...] += dot(act, dn_s[p], NN)
        dn2_s[...] += dot(d_pre, up_s[p], NT)
        gdn_s[p] = dot(act, cot_s[...], TN).astype(bf16)
        gup_s[p] = dot(n2t_s[...], d_pre, NN).astype(bf16)
        upbg_ref[pl.ds(p, 1), :] = jnp.sum(d_pre.astype(f32), axis=0, keepdims=True)
        return carry

    lax.fori_loop(0, 4, piece, 0)
    for i, p in enumerate((0, 2)):
        ga_up[i] = gup_s[p]
        ga_dn[i] = gdn_s[p]
    for i, p in enumerate((1, 3)):
        gb_up[i] = gup_s[p]
        gb_dn[i] = gdn_s[p]
    out_ref[...] = pltpu.roll(acc_s[...], start, 0).astype(bf16)
    xhat, rstd = normalize(mid_s[...])
    d_n2 = dn2_s[...]
    e = d_n2 * gain
    d_cot = cot_s[...].astype(f32)
    d_mid = d_cot + rstd * (
        e - jnp.mean(e, axis=-1, keepdims=True) - xhat * jnp.mean(e * xhat, axis=-1, keepdims=True)
    )
    dmid_ref[...] = d_mid
    d_attn = d_mid.astype(bf16)
    vecg_ref[0:1, :] = jnp.sum(d_attn.astype(f32), axis=0, keepdims=True)
    vecg_ref[1:2, :] = jnp.sum(d_n2 * xhat, axis=0, keepdims=True)
    vecg_ref[2:3, :] = jnp.sum(d_n2, axis=0, keepdims=True)
    vecg_ref[3:4, :] = jnp.sum(d_cot, axis=0, keepdims=True)
    mid_t[...] = d_mid.T
    d_attn_t = mid_t[...].astype(bf16)
    go_s[...] = dot(d_attn_t, ctx_ref[...].astype(bf16), NT).astype(bf16)
    for i, p in enumerate((0, 2)):
        ga_o[i] = go_s[pl.ds(OW * (pos ^ p), OW), :]
    for i, p in enumerate((1, 3)):
        gb_o[i] = go_s[pl.ds(OW * (pos ^ p), OW), :]
    d_ctx = None
    for p in range(4):
        t = dot(wos[p][...], mid_t[pl.ds(OW * (pos ^ p), OW), :].astype(bf16), NN)
        d_ctx = t if d_ctx is None else d_ctx + t
    d_ctx = d_ctx.astype(bf16)
    dctx_ref[...] = d_ctx
    product = d_ctx.astype(f32) * ctx_ref[...]
    for h in range(HEADS):
        delta_ref[h] = jnp.sum(product[32 * h : 32 * h + 32], axis=0, keepdims=True)


def middle(scalars, ctx, tok, cot, wos, vec, upb, ups, downs):
    sds = jax.ShapeDtypeStruct
    big = sds((2, D, D), bf16)
    small = sds((2, OW, D), bf16)
    return pl.pallas_call(
        middle_kernel,
        in_specs=[SMEM] + [VMEM] * 9 + [ANY] * 8,
        out_specs=[VMEM] * 12,
        out_shape=[
            sds((ROWS, D), bf16), sds((ROWS, D), f32), sds((D, ROWS), bf16), sds((HEADS, 1, ROWS), f32),
            sds((4, D), f32), sds((4, D), f32), big, big, big, big, small, small,
        ],
        scratch_shapes=[
            pltpu.VMEM((4, D, D), bf16), pltpu.VMEM((4, D, D), bf16), pltpu.VMEM((D, ROWS), f32),
            pltpu.VMEM((ROWS, D), f32), pltpu.VMEM((ROWS, D), bf16), pltpu.VMEM((D, ROWS), bf16),
            pltpu.VMEM((ROWS, D), bf16), pltpu.VMEM((ROWS, D), f32), pltpu.VMEM((ROWS, D), f32),
            pltpu.VMEM((4, D, D), bf16), pltpu.VMEM((4, D, D), bf16), pltpu.VMEM((D, D), bf16),
            pltpu.SemaphoreType.DMA((8,)),
        ],
        compiler_params=BIG,
        cost_estimate=pl.CostEstimate(
            flops=2 * ROWS * D * (6 * FF + 3 * D), bytes_accessed=24 * 2**20, transcendentals=2 * ROWS * FF
        ),
    )(scalars, ctx, tok, cot, *wos, vec, upb, *ups, *downs)


def attend_back_kernel(
    q_ref, ka_ref, kb_ref, va_ref, vb_ref, do_ref, l_ref, dl_ref, mask_ref, cos_ref, sin_ref,
    dq_ref, dk_ref, dv_ref, *, heads,
):
    def back(g, c, s):
        a, b = g[0:HALF], g[HALF : 2 * HALF]
        return jnp.concatenate([a * c + b * s, b * c - a * s], axis=0).astype(bf16)

    for h in range(heads):
        hs = slice(32 * h, 32 * h + 32)
        for seg in range(2):
            cs = slice(SEG * seg, SEG * seg + SEG)
            q, d_o = q_ref[hs, cs], do_ref[hs, cs]
            log_total, delta = l_ref[h, :, cs], dl_ref[h, :, cs]
            d_q = None
            for p in range(4):
                k = (ka_ref, kb_ref)[p // 2][p % 2, hs, cs]
                v = (va_ref, vb_ref)[p // 2][p % 2, hs, cs]
                s = dot(k, q, TN)
                if seg == 1:
                    s = s + mask_ref[...]
                e = jnp.exp2(s * SCALE2 - log_total)
                d_s = (e * (dot(v, d_o, TN) - delta)).astype(bf16)
                dv_ref[p, hs, cs] = dot(d_o, e.astype(bf16), NT).astype(bf16)
                d_k = dot(q, d_s, NT) * SCALE
                dk_ref[p, hs, cs] = back(d_k, cos_ref[p, :, cs], sin_ref[p, :, cs])
                t = dot(k, d_s, NN)
                d_q = t if d_q is None else d_q + t
            dq_ref[hs, cs] = back(d_q * SCALE, cos_ref[0, :, cs], sin_ref[0, :, cs])


def attend_back(q, ka, kb, va, vb, d_o, log_total, delta, mask, cos, sin):
    heads = 2
    row = pl.BlockSpec((32 * heads, ROWS), lambda h: (h, 0))
    pair = pl.BlockSpec((2, 32 * heads, ROWS), lambda h: (0, h, 0))
    four = pl.BlockSpec((4, 32 * heads, ROWS), lambda h: (0, h, 0))
    stat = pl.BlockSpec((heads, 1, ROWS), lambda h: (h, 0, 0))
    table = pl.BlockSpec((4, HALF, ROWS), lambda h: (0, 0, 0))
    return pl.pallas_call(
        functools.partial(attend_back_kernel, heads=heads),
        grid=(HEADS // heads,),
        in_specs=[row, pair, pair, pair, pair, row, stat, stat]
        + [pl.BlockSpec((SEG, SEG), lambda h: (0, 0)), table, table],
        out_specs=[row, four, four],
        out_shape=[
            jax.ShapeDtypeStruct((D, ROWS), bf16),
            jax.ShapeDtypeStruct((4, D, ROWS), bf16),
            jax.ShapeDtypeStruct((4, D, ROWS), bf16),
        ],
        compiler_params=BIG,
        cost_estimate=pl.CostEstimate(
            flops=20 * 2**30, bytes_accessed=12 * 2**20, transcendentals=HEADS * ROWS * 1024
        ),
    )(q, ka, kb, va, vb, d_o, log_total, delta, mask, cos, sin)


def project_back_kernel(
    sc, dq, dk, dv, na, nb, wt, t0, t1, t2, t3,
    dn0, dnx, dnb, ga, gb, bias_g, norm_g, g_s,
):
    pos, start = sc[0], sc[1]
    ones = jnp.ones((8, ROWS), bf16)
    normed = [na[0], na[1], nb[0], nb[1]]
    g_s[0:D, :] = dot(dq[...], normed[0], NN)
    bias_g[0:1, :] = dot(ones, dq[...], NT)[0:1]
    for part, ref in ((1, dk), (2, dv)):
        g = b = None
        for p in range(4):
            t = dot(ref[p], normed[p], NN)
            u = dot(ones, ref[p], NT)[0:1]
            g = t if g is None else g + t
            b = u if b is None else b + u
        g_s[D * part : D * part + D, :] = g
        bias_g[part : part + 1, :] = b
    for i, p in enumerate((0, 2)):
        ga[i] = g_s[pl.ds(QW * (pos ^ p), QW), :].astype(bf16)
    for i, p in enumerate((1, 3)):
        gb[i] = g_s[pl.ds(QW * (pos ^ p), QW), :].astype(bf16)
    gain_g = shift_g = 0.0
    for p, tok in enumerate((t0, t1, t2, t3)):
        d_n = dot(dk[p], wt[D : 2 * D, :], TN) + dot(dv[p], wt[2 * D : 3 * D, :], TN)
        if p == 0:
            d_n = d_n + dot(dq[...], wt[0:D, :], TN)
        xhat, _ = normalize(rolled(tok, start))
        gain_g = gain_g + jnp.sum(d_n * xhat, axis=0, keepdims=True)
        shift_g = shift_g + jnp.sum(d_n, axis=0, keepdims=True)
        low = d_n.astype(bf16)
        if p == 0:
            dn0[...] = low
        elif p == 2:
            dnx[...] = low
        else:
            dnb[p // 2] = low
    norm_g[0:1, :] = gain_g
    norm_g[1:2, :] = shift_g


def project_back(scalars, dq, dk, dv, na, nb, wt, toks):
    sds = jax.ShapeDtypeStruct
    return pl.pallas_call(
        project_back_kernel,
        in_specs=[SMEM] + [VMEM] * 10,
        out_specs=[VMEM] * 7,
        out_shape=[
            sds((ROWS, D), bf16), sds((ROWS, D), bf16), sds((2, ROWS, D), bf16),
            sds((2, QW, D), bf16), sds((2, QW, D), bf16), sds((3, D), f32), sds((2, D), f32),
        ],
        scratch_shapes=[pltpu.VMEM((3 * D, D), f32)],
        compiler_params=BIG,
        cost_estimate=pl.CostEstimate(
            flops=2 * 18 * ROWS * D * D, bytes_accessed=24 * 2**20, transcendentals=0
        ),
    )(scalars, dq, dk, dv, na, nb, wt, *toks)


def finish_kernel(sc, tok, gain, own, core, across, d_mid, out):
    start = sc[1]
    xhat, rstd = normalize(rolled(tok, start))
    d_n = own[...].astype(f32) + core[...].astype(f32) + across[...].astype(f32)
    e = d_n * gain[...]
    grad = d_mid[...] + rstd * (
        e - jnp.mean(e, axis=-1, keepdims=True) - xhat * jnp.mean(e * xhat, axis=-1, keepdims=True)
    )
    out[...] = pltpu.roll(grad, start, 0)


def finish(scalars, tok, gain, own, core, across, d_mid):
    return pl.pallas_call(
        finish_kernel,
        in_specs=[SMEM] + [VMEM] * 6,
        out_specs=VMEM,
        out_shape=jax.ShapeDtypeStruct((ROWS, D), f32),
        compiler_params=BIG,
        cost_estimate=pl.CostEstimate(flops=10**7, bytes_accessed=6 * 2**20, transcendentals=0),
    )(scalars, tok, gain, own, core, across, d_mid)


def local(
    tokens, cotangent, quarters, qkv_weight, qkv_bias, out_weight, out_bias, attn_gain, attn_shift,
    ffn_gain, ffn_shift, up_weight, up_bias, down_weight, down_bias, *, n_dp,
):
    pos = lax.axis_index("seq")
    group = lax.axis_index("dp")

    def swap(x, seq_mask, dp_mask=0):
        pairs = []
        for s in range(4):
            for d in range(n_dp):
                pairs.append((s * n_dp + d, (s ^ seq_mask) * n_dp + (d ^ dp_mask)))
        return lax.ppermute(x, ("seq", "dp"), pairs)

    def gather(x):
        near = swap(x, 1)
        far = swap(x, 2)
        return x, near, far, swap(far, 1)

    def absolute(parts):
        t = jnp.stack(parts)
        t = jnp.where((pos & 1) == 1, t[jnp.array([1, 0, 3, 2])], t)
        return jnp.where((pos & 2) == 2, t[jnp.array([2, 3, 0, 1])], t)

    tok, cot = tokens[0], cotangent[0]
    ws = gather(qkv_weight)
    packed = jnp.concatenate(
        [qkv_bias, out_bias, attn_gain, attn_shift, ffn_gain, ffn_shift, down_bias, up_bias]
    )
    vecs = gather(packed)
    toks = gather(tok)
    wos = gather(out_weight)
    ups = gather(up_weight)
    downs = gather(down_weight)

    quarter = quarters[0]
    ends = jnp.cumsum(quarter)
    starts = ends - quarter
    start = jnp.sum(jnp.where(quarter == SEG, starts, 0)).astype(jnp.int32)
    scalars = jnp.stack([pos.astype(jnp.int32), start])
    row = (jnp.arange(ROWS, dtype=jnp.int32) + start) % ROWS
    after = row[:, None] >= ends[None, :]
    inside = jnp.logical_and(row[:, None] >= starts[None, :], jnp.logical_not(after))
    crop = jnp.sum(after.astype(jnp.int32), axis=1)
    offset = jnp.sum(jnp.where(inside, starts[None, :], 0), axis=1)
    length = jnp.sum(jnp.where(inside, quarter[None, :], 0), axis=1)
    shard = jnp.stack([pos ^ p for p in range(4)])
    position = (shard[:, None] * length[None, :] + (row - offset)[None, :]).astype(f32)
    freqs = 10000.0 ** (-jnp.arange(0, HEAD_DIM, 2).astype(f32) / HEAD_DIM)
    angles = position[:, None, :] * freqs[None, :, None]
    cos, sin = jnp.cos(angles), jnp.sin(angles)
    mask = jnp.where(crop[SEG:, None] == crop[None, SEG:], 0.0, -1e30).astype(f32)

    vec = absolute(vecs).astype(f32)
    bias = jnp.broadcast_to(vec[:, 0:QW].reshape(1, 3 * D), (8, 3 * D))
    rows = vec[:, QW : QW + 6 * OW].reshape(4, 6, OW).transpose(1, 0, 2).reshape(6, D)
    upb = jnp.stack([v[QW + 6 * OW :] for v in vecs]).astype(f32)
    gain, shift = rows[1:2], rows[2:3]
    mid_rows = jnp.concatenate([rows[0:1], rows[3:6]])

    q, ka, va, na, wt = project(scalars, toks[0], toks[1], ws, bias, gain, shift, cos[0:2], sin[0:2], True)
    kb, vb, nb = project(scalars, toks[2], toks[3], wt, bias, gain, shift, cos[2:4], sin[2:4], False)
    ctx, log_total = attend(q, ka, kb, va, vb, mask)
    (out, d_mid, d_ctx, delta, vec_g, upb_g, gau, gbu, gad, gbd, gao, gbo) = middle(
        scalars, ctx, tok, cot, wos, mid_rows, upb, ups, downs
    )

    def reduce_seq(a, b):
        t = (a.astype(f32) + swap(b, 1).astype(f32)).astype(bf16)
        return (t[0].astype(f32) + swap(t[1], 2).astype(f32)).astype(bf16)

    def reduce_dp(x):
        bits = [1 << i for i in range(n_dp.bit_length() - 1)]
        n = x.shape[0]
        sizes = []
        for b in bits[:3]:
            n //= 2
            mine = (group & b) != 0
            low, high = x[:n], x[n:]
            keep, send = jnp.where(mine, high, low), jnp.where(mine, low, high)
            x = (keep.astype(f32) + swap(send, 0, b).astype(f32)).astype(bf16)
        for b in bits[3:]:
            x = (x.astype(f32) + swap(x, 0, b).astype(f32)).astype(bf16)
        for b in bits[:3][::-1]:
            mine = (group & b) != 0
            other = swap(x, 0, b)
            x = jnp.concatenate([jnp.where(mine, other, x), jnp.where(mine, x, other)])
        return x

    sum_dn = reduce_dp(reduce_seq(gad, gbd))
    sum_up = reduce_dp(reduce_seq(gau, gbu))
    sum_out = reduce_dp(reduce_seq(gao, gbo))

    dq, dk, dv = attend_back(q, ka, kb, va, vb, d_ctx, log_total, delta, mask, cos, sin)
    dn0, dnx, dnb, ga, gb, bias_g, norm_g = project_back(scalars, dq, dk, dv, na, nb, wt, toks)
    back = swap(dnb, 1)
    across = swap((dnx.astype(f32) + back[1].astype(f32)).astype(bf16), 2)
    grad_tok = finish(scalars, tok, gain, dn0, back[0], across, d_mid)

    sum_qkv = reduce_dp(reduce_seq(ga, gb))

    upb_abs = absolute([upb_g[p] for p in range(4)])
    vectors = jnp.concatenate([bias_g, vec_g, norm_g, upb_abs]).astype(bf16)
    for m in (1, 2):
        vectors = (vectors.astype(f32) + swap(vectors, m).astype(f32)).astype(bf16)
    for i in range(n_dp.bit_length() - 1):
        vectors = (vectors.astype(f32) + swap(vectors, 0, 1 << i).astype(f32)).astype(bf16)
    vectors = vectors.astype(f32)

    def own(x, width):
        return lax.dynamic_slice_in_dim(x.reshape(-1), pos * width, width)

    return (
        out[None],
        grad_tok[None],
        sum_qkv.astype(f32).T,
        own(vectors[0:3], QW),
        sum_out.astype(f32).T,
        own(vectors[3], OW),
        own(vectors[7], OW),
        own(vectors[8], OW),
        own(vectors[4], OW),
        own(vectors[5], OW),
        sum_up.astype(f32),
        own(vectors[9:13], D),
        sum_dn.astype(f32),
        own(vectors[6], OW),
    )


def solution(mesh):
    rows, vector = P("dp", "seq", None), P("seq")
    columns = P(None, "seq")
    return jax.shard_map(
        functools.partial(local, n_dp=mesh.shape["dp"]),
        mesh=mesh,
        in_specs=(rows, rows, P("dp", None), columns, vector, columns, vector, vector, vector, vector, vector,
                  columns, vector, P("seq", None), vector),
        out_specs=(rows, rows, columns, vector, columns, vector, vector, vector, vector, vector,
                   columns, vector, P("seq", None), vector),
        check_vma=False,
    )
```

```python
import functools
import math

import jax
import jax.numpy as jnp
from jax import lax
from jax.experimental import pallas as pl
from jax.experimental.pallas import tpu as pltpu
from jax.sharding import PartitionSpec as P

HEADS = 20
HEAD_DIM = 32
HALF = 16
D = 640
FF = 2560
ROWS = 512
SEG = 256
QW = 480
OW = 160
EPS = 1e-05
SCALE = 1.0 / math.sqrt(HEAD_DIM)
SCALE2 = SCALE * math.log2(math.e)

bf16 = jnp.bfloat16
f32 = jnp.float32

NN = (((1,), (0,)), ((), ()))
NT = (((1,), (1,)), ((), ()))
TN = (((0,), (0,)), ((), ()))
TT = (((0,), (1,)), ((), ()))

VMEM = pl.BlockSpec(memory_space=pltpu.VMEM)
SMEM = pl.BlockSpec(memory_space=pltpu.SMEM)
ANY = pl.BlockSpec(memory_space=pl.ANY)
SHORT = pl.CostEstimate(flops=10**6, bytes_accessed=10**5, transcendentals=0)
BIG = pltpu.CompilerParams(vmem_limit_bytes=60 * 2**20)


def dot(a, b, dims):
    return lax.dot_general(a, b, dims, preferred_element_type=f32)


def normalize(x):
    center = x - jnp.mean(x, axis=-1, keepdims=True)
    spread = jnp.mean(center * center, axis=-1, keepdims=True)
    rstd = lax.rsqrt(spread + EPS)
    return center * rstd, rstd


def first_row(quarters):
    start = jnp.int32(0)
    before = jnp.int32(0)
    for c in range(4):
        size = quarters[0, c]
        start = jnp.where(size == SEG, before, start)
        before = before + size
    return start


def rolled(ref, start):
    return pltpu.roll(ref[...].astype(f32), ROWS - start, 0)


def tables_kernel(quarters, freqs, cos, sin, mask):
    pos = lax.axis_index("seq")
    start = first_row(quarters)

    def crops(shape, dim, first):
        row = (lax.broadcasted_iota(jnp.int32, shape, dim) + (first + start)) % ROWS
        end = jnp.int32(0)
        crop = jnp.zeros(shape, jnp.int32)
        offset, length = crop, crop
        for c in range(4):
            size = quarters[0, c]
            begin, end = end, end + size
            crop = crop + (row >= end).astype(jnp.int32)
            inside = jnp.logical_and(row >= begin, row < end)
            offset = jnp.where(inside, begin, offset)
            length = jnp.where(inside, size, length)
        return crop, row - offset, length

    _, place, length = crops((HALF, ROWS), 1, 0)
    for p in range(4):
        angles = ((pos ^ p) * length + place).astype(f32) * freqs[...][:, 0:1]
        cos[p] = jnp.cos(angles)
        sin[p] = jnp.sin(angles)
    down = crops((SEG, SEG), 0, SEG)[0]
    along = crops((SEG, SEG), 1, SEG)[0]
    mask[...] = jnp.where(down == along, 0.0, -1e30)


def tables(quarters):
    freqs = 10000.0 ** (-jnp.arange(0, HEAD_DIM, 2).astype(f32) / HEAD_DIM)
    table = jax.ShapeDtypeStruct((4, HALF, ROWS), f32)
    return pl.pallas_call(
        tables_kernel,
        in_specs=[SMEM, VMEM],
        out_specs=[VMEM] * 3,
        out_shape=[table, table, jax.ShapeDtypeStruct((SEG, SEG), f32)],
        compiler_params=BIG,
    )(quarters, jnp.broadcast_to(freqs[:, None], (HALF, 128)))


def project_rows(p, x, wt, column, gain, shift, cos, sin, q_out, k_out, v_out, n_out):
    xhat, _ = normalize(x)
    normed = (xhat * gain + shift).astype(bf16)
    n_out[p] = normed
    for part in range(0 if q_out is not None else 1, 3):
        rows = slice(D * part, D * part + D)
        y = dot(wt[rows, :], normed, NT) + column[rows]
        if part == 2:
            v_out[p] = y.astype(bf16)
            continue
        c, s = cos[p], sin[p]
        for h in range(HEADS):
            a = y[32 * h : 32 * h + 16]
            b = y[32 * h + 16 : 32 * h + 32]
            r = jnp.concatenate([a * c - b * s, b * c + a * s], axis=0).astype(bf16)
            if part == 0:
                q_out[32 * h : 32 * h + 32, :] = r
            else:
                k_out[p, 32 * h : 32 * h + 32, :] = r


PACK = QW + 16 + ROWS


def pack_kernel(*refs):
    w, tok, out = refs[0], refs[1], refs[10]
    out[0:QW, :] = w[...]
    out[QW + 16 : PACK, :] = tok[...]
    rows = []
    for v in refs[2:10]:
        n = v.shape[0]
        row = v[...].astype(f32).reshape(1, n)
        rows.append(row if n == D else jnp.concatenate([row, jnp.zeros((1, D - n), f32)], axis=1))
    rows.append(jnp.zeros((8, D), f32))
    out[QW : QW + 16, :] = jnp.concatenate(rows, axis=0).astype(bf16)


def pack(w, tok, vectors):
    return pl.pallas_call(
        pack_kernel,
        in_specs=[VMEM] * 10,
        out_specs=VMEM,
        out_shape=jax.ShapeDtypeStruct((PACK, D), bf16),
        compiler_params=BIG,
        cost_estimate=SHORT,
    )(w, tok, *vectors)


def project_kernel(
    quarters, m0, m1, m2, m3, cos, sin,
    q_out, k_out, v_out, n_out, wt, rows_out, upb_out, vt, col,
):
    pos = lax.axis_index("seq")
    start = first_row(quarters)
    parts = (m0, m1, m2, m3)
    for p, m in enumerate(parts):
        wt[pl.ds(QW * (pos ^ p), QW), :] = m[0:QW, :]
        v = m[QW : QW + 16, :].astype(f32)[0:8]
        t = v.T
        col[pl.ds(QW * (pos ^ p), QW), :] = t[0:QW]
        vt[pl.ds(OW * (pos ^ p), OW), :] = t[0:OW]
        upb_out[p : p + 1, :] = v[7:8, :]
    rows = vt[...].T
    rows_out[...] = rows
    column = col[:, 0:1]
    gain, shift = rows[2:3], rows[3:4]
    for p, m in enumerate(parts):
        x = pltpu.roll(m[QW + 16 : PACK, :].astype(f32), ROWS - start, 0)
        project_rows(
            p, x, wt, column, gain, shift, cos, sin, q_out if p == 0 else None, k_out, v_out, n_out
        )


def project(quarters, parts, cos, sin):
    sds = jax.ShapeDtypeStruct
    kv = sds((4, D, ROWS), bf16)
    return pl.pallas_call(
        project_kernel,
        in_specs=[SMEM] + [VMEM] * 6,
        out_specs=[VMEM] * 7,
        out_shape=[
            sds((D, ROWS), bf16), kv, kv, sds((4, ROWS, D), bf16), sds((3 * D, D), bf16),
            sds((8, D), f32), sds((4, D), f32),
        ],
        scratch_shapes=[pltpu.VMEM((D, 8), f32), pltpu.VMEM((3 * D, 8), f32)],
        compiler_params=BIG,
        cost_estimate=SHORT,
    )(quarters, *parts, cos, sin)


def attend_kernel(q_ref, k_ref, v_ref, mask_ref, o_ref, l_ref, *, heads):
    for h in range(heads):
        hs = slice(32 * h, 32 * h + 32)
        for seg in range(2):
            cs = slice(SEG * seg, SEG * seg + SEG)
            q = q_ref[hs, cs]
            scores = []
            for p in range(4):
                s = dot(k_ref[p, hs, cs], q, TN)
                if seg == 1:
                    s = s + mask_ref[...]
                scores.append(s)
            top = scores[0].max(0, keepdims=True)
            for s in scores[1:]:
                top = jnp.maximum(top, s.max(0, keepdims=True))
            acc = jnp.zeros((HEAD_DIM, SEG), f32)
            total = jnp.zeros((1, SEG), f32)
            for p in range(4):
                e = jnp.exp2((scores[p] - top) * SCALE2)
                total = total + e.sum(0, keepdims=True)
                acc = acc + dot(v_ref[p, hs, cs], e.astype(bf16), NN)
            o_ref[hs, cs] = acc / total
            l_ref[h, :, cs] = top * SCALE2 + jnp.log2(total)


def attend(q, k, v, mask):
    heads = 2
    row = pl.BlockSpec((32 * heads, ROWS), lambda h: (h, 0))
    four = pl.BlockSpec((4, 32 * heads, ROWS), lambda h: (0, h, 0))
    return pl.pallas_call(
        functools.partial(attend_kernel, heads=heads),
        grid=(HEADS // heads,),
        in_specs=[row, four, four, pl.BlockSpec((SEG, SEG), lambda h: (0, 0))],
        out_specs=[row, pl.BlockSpec((heads, 1, ROWS), lambda h: (h, 0, 0))],
        out_shape=[
            jax.ShapeDtypeStruct((D, ROWS), f32),
            jax.ShapeDtypeStruct((HEADS, 1, ROWS), f32),
        ],
        compiler_params=BIG,
        cost_estimate=SHORT,
    )(q, k, v, mask)


GA = 1472
HD = 320


def middle_kernel(
    quarters, ctx_ref, tok, cot, wo0, wo1, wo2, wo3, vec, upb,
    up0, up1, up2, up3, uq0, uq1, uq2, uq3, dn0, dn1, dn2, dn3,
    out_ref, dmid_ref, dctx_ref, delta_ref, vecg_ref, upbg_ref, ga, gb,
    up_s, dn_s, wo_s, mid_s, n2_s, n2t_s, cot_s, acc_s, dn2_s, g_s, go_s, sems,
):
    pos = lax.axis_index("seq")
    start = first_row(quarters)
    copies = []
    weights = ((up0, uq0, dn0), (up1, uq1, dn1), (up2, uq2, dn2), (up3, uq3, dn3))
    for p, (u, uq, d) in enumerate(weights):
        copies.append(pltpu.make_async_copy(u, up_s.at[p, pl.ds(0, HD), :], sems.at[3 * p]))
        copies.append(pltpu.make_async_copy(uq, up_s.at[p, pl.ds(HD, HD), :], sems.at[3 * p + 1]))
        copies.append(pltpu.make_async_copy(d, dn_s.at[p], sems.at[3 * p + 2]))
    for c in copies:
        c.start()
    for p, wo in enumerate((wo0, wo1, wo2, wo3)):
        wo_s[pl.ds(OW * (pos ^ p), OW), :] = wo[...]
    ctx_low = ctx_ref[...].astype(bf16)
    out_bias, gain, shift, down_bias = (vec[i : i + 1, :] for i in (1, 4, 5, 6))
    mid = rolled(tok, start) + dot(wo_s[...], ctx_low, NN).T + out_bias
    mid_s[...] = mid
    xhat, rstd = normalize(mid)
    normed2 = (xhat * gain + shift).astype(bf16)
    n2_s[...] = normed2
    n2t_s[...] = normed2.T
    cot_s[...] = rolled(cot, start).astype(bf16)
    acc_s[...] = mid + down_bias
    dn2_s[...] = jnp.zeros_like(dn2_s)
    for c in copies:
        c.wait()

    def piece(p, carry):
        pre = dot(n2_s[...], up_s[p], NN) + upb[pl.ds(p, 1), :]
        d_act = dot(cot_s[...], dn_s[p], NT)
        cdf = 0.5 + 0.5 * lax.erf(pre * (1.0 / math.sqrt(2.0)))
        pdf = jnp.exp(-0.5 * pre * pre) * (1.0 / math.sqrt(2.0 * math.pi))
        act = (pre * cdf).astype(bf16)
        d_pre = (d_act * (cdf + pre * pdf)).astype(bf16)
        acc_s[...] += dot(act, dn_s[p], NN)
        dn2_s[...] += dot(d_pre, up_s[p], NT)
        g_s[p, 0:D, :] = dot(act, cot_s[...], TN).astype(bf16)
        g_s[p, D : 2 * D, :] = dot(n2t_s[...], d_pre, NN).astype(bf16)
        upbg_ref[pl.ds(p, 1), :] = jnp.sum(d_pre.astype(f32), axis=0, keepdims=True)
        return carry

    lax.fori_loop(0, 4, piece, 0)
    out_ref[...] = pltpu.roll(acc_s[...], start, 0).astype(bf16)
    xhat, rstd = normalize(mid_s[...])
    d_n2 = dn2_s[...]
    e = d_n2 * gain
    d_cot = cot_s[...].astype(f32)
    d_mid = d_cot + rstd * (
        e - jnp.mean(e, axis=-1, keepdims=True) - xhat * jnp.mean(e * xhat, axis=-1, keepdims=True)
    )
    dmid_ref[...] = d_mid
    d_attn = d_mid.astype(bf16)
    vecg_ref[0:1, :] = jnp.sum(d_attn.astype(f32), axis=0, keepdims=True)
    vecg_ref[1:3, :] = jnp.zeros((2, D), f32)
    vecg_ref[3:4, :] = jnp.sum(d_n2 * xhat, axis=0, keepdims=True)
    vecg_ref[4:5, :] = jnp.sum(d_n2, axis=0, keepdims=True)
    vecg_ref[5:6, :] = jnp.sum(d_cot, axis=0, keepdims=True)
    vecg_ref[6:8, :] = jnp.zeros((2, D), f32)
    d_attn_t = d_attn.T
    go_s[...] = dot(d_attn_t, ctx_ref[...].astype(bf16), NT).astype(bf16)
    for p in range(4):
        out = (ga, gb)[p % 2]
        out[p // 2, 0 : 2 * D, :] = g_s[p]
        out[p // 2, 2 * D : 2 * D + OW, :] = go_s[pl.ds(OW * (pos ^ p), OW), :]
        out[p // 2, 2 * D + OW : GA, :] = jnp.zeros((GA - 2 * D - OW, D), bf16)
    d_ctx = dot(wo_s[...], d_attn_t, TN).astype(bf16)
    dctx_ref[...] = d_ctx
    product = d_ctx.astype(f32) * ctx_ref[...]
    for h in range(HEADS):
        delta_ref[h] = jnp.sum(product[32 * h : 32 * h + 32], axis=0, keepdims=True)


def middle(quarters, ctx, tok, cot, wos, vec, upb, ups, upqs, downs):
    sds = jax.ShapeDtypeStruct
    big = sds((2, GA, D), bf16)
    return pl.pallas_call(
        middle_kernel,
        in_specs=[SMEM] + [VMEM] * 9 + [ANY] * 12,
        out_specs=[VMEM] * 8,
        out_shape=[
            sds((ROWS, D), bf16), sds((ROWS, D), f32), sds((D, ROWS), bf16), sds((HEADS, 1, ROWS), f32),
            sds((8, D), f32), sds((4, D), f32), big, big,
        ],
        scratch_shapes=[
            pltpu.VMEM((4, D, D), bf16), pltpu.VMEM((4, D, D), bf16), pltpu.VMEM((D, D), bf16),
            pltpu.VMEM((ROWS, D), f32), pltpu.VMEM((ROWS, D), bf16), pltpu.VMEM((D, ROWS), bf16),
            pltpu.VMEM((ROWS, D), bf16), pltpu.VMEM((ROWS, D), f32), pltpu.VMEM((ROWS, D), f32),
            pltpu.VMEM((4, 2 * D, D), bf16), pltpu.VMEM((D, D), bf16),
            pltpu.SemaphoreType.DMA((12,)),
        ],
        compiler_params=BIG,
        cost_estimate=SHORT,
    )(quarters, ctx, tok, cot, *wos, vec, upb, *ups, *upqs, *downs)


def attend_back_kernel(
    q_ref, k_ref, v_ref, do_ref, l_ref, dl_ref, mask_ref, cos_ref, sin_ref,
    dq_ref, dk_ref, dv_ref, *, heads,
):
    def back(g, c, s):
        a, b = g[0:HALF], g[HALF : 2 * HALF]
        return jnp.concatenate([a * c + b * s, b * c - a * s], axis=0).astype(bf16)

    for h in range(heads):
        hs = slice(32 * h, 32 * h + 32)
        for seg in range(2):
            cs = slice(SEG * seg, SEG * seg + SEG)
            q, d_o = q_ref[hs, cs], do_ref[hs, cs]
            log_total, delta = l_ref[h, :, cs], dl_ref[h, :, cs]
            d_q = None
            for p in range(4):
                k = k_ref[p, hs, cs]
                v = v_ref[p, hs, cs]
                s = dot(k, q, TN)
                if seg == 1:
                    s = s + mask_ref[...]
                e = jnp.exp2(s * SCALE2 - log_total)
                d_s = (e * (dot(v, d_o, TN) - delta)).astype(bf16)
                dv_ref[p, hs, cs] = dot(d_o, e.astype(bf16), NT).astype(bf16)
                d_k = dot(q, d_s, NT) * SCALE
                dk_ref[p, hs, cs] = back(d_k, cos_ref[p, :, cs], sin_ref[p, :, cs])
                t = dot(k, d_s, NN)
                d_q = t if d_q is None else d_q + t
            dq_ref[hs, cs] = back(d_q * SCALE, cos_ref[0, :, cs], sin_ref[0, :, cs])


def attend_back(q, k, v, d_o, log_total, delta, mask, cos, sin, first, count, earlier=None):
    heads = 2
    off = first // heads
    row = pl.BlockSpec((32 * heads, ROWS), lambda h: (h + off, 0))
    four = pl.BlockSpec((4, 32 * heads, ROWS), lambda h: (0, h + off, 0))
    stat = pl.BlockSpec((heads, 1, ROWS), lambda h: (h + off, 0, 0))
    table = pl.BlockSpec((4, HALF, ROWS), lambda h: (0, 0, 0))
    operands = [q, k, v, d_o, log_total, delta, mask, cos, sin]
    specs = [row, four, four, row, stat, stat]
    specs += [pl.BlockSpec((SEG, SEG), lambda h: (0, 0)), table, table]
    body = functools.partial(attend_back_kernel, heads=heads)
    kernel, aliases = body, {}
    if earlier is not None:
        aliases = {len(operands) + i: i for i in range(3)}
        operands += list(earlier)
        specs += [ANY] * 3
        kernel = lambda *refs: body(*refs[:9], *refs[12:])
    return pl.pallas_call(
        kernel,
        grid=(count // heads,),
        in_specs=specs,
        out_specs=[row, four, four],
        out_shape=[
            jax.ShapeDtypeStruct((D, ROWS), bf16),
            jax.ShapeDtypeStruct((4, D, ROWS), bf16),
            jax.ShapeDtypeStruct((4, D, ROWS), bf16),
        ],
        input_output_aliases=aliases,
        compiler_params=BIG,
        cost_estimate=SHORT,
    )(*operands)


GB = 512


def weights_back_kernel(dq, dk, dv, normed, wt, rows, vec_g, upb_g, ga, gb, g_s, b_s, v_s, o_s):
    pos = lax.axis_index("seq")
    g_s[0:D, :] = dot(dq[...], normed[0], NN)
    b_s[0:D, :] = jnp.broadcast_to(jnp.sum(dq[...].astype(f32), axis=1, keepdims=True), (D, 8))
    for part, ref in ((1, dk), (2, dv)):
        g = b = None
        for p in range(4):
            t = dot(ref[p], normed[p], NN)
            u = ref[p].astype(f32)
            g = t if g is None else g + t
            b = u if b is None else b + u
        g_s[D * part : D * part + D, :] = g
        b_s[D * part : D * part + D, :] = jnp.broadcast_to(jnp.sum(b, axis=1, keepdims=True), (D, 8))
    w = wt[...].astype(f32)
    both = jnp.sum(w * g_s[...], axis=0, keepdims=True)
    shift_g = jnp.sum(w * b_s[:, 0:1], axis=0, keepdims=True)
    gain_g = (both - rows[3:4, :] * shift_g) / rows[2:3, :]
    v_s[...] = jnp.concatenate([vec_g[0:1, :], gain_g, shift_g, vec_g[3:8, :]], axis=0).T
    o_s[...] = jnp.zeros_like(o_s)
    for p in range(4):
        out = (ga, gb)[p % 2]
        own = pos ^ p
        out[p // 2, 0:QW, :] = g_s[pl.ds(QW * own, QW), :].astype(bf16)
        o_s[0:8, 0:OW] = v_s[pl.ds(OW * own, OW), :].T
        o_s[8:16, 0:QW] = b_s[pl.ds(QW * own, QW), :].T
        o_s[16:24, :] = jnp.broadcast_to(upb_g[p : p + 1, :], (8, D))
        out[p // 2, QW:GB, :] = o_s[...].astype(bf16)


def weights_back(dq, dk, dv, normed, wt, rows, vec_g, upb_g):
    block = jax.ShapeDtypeStruct((2, GB, D), bf16)
    return pl.pallas_call(
        weights_back_kernel,
        in_specs=[VMEM] * 8,
        out_specs=[VMEM] * 2,
        out_shape=[block, block],
        scratch_shapes=[
            pltpu.VMEM((3 * D, D), f32), pltpu.VMEM((3 * D, 8), f32), pltpu.VMEM((D, 8), f32), pltpu.VMEM((32, D), f32),
        ],
        compiler_params=BIG,
        cost_estimate=SHORT,
    )(dq, dk, dv, normed, wt, rows, vec_g, upb_g)


def rows_back_kernel(dq, dk, dv, wt, dn0, dnx, dnb):
    for p in (1, 3, 2, 0):
        d_n = dot(dk[p], wt[D : 2 * D, :], TN) + dot(dv[p], wt[2 * D : 3 * D, :], TN)
        if p == 0:
            d_n = d_n + dot(dq[...], wt[0:D, :], TN)
        low = d_n.astype(bf16)
        if p == 0:
            dn0[...] = low
        elif p == 2:
            dnx[...] = low
        else:
            dnb[p // 2] = low


def rows_back(dq, dk, dv, wt):
    sds = jax.ShapeDtypeStruct
    return pl.pallas_call(
        rows_back_kernel,
        in_specs=[VMEM] * 4,
        out_specs=[VMEM] * 3,
        out_shape=[sds((ROWS, D), bf16), sds((ROWS, D), bf16), sds((2, ROWS, D), bf16)],
        compiler_params=BIG,
        cost_estimate=SHORT,
    )(dq, dk, dv, wt)


def finish_kernel(quarters, tok, rows, own, core, across, d_mid, out):
    start = first_row(quarters)
    xhat, rstd = normalize(rolled(tok, start))
    d_n = own[...].astype(f32) + core[0].astype(f32) + across[...].astype(f32)
    e = d_n * rows[2:3, :]
    grad = d_mid[...] + rstd * (
        e - jnp.mean(e, axis=-1, keepdims=True) - xhat * jnp.mean(e * xhat, axis=-1, keepdims=True)
    )
    out[...] = pltpu.roll(grad, start, 0)


def finish(quarters, tok, rows, own, core, across, d_mid):
    return pl.pallas_call(
        finish_kernel,
        in_specs=[SMEM] + [VMEM] * 6,
        out_specs=VMEM,
        out_shape=jax.ShapeDtypeStruct((ROWS, D), f32),
        compiler_params=BIG,
        cost_estimate=SHORT,
    )(quarters, tok, rows, own, core, across, d_mid)


def place(near, far, total):
    n = near.shape[0] // 4
    group = lax.axis_index("dp")
    y, z = group & 1, (group >> 1) & 3
    for i in range(8):
        row = ((y ^ (i // 4)) * 4 + (z ^ (i % 4))) * n
        part = (near, far)[i // 4][n * (i % 4) : n * (i % 4) + n, :]
        total[pl.ds(pl.multiple_of(row, 8), n), :] = part.astype(f32)


def place_a_kernel(near, far, down, up, out, total):
    place(near, far, total)
    down[...] = total[0:D, :]
    up[...] = total[D : 2 * D, :]
    out[...] = total[2 * D : 2 * D + OW, :]


def place_b_kernel(near, far, qkv, six, bias, upb, total):
    place(near, far, total)
    qkv[...] = total[0:QW, :]
    six[...] = total[QW : QW + 8, 0:OW]
    bias[...] = total[QW + 8 : QW + 9, 0:QW]
    upb[...] = total[QW + 16 : QW + 17, :]


def place_call(kernel, parts, shapes, rows):
    return pl.pallas_call(
        kernel,
        in_specs=[VMEM] * len(parts),
        out_specs=[VMEM] * len(shapes),
        out_shape=[jax.ShapeDtypeStruct(s, f32) for s in shapes],
        scratch_shapes=[pltpu.VMEM((rows, D), f32)],
        compiler_params=BIG,
        cost_estimate=SHORT,
    )(*parts)


def tie(terms, *others):
    return lax.optimization_barrier((tuple(terms),) + others)[0]


def after(x, *others):
    return lax.optimization_barrier((x,) + others)[0]


def local(
    tokens, cotangent, quarters, qkv_weight, qkv_bias, out_weight, out_bias, attn_gain, attn_shift,
    ffn_gain, ffn_shift, up_weight, up_bias, down_weight, down_bias, *, n_dp,
):
    group = lax.axis_index("dp")

    def swap(x, seq_mask, dp_mask=0):
        pairs = []
        for s in range(4):
            for d in range(n_dp):
                pairs.append((s * n_dp + d, (s ^ seq_mask) * n_dp + (d ^ dp_mask)))
        return lax.ppermute(x, ("seq", "dp"), pairs)

    tok, cot = tokens[0], cotangent[0]
    vectors = (qkv_bias, out_bias, attn_gain, attn_shift, ffn_gain, ffn_shift, down_bias, up_bias)
    first = pack(qkv_weight.T, tok, vectors)
    first_far, first_near = swap(first, 2), swap(first, 1)
    cos, sin, mask = tables(after(quarters, first_near))
    first_last = swap(after(first_far, mask), 1)
    q, k, v, normed, wt, rows, upb = project(quarters, (first, first_near, first_far, first_last), cos, sin)
    wo, up_a, up_b = tie((out_weight.T, up_weight[0:HD], up_weight[HD:D]), first_far)
    wo_far, wo_near = swap(wo, 2), swap(wo, 1)
    upa_far, upa_near = swap(up_a, 2), swap(up_a, 1)
    wo_far, upa_far = tie((wo_far, upa_far), q)
    wo_last, upa_last = swap(wo_far, 1), swap(upa_far, 1)
    upb_far, upb_near = swap(after(up_b, wo_far), 2), swap(up_b, 1)
    dn_far, dn_near = swap(after(down_weight, wo_far), 2), swap(down_weight, 1)
    ctx, log_total = attend(after(q, wo_far, upa_far), k, v, mask)
    upb_far, dn_far = tie((upb_far, dn_far), log_total)
    upb_last, dn_last = swap(upb_far, 1), swap(dn_far, 1)
    out, d_mid, d_ctx, delta, vec_g, upb_g, ga, gb = middle(
        quarters, ctx, tok, cot, (out_weight.T, wo_near, wo_far, wo_last), rows, upb,
        (up_a, upa_near, upa_far, upa_last), (up_b, upb_near, upb_far, upb_last),
        (down_weight, dn_near, dn_far, dn_last),
    )

    bits = n_dp.bit_length() - 1
    y, z = group & 1, (group >> 1) & 3

    def total(terms):
        s = terms[0].astype(f32)
        for t in terms[1:]:
            s = s + t.astype(f32)
        return s.astype(bf16)

    def square_parts(a, b, first, rows):
        h = rows // 2

        def part(i, half):
            return total([lax.dynamic_slice(t, (i, first + half * h, 0), (1, h, D))[0] for t in (a, b)])

        return part(0, y), part(1, y), part(0, 1 - y), part(1, 1 - y)

    def square(parts):
        return parts[0], swap(parts[1], 2), swap(parts[2], 0, 1), swap(parts[3], 2, 1)

    def line_parts(terms):
        n = terms[0].shape[0] // 4

        def part(m):
            return total([lax.dynamic_slice(t, ((z ^ m) * n, 0), (n, D)) for t in terms])

        return tuple(part(m) for m in range(4))

    def line(parts):
        return (parts[0],) + tuple(swap(parts[m], 0, 2 * m) for m in (1, 2, 3))

    def line_total(terms):
        s = total(terms)
        for b in range(3, bits):
            s = total([s, swap(s, 0, 1 << b)])
        return s

    def line_spread(s):
        return (s,) + tuple(swap(s, 0, 2 * m) for m in (1, 2, 3))

    args = (k, v, d_ctx, log_total, delta, mask, cos, sin)
    gb_in = swap(gb, 1)
    grads = attend_back(q, *args, 0, 4)
    partsa = square_parts(*tie((ga, gb_in), grads[0]), 0, GA)
    sqa = square(partsa)
    dq, dk, dv = attend_back(after(q, *partsa), *args, 4, 16, grads)
    linea = line_parts(tie(sqa, dq))
    lna = line(linea)
    ha, hb = weights_back(after(dq, *linea), dk, dv, normed, wt, rows, vec_g, upb_g)
    hb_in = swap(hb, 1)
    suma = line_total(tie(lna, ha))
    alla = line_spread(suma)
    partsb = square_parts(after(ha, suma), hb_in, 0, GB)
    sqb = square(partsb)
    dn0, dnx, dnb = rows_back(after(dq, *partsb), dk, dv, wt)
    core = swap(dnb, 1)
    lineb = line_parts(tie(sqb, dn0))
    lnb = line(lineb)
    d_sum = total([dnx, after(core, *lineb)[1]])
    across = swap(d_sum, 2)
    neara = jnp.concatenate(tie(alla, d_sum))
    fara = swap(neara, 0, 1)
    sumb = line_total(tie(lnb, neara))
    allb = line_spread(sumb)
    grad_tok = finish(quarters, tok, rows, after(dn0, sumb), core, across, d_mid)
    nearb = jnp.concatenate(tie(allb, grad_tok))
    farb = swap(nearb, 0, 1)
    g_down, g_up, g_out = place_call(
        place_a_kernel, (after(neara, nearb), fara), ((D, D), (D, D), (OW, D)), GA
    )
    g_qkv, six, g_bias, g_upb = place_call(
        place_b_kernel, (nearb, after(farb, g_down)), ((QW, D), (8, OW), (1, QW), (1, D)), GB
    )

    return (
        out[None], grad_tok[None], g_qkv.T, g_bias[0], g_out.T, six[0], six[1], six[2], six[3], six[4],
        g_up, g_upb[0], g_down, six[5],
    )


def solution(mesh):
    rows, vector = P("dp", "seq", None), P("seq")
    columns = P(None, "seq")
    return jax.shard_map(
        functools.partial(local, n_dp=mesh.shape["dp"]),
        mesh=mesh,
        in_specs=(rows, rows, P("dp", None), columns, vector, columns, vector, vector, vector, vector, vector,
                  columns, vector, P("seq", None), vector),
        out_specs=(rows, rows, columns, vector, columns, vector, vector, vector, vector, vector,
                   columns, vector, P("seq", None), vector),
        check_vma=False,
    )
```

```python
import functools
import math

import jax
import jax.numpy as jnp
import numpy as np
from jax import lax
from jax.experimental import pallas as pl
from jax.experimental.pallas import tpu as pltpu
from jax.sharding import PartitionSpec as P

HEADS = 20
HEAD_DIM = 32
HALF = 16
D = 640
FF = 2560
ROWS = 512
SEG = 256
QW = 480
OW = 160
EPS = 1e-05
SCALE = 1.0 / math.sqrt(HEAD_DIM)
SCALE2 = SCALE * math.log2(math.e)

bf16 = jnp.bfloat16
f32 = jnp.float32

NN = (((1,), (0,)), ((), ()))
NT = (((1,), (1,)), ((), ()))
TN = (((0,), (0,)), ((), ()))
TT = (((0,), (1,)), ((), ()))

VMEM = pl.BlockSpec(memory_space=pltpu.VMEM)
SMEM = pl.BlockSpec(memory_space=pltpu.SMEM)
ANY = pl.BlockSpec(memory_space=pl.ANY)
SHORT = pl.CostEstimate(flops=10**6, bytes_accessed=10**5, transcendentals=0)


def vmem(mebibytes):
    return pltpu.CompilerParams(vmem_limit_bytes=mebibytes * 2**20)


def dot(a, b, dims):
    return lax.dot_general(a, b, dims, preferred_element_type=f32)


def normalize(x):
    center = x - jnp.mean(x, axis=-1, keepdims=True)
    spread = jnp.mean(center * center, axis=-1, keepdims=True)
    rstd = lax.rsqrt(spread + EPS)
    return center * rstd, rstd


def first_row(quarters):
    start = jnp.int32(0)
    before = jnp.int32(0)
    for c in range(4):
        size = quarters[0, c]
        start = jnp.where(size == SEG, before, start)
        before = before + size
    return start


def rolled(ref, start):
    return pltpu.roll(ref[...].astype(f32), ROWS - start, 0)


def tables_kernel(quarters, freqs, cos, sin, mask):
    pos = lax.axis_index("seq")
    start = first_row(quarters)

    def crops(shape, dim, first):
        row = (lax.broadcasted_iota(jnp.int32, shape, dim) + (first + start)) % ROWS
        end = jnp.int32(0)
        crop = jnp.zeros(shape, jnp.int32)
        offset, length = crop, crop
        for c in range(4):
            size = quarters[0, c]
            begin, end = end, end + size
            crop = crop + (row >= end).astype(jnp.int32)
            inside = jnp.logical_and(row >= begin, row < end)
            offset = jnp.where(inside, begin, offset)
            length = jnp.where(inside, size, length)
        return crop, row - offset, length

    _, place, length = crops((HALF, ROWS), 1, 0)
    for p in range(4):
        angles = ((pos ^ p) * length + place).astype(f32) * freqs[...][:, 0:1]
        cos[p] = jnp.cos(angles)
        sin[p] = jnp.sin(angles)
    down = crops((SEG, SEG), 0, SEG)[0]
    along = crops((SEG, SEG), 1, SEG)[0]
    mask[...] = jnp.where(down == along, 0.0, -1e30)


def tables(quarters):
    freqs = np.float32(10000.0) ** (-np.arange(0, HEAD_DIM, 2).astype(np.float32) / np.float32(HEAD_DIM))
    table = jax.ShapeDtypeStruct((4, HALF, ROWS), f32)
    return pl.pallas_call(
        tables_kernel,
        in_specs=[SMEM, VMEM],
        out_specs=[VMEM] * 3,
        out_shape=[table, table, jax.ShapeDtypeStruct((SEG, SEG), f32)],
        compiler_params=vmem(60),
    )(quarters, jnp.asarray(np.repeat(freqs[:, None], 128, axis=1)))


def project_rows(p, x, wt, column, gain, shift, cos, sin, q_out, k_out, v_out, n_out):
    xhat, _ = normalize(x)
    normed = (xhat * gain + shift).astype(bf16)
    n_out[p] = normed
    for part in range(0 if q_out is not None else 1, 3):
        rows = slice(D * part, D * part + D)
        y = dot(wt[rows, :], normed, NT) + column[rows]
        if part == 2:
            v_out[p] = y.astype(bf16)
            continue
        c, s = cos[p], sin[p]
        for h in range(HEADS):
            a = y[32 * h : 32 * h + 16]
            b = y[32 * h + 16 : 32 * h + 32]
            r = jnp.concatenate([a * c - b * s, b * c + a * s], axis=0).astype(bf16)
            if part == 0:
                q_out[32 * h : 32 * h + 32, :] = r
            else:
                k_out[p, 32 * h : 32 * h + 32, :] = r


WPART = 512
PART = WPART // 4
PACK = WPART + ROWS


def pack_kernel(*refs):
    w, tok, out, part = refs[0], refs[1], refs[10], refs[11]
    out[0:QW, :] = w[...]
    out[WPART:PACK, :] = tok[...]
    rows = []
    for v in refs[2:10]:
        n = v.shape[0]
        row = v[...].astype(f32).reshape(1, n)
        rows.append(row if n == D else jnp.concatenate([row, jnp.zeros((1, D - n), f32)], axis=1))
    rows.append(jnp.zeros((WPART - QW - 8, D), f32))
    out[QW:WPART, :] = jnp.concatenate(rows, axis=0).astype(bf16)
    which = lax.axis_index("dp") & 3
    part[...] = out[pl.ds(pl.multiple_of(which * PART, PART), PART), :]


def pack(w, tok, vectors):
    return pl.pallas_call(
        pack_kernel,
        in_specs=[VMEM] * 10,
        out_specs=[VMEM] * 2,
        out_shape=[jax.ShapeDtypeStruct((PACK, D), bf16), jax.ShapeDtypeStruct((PART, D), bf16)],
        compiler_params=vmem(60),
        cost_estimate=SHORT,
    )(w, tok, *vectors)


def project_kernel(
    quarters, own, near, tok_far, tok_last, far0, far1, far2, last0, last1, last2, cos, sin,
    q_out, k_out, v_out, n_out, wt, rows_out, upb_out, vt, col, w_far, w_last,
):
    pos = lax.axis_index("seq")
    which = lax.axis_index("dp") & 3
    start = first_row(quarters)
    for whole, p0, p1, p2 in ((w_far, far0, far1, far2), (w_last, last0, last1, last2)):
        pieces = (p0[...], p1[...], p2[0:PART, :], p2[PART : 2 * PART, :])
        for i, piece in enumerate(pieces):
            whole[pl.ds(pl.multiple_of((which ^ i) * PART, PART), PART), :] = piece
    for p, m in enumerate((own, near, w_far, w_last)):
        wt[pl.ds(QW * (pos ^ p), QW), :] = m[0:QW, :]
        v = m[QW : QW + 16, :].astype(f32)[0:8]
        t = v.T
        col[pl.ds(QW * (pos ^ p), QW), :] = t[0:QW]
        vt[pl.ds(OW * (pos ^ p), OW), :] = t[0:OW]
        upb_out[p : p + 1, :] = v[7:8, :]
    rows = vt[...].T
    rows_out[...] = rows
    column = col[:, 0:1]
    gain, shift = rows[2:3], rows[3:4]
    toks = (own.at[pl.ds(WPART, ROWS), :], near.at[pl.ds(WPART, ROWS), :], tok_far, tok_last)
    for p, tok in enumerate(toks):
        project_rows(
            p, rolled(tok, start), wt, column, gain, shift, cos, sin,
            q_out if p == 0 else None, k_out, v_out, n_out,
        )


def project(quarters, parts, cos, sin):
    sds = jax.ShapeDtypeStruct
    kv = sds((4, D, ROWS), bf16)
    return pl.pallas_call(
        project_kernel,
        in_specs=[SMEM] + [VMEM] * 12,
        out_specs=[VMEM] * 7,
        out_shape=[
            sds((D, ROWS), bf16), kv, kv, sds((4, ROWS, D), bf16), sds((3 * D, D), bf16),
            sds((8, D), f32), sds((4, D), f32),
        ],
        scratch_shapes=[
            pltpu.VMEM((D, 8), f32), pltpu.VMEM((3 * D, 8), f32),
            pltpu.VMEM((WPART, D), bf16), pltpu.VMEM((WPART, D), bf16),
        ],
        compiler_params=vmem(60),
        cost_estimate=SHORT,
    )(quarters, *parts, cos, sin)


def attend_kernel(q_ref, k_ref, v_ref, mask_ref, o_ref, l_ref, *, heads):
    for h in range(heads):
        hs = slice(32 * h, 32 * h + 32)
        for seg in range(2):
            cs = slice(SEG * seg, SEG * seg + SEG)
            q = q_ref[hs, cs]
            scores = []
            for p in range(4):
                s = dot(k_ref[p, hs, cs], q, TN)
                if seg == 1:
                    s = s + mask_ref[...]
                scores.append(s)
            top = scores[0].max(0, keepdims=True)
            for s in scores[1:]:
                top = jnp.maximum(top, s.max(0, keepdims=True))
            acc = jnp.zeros((HEAD_DIM, SEG), f32)
            total = jnp.zeros((1, SEG), f32)
            for p in range(4):
                e = jnp.exp2((scores[p] - top) * SCALE2)
                total = total + e.sum(0, keepdims=True)
                acc = acc + dot(v_ref[p, hs, cs], e.astype(bf16), NN)
            o_ref[hs, cs] = acc / total
            l_ref[h, :, cs] = top * SCALE2 + jnp.log2(total)


def attend(q, k, v, mask):
    heads = 2
    row = pl.BlockSpec((32 * heads, ROWS), lambda h: (h, 0))
    four = pl.BlockSpec((4, 32 * heads, ROWS), lambda h: (0, h, 0))
    return pl.pallas_call(
        functools.partial(attend_kernel, heads=heads),
        grid=(HEADS // heads,),
        in_specs=[row, four, four, pl.BlockSpec((SEG, SEG), lambda h: (0, 0))],
        out_specs=[row, pl.BlockSpec((heads, 1, ROWS), lambda h: (h, 0, 0))],
        out_shape=[
            jax.ShapeDtypeStruct((D, ROWS), f32),
            jax.ShapeDtypeStruct((HEADS, 1, ROWS), f32),
        ],
        compiler_params=vmem(60),
        cost_estimate=SHORT,
    )(q, k, v, mask)


GA = 1472
HD = 320


def middle_kernel(
    quarters, ctx_ref, tok, cot, wo0, wo1, wo2, wo3, vec, upb,
    up0, up1, up2, up3, dn0, dn1, dn2, dn3, dq2, dq3,
    out_ref, dmid_ref, dctx_ref, delta_ref, vecg_ref, upbg_ref, ga, gb,
    up_s, dn_s, wo_s, mid_s, n2_s, n2t_s, cot_s, acc_s, dn2_s, g_s, go_s, sems,
):
    pos = lax.axis_index("seq")
    start = first_row(quarters)
    copies = []
    half = lax.axis_index("dp") & 1
    for p, (u, d) in enumerate(((up0, dn0), (up1, dn1), (up2, dn2), (up3, dn3))):
        copies.append(pltpu.make_async_copy(u, up_s.at[p], sems.at[3 * p]))
        if p < 2:
            copies.append(pltpu.make_async_copy(d, dn_s.at[p], sems.at[3 * p + 1]))
            continue
        for i, h in enumerate((d, (dq2, dq3)[p - 2])):
            to = dn_s.at[p, pl.ds(pl.multiple_of(HD * (half ^ i), HD), HD), :]
            copies.append(pltpu.make_async_copy(h, to, sems.at[3 * p + 1 + i]))
    for c in copies:
        c.start()
    for p, wo in enumerate((wo0, wo1, wo2, wo3)):
        wo_s[pl.ds(OW * (pos ^ p), OW), :] = wo[...]
    ctx_low = ctx_ref[...].astype(bf16)
    out_bias, gain, shift, down_bias = (vec[i : i + 1, :] for i in (1, 4, 5, 6))
    mid = rolled(tok, start) + dot(wo_s[...], ctx_low, NN).T + out_bias
    mid_s[...] = mid
    xhat, rstd = normalize(mid)
    normed2 = (xhat * gain + shift).astype(bf16)
    n2_s[...] = normed2
    n2t_s[...] = normed2.T
    cot_s[...] = rolled(cot, start).astype(bf16)
    acc_s[...] = mid + down_bias
    dn2_s[...] = jnp.zeros_like(dn2_s)
    for c in copies:
        c.wait()

    def piece(p, carry):
        pre = dot(n2_s[...], up_s[p], NN) + upb[pl.ds(p, 1), :]
        d_act = dot(cot_s[...], dn_s[p], NT)
        cdf = 0.5 + 0.5 * lax.erf(pre * (1.0 / math.sqrt(2.0)))
        pdf = jnp.exp(-0.5 * pre * pre) * (1.0 / math.sqrt(2.0 * math.pi))
        act = (pre * cdf).astype(bf16)
        d_pre = (d_act * (cdf + pre * pdf)).astype(bf16)
        acc_s[...] += dot(act, dn_s[p], NN)
        dn2_s[...] += dot(d_pre, up_s[p], NT)
        g_s[p, 0:D, :] = dot(act, cot_s[...], TN).astype(bf16)
        g_s[p, D : 2 * D, :] = dot(n2t_s[...], d_pre, NN).astype(bf16)
        upbg_ref[pl.ds(p, 1), :] = jnp.sum(d_pre.astype(f32), axis=0, keepdims=True)
        return carry

    lax.fori_loop(0, 4, piece, 0)
    out_ref[...] = pltpu.roll(acc_s[...], start, 0).astype(bf16)
    xhat, rstd = normalize(mid_s[...])
    d_n2 = dn2_s[...]
    e = d_n2 * gain
    d_cot = cot_s[...].astype(f32)
    d_mid = d_cot + rstd * (
        e - jnp.mean(e, axis=-1, keepdims=True) - xhat * jnp.mean(e * xhat, axis=-1, keepdims=True)
    )
    dmid_ref[...] = d_mid
    d_attn = d_mid.astype(bf16)
    vecg_ref[0:1, :] = jnp.sum(d_attn.astype(f32), axis=0, keepdims=True)
    vecg_ref[1:3, :] = jnp.zeros((2, D), f32)
    vecg_ref[3:4, :] = jnp.sum(d_n2 * xhat, axis=0, keepdims=True)
    vecg_ref[4:5, :] = jnp.sum(d_n2, axis=0, keepdims=True)
    vecg_ref[5:6, :] = jnp.sum(d_cot, axis=0, keepdims=True)
    vecg_ref[6:8, :] = jnp.zeros((2, D), f32)
    d_attn_t = d_attn.T
    go_s[...] = dot(d_attn_t, ctx_ref[...].astype(bf16), NT).astype(bf16)
    for p in range(4):
        out = (ga, gb)[p % 2]
        out[p // 2, 0 : 2 * D, :] = g_s[p]
        out[p // 2, 2 * D : 2 * D + OW, :] = go_s[pl.ds(OW * (pos ^ p), OW), :]
        out[p // 2, 2 * D + OW : GA, :] = jnp.zeros((GA - 2 * D - OW, D), bf16)
    d_ctx = dot(wo_s[...], d_attn_t, TN).astype(bf16)
    dctx_ref[...] = d_ctx
    product = d_ctx.astype(f32) * ctx_ref[...]
    for h in range(HEADS):
        delta_ref[h] = jnp.sum(product[32 * h : 32 * h + 32], axis=0, keepdims=True)


def middle(quarters, ctx, tok, cot, wos, vec, upb, ups, downs):
    sds = jax.ShapeDtypeStruct
    big = sds((2, GA, D), bf16)
    return pl.pallas_call(
        middle_kernel,
        in_specs=[SMEM] + [VMEM] * 9 + [ANY] * 10,
        out_specs=[VMEM] * 8,
        out_shape=[
            sds((ROWS, D), bf16), sds((ROWS, D), f32), sds((D, ROWS), bf16), sds((HEADS, 1, ROWS), f32),
            sds((8, D), f32), sds((4, D), f32), big, big,
        ],
        scratch_shapes=[
            pltpu.VMEM((4, D, D), bf16), pltpu.VMEM((4, D, D), bf16), pltpu.VMEM((D, D), bf16),
            pltpu.VMEM((ROWS, D), f32), pltpu.VMEM((ROWS, D), bf16), pltpu.VMEM((D, ROWS), bf16),
            pltpu.VMEM((ROWS, D), bf16), pltpu.VMEM((ROWS, D), f32), pltpu.VMEM((ROWS, D), f32),
            pltpu.VMEM((4, 2 * D, D), bf16), pltpu.VMEM((D, D), bf16),
            pltpu.SemaphoreType.DMA((12,)),
        ],
        compiler_params=vmem(58),
        cost_estimate=SHORT,
    )(quarters, ctx, tok, cot, *wos, vec, upb, *ups, *downs)


def attend_back_kernel(
    q_ref, k_ref, v_ref, do_ref, l_ref, dl_ref, mask_ref, cos_ref, sin_ref,
    dq_ref, dk_ref, dv_ref, *, heads,
):
    def back(g, c, s):
        a, b = g[0:HALF], g[HALF : 2 * HALF]
        return jnp.concatenate([a * c + b * s, b * c - a * s], axis=0).astype(bf16)

    for h in range(heads):
        hs = slice(32 * h, 32 * h + 32)
        for seg in range(2):
            cs = slice(SEG * seg, SEG * seg + SEG)
            q, d_o = q_ref[hs, cs], do_ref[hs, cs]
            log_total, delta = l_ref[h, :, cs], dl_ref[h, :, cs]
            d_q = None
            for p in range(4):
                k = k_ref[p, hs, cs]
                v = v_ref[p, hs, cs]
                s = dot(k, q, TN)
                if seg == 1:
                    s = s + mask_ref[...]
                e = jnp.exp2(s * SCALE2 - log_total)
                d_s = (e * (dot(v, d_o, TN) - delta)).astype(bf16)
                dv_ref[p, hs, cs] = dot(d_o, e.astype(bf16), NT).astype(bf16)
                d_k = dot(q, d_s, NT) * SCALE
                dk_ref[p, hs, cs] = back(d_k, cos_ref[p, :, cs], sin_ref[p, :, cs])
                t = dot(k, d_s, NN)
                d_q = t if d_q is None else d_q + t
            dq_ref[hs, cs] = back(d_q * SCALE, cos_ref[0, :, cs], sin_ref[0, :, cs])


def attend_back(q, k, v, d_o, log_total, delta, mask, cos, sin, first, count, earlier=None):
    heads = 2
    off = first // heads
    row = pl.BlockSpec((32 * heads, ROWS), lambda h: (h + off, 0))
    four = pl.BlockSpec((4, 32 * heads, ROWS), lambda h: (0, h + off, 0))
    stat = pl.BlockSpec((heads, 1, ROWS), lambda h: (h + off, 0, 0))
    table = pl.BlockSpec((4, HALF, ROWS), lambda h: (0, 0, 0))
    operands = [q, k, v, d_o, log_total, delta, mask, cos, sin]
    specs = [row, four, four, row, stat, stat]
    specs += [pl.BlockSpec((SEG, SEG), lambda h: (0, 0)), table, table]
    body = functools.partial(attend_back_kernel, heads=heads)
    kernel, aliases = body, {}
    if earlier is not None:
        aliases = {len(operands) + i: i for i in range(3)}
        operands += list(earlier)
        specs += [ANY] * 3
        kernel = lambda *refs: body(*refs[:9], *refs[12:])
    return pl.pallas_call(
        kernel,
        grid=(count // heads,),
        in_specs=specs,
        out_specs=[row, four, four],
        out_shape=[
            jax.ShapeDtypeStruct((D, ROWS), bf16),
            jax.ShapeDtypeStruct((4, D, ROWS), bf16),
            jax.ShapeDtypeStruct((4, D, ROWS), bf16),
        ],
        input_output_aliases=aliases,
        compiler_params=vmem(60),
        cost_estimate=SHORT,
    )(*operands)


GB = 512


def weights_back_kernel(dq, dk, dv, normed, wt, rows, vec_g, upb_g, ga, gb, g_s, b_s, v_s, o_s):
    pos = lax.axis_index("seq")
    g_s[0:D, :] = dot(dq[...], normed[0], NN)
    b_s[0:D, :] = jnp.broadcast_to(jnp.sum(dq[...].astype(f32), axis=1, keepdims=True), (D, 8))
    for part, ref in ((1, dk), (2, dv)):
        g = b = None
        for p in range(4):
            t = dot(ref[p], normed[p], NN)
            u = ref[p].astype(f32)
            g = t if g is None else g + t
            b = u if b is None else b + u
        g_s[D * part : D * part + D, :] = g
        b_s[D * part : D * part + D, :] = jnp.broadcast_to(jnp.sum(b, axis=1, keepdims=True), (D, 8))
    w = wt[...].astype(f32)
    both = jnp.sum(w * g_s[...], axis=0, keepdims=True)
    shift_g = jnp.sum(w * b_s[:, 0:1], axis=0, keepdims=True)
    gain_g = (both - rows[3:4, :] * shift_g) / rows[2:3, :]
    v_s[...] = jnp.concatenate([vec_g[0:1, :], gain_g, shift_g, vec_g[3:8, :]], axis=0).T
    o_s[...] = jnp.zeros_like(o_s)
    for p in range(4):
        out = (ga, gb)[p % 2]
        own = pos ^ p
        out[p // 2, 0:QW, :] = g_s[pl.ds(QW * own, QW), :].astype(bf16)
        o_s[0:8, 0:OW] = v_s[pl.ds(OW * own, OW), :].T
        o_s[8:16, 0:QW] = b_s[pl.ds(QW * own, QW), :].T
        o_s[16:24, :] = jnp.broadcast_to(upb_g[p : p + 1, :], (8, D))
        out[p // 2, QW:GB, :] = o_s[...].astype(bf16)


def weights_back(dq, dk, dv, normed, wt, rows, vec_g, upb_g):
    block = jax.ShapeDtypeStruct((2, GB, D), bf16)
    return pl.pallas_call(
        weights_back_kernel,
        in_specs=[VMEM] * 8,
        out_specs=[VMEM] * 2,
        out_shape=[block, block],
        scratch_shapes=[
            pltpu.VMEM((3 * D, D), f32), pltpu.VMEM((3 * D, 8), f32), pltpu.VMEM((D, 8), f32), pltpu.VMEM((32, D), f32),
        ],
        compiler_params=vmem(60),
        cost_estimate=SHORT,
    )(dq, dk, dv, normed, wt, rows, vec_g, upb_g)


def rows_back_kernel(dq, dk, dv, wt, dn0, dnx, dnb):
    for p in (1, 3, 2, 0):
        d_n = dot(dk[p], wt[D : 2 * D, :], TN) + dot(dv[p], wt[2 * D : 3 * D, :], TN)
        if p == 0:
            d_n = d_n + dot(dq[...], wt[0:D, :], TN)
        low = d_n.astype(bf16)
        if p == 0:
            dn0[...] = low
        elif p == 2:
            dnx[...] = low
        else:
            dnb[p // 2] = low


def rows_back(dq, dk, dv, wt):
    sds = jax.ShapeDtypeStruct
    return pl.pallas_call(
        rows_back_kernel,
        in_specs=[VMEM] * 4,
        out_specs=[VMEM] * 3,
        out_shape=[sds((ROWS, D), bf16), sds((ROWS, D), bf16), sds((2, ROWS, D), bf16)],
        compiler_params=vmem(60),
        cost_estimate=SHORT,
    )(dq, dk, dv, wt)


def finish_kernel(quarters, tok, rows, own, core, across, d_mid, out):
    start = first_row(quarters)
    xhat, rstd = normalize(rolled(tok, start))
    d_n = own[...].astype(f32) + core[0].astype(f32) + across[...].astype(f32)
    e = d_n * rows[2:3, :]
    grad = d_mid[...] + rstd * (
        e - jnp.mean(e, axis=-1, keepdims=True) - xhat * jnp.mean(e * xhat, axis=-1, keepdims=True)
    )
    out[...] = pltpu.roll(grad, start, 0)


def finish(quarters, tok, rows, own, core, across, d_mid):
    return pl.pallas_call(
        finish_kernel,
        in_specs=[SMEM] + [VMEM] * 6,
        out_specs=VMEM,
        out_shape=jax.ShapeDtypeStruct((ROWS, D), f32),
        compiler_params=vmem(16),
        cost_estimate=SHORT,
    )(quarters, tok, rows, own, core, across, d_mid)


def place(near, far, total):
    n = near.shape[0] // 4
    group = lax.axis_index("dp")
    y, z = group & 1, (group >> 1) & 3
    for i in range(8):
        row = ((y ^ (i // 4)) * 4 + (z ^ (i % 4))) * n
        part = (near, far)[i // 4][n * (i % 4) : n * (i % 4) + n, :]
        total[pl.ds(pl.multiple_of(row, 8), n), :] = part.astype(f32)


def place_a_kernel(near, far, down, up, out, total):
    place(near, far, total)
    down[...] = total[0:D, :]
    up[...] = total[D : 2 * D, :]
    out[...] = total[2 * D : 2 * D + OW, :]


def place_b_kernel(near, far, qkv, six, bias, upb, total):
    place(near, far, total)
    qkv[...] = total[0:QW, :]
    six[...] = total[QW : QW + 8, 0:OW]
    bias[...] = total[QW + 8 : QW + 9, 0:QW]
    upb[...] = total[QW + 16 : QW + 17, :]


def place_call(kernel, parts, shapes, rows):
    return pl.pallas_call(
        kernel,
        in_specs=[VMEM] * len(parts),
        out_specs=[VMEM] * len(shapes),
        out_shape=[jax.ShapeDtypeStruct(s, f32) for s in shapes],
        scratch_shapes=[pltpu.VMEM((rows, D), f32)],
        compiler_params=vmem(24),
        cost_estimate=SHORT,
    )(*parts)


def tie(terms, *others):
    return lax.optimization_barrier((tuple(terms),) + others)[0]


def after(x, *others):
    return lax.optimization_barrier((x,) + others)[0]


def local(
    tokens, cotangent, quarters, qkv_weight, qkv_bias, out_weight, out_bias, attn_gain, attn_shift,
    ffn_gain, ffn_shift, up_weight, up_bias, down_weight, down_bias, *, n_dp,
):
    group = lax.axis_index("dp")

    def swap(x, seq_mask, dp_mask=0):
        pairs = []
        for s in range(4):
            for d in range(n_dp):
                pairs.append((s * n_dp + d, (s ^ seq_mask) * n_dp + (d ^ dp_mask)))
        return lax.ppermute(x, ("seq", "dp"), pairs)

    tok, cot = tokens[0], cotangent[0]
    vectors = (qkv_bias, out_bias, attn_gain, attn_shift, ffn_gain, ffn_shift, down_bias, up_bias)
    own, part = pack(qkv_weight.T, tok, vectors)
    far0 = swap(part, 2)
    near = swap(own, 1)
    tok_far = swap(after(tok, far0), 2)
    far1 = swap(far0, 0, 1)
    cos, sin, mask = tables(after(quarters, far0))
    far2 = swap(jnp.concatenate([after(far0, mask), far1]), 0, 2)
    last = [swap(x, 1) for x in (far0, far1, far2)]
    tok_last = swap(tok_far, 1)
    q, k, v, normed, wt, rows, upb = project(
        quarters, (own, near, tok_far, tok_last, far0, far1, far2, *last), cos, sin
    )
    half = lax.dynamic_slice_in_dim(down_weight, (group & 1) * HD, HD)
    wo, half = tie((out_weight.T, half), tok_far)
    wo_far, wo_near = swap(wo, 2), swap(wo, 1)
    dn_far, dn_near = swap(half, 2), swap(down_weight, 1)
    wo_far, dn_far = tie((wo_far, dn_far), q)
    wo_last, dn_last = swap(wo_far, 1), swap(dn_far, 1)
    dn_far2 = swap(dn_far, 0, 1)
    up_far, up_near = swap(after(up_weight, wo_far), 2), swap(up_weight, 1)
    ctx, log_total = attend(after(q, wo_far, dn_far), k, v, mask)
    up_far, dn_far2 = tie((up_far, dn_far2), log_total)
    up_last, dn_last2 = swap(up_far, 1), swap(dn_far2, 1)
    out, d_mid, d_ctx, delta, vec_g, upb_g, ga, gb = middle(
        quarters, ctx, tok, cot, (out_weight.T, wo_near, wo_far, wo_last), rows, upb,
        (up_weight, up_near, up_far, up_last),
        (down_weight, dn_near, dn_far, dn_last, dn_far2, dn_last2),
    )

    bits = n_dp.bit_length() - 1
    y, z = group & 1, (group >> 1) & 3

    def total(terms):
        s = terms[0].astype(f32)
        for t in terms[1:]:
            s = s + t.astype(f32)
        return s.astype(bf16)

    def square_parts(a, b, first, rows):
        h = rows // 2

        def part(i, half):
            return total([lax.dynamic_slice(t, (i, first + half * h, 0), (1, h, D))[0] for t in (a, b)])

        return part(0, y), part(1, y), part(0, 1 - y), part(1, 1 - y)

    def square(parts):
        return parts[0], swap(parts[1], 2), swap(parts[2], 0, 1), swap(parts[3], 2, 1)

    def line_parts(terms):
        n = terms[0].shape[0] // 4

        def part(m):
            return total([lax.dynamic_slice(t, ((z ^ m) * n, 0), (n, D)) for t in terms])

        return tuple(part(m) for m in range(4))

    def line(parts):
        return (parts[0],) + tuple(swap(parts[m], 0, 2 * m) for m in (1, 2, 3))

    def line_total(terms):
        s = total(terms)
        for b in range(3, bits):
            s = total([s, swap(s, 0, 1 << b)])
        return s

    def line_spread(s):
        return (s,) + tuple(swap(s, 0, 2 * m) for m in (1, 2, 3))

    args = (k, v, d_ctx, log_total, delta, mask, cos, sin)
    gb_in = swap(gb, 1)
    grads = attend_back(q, *args, 0, 4)
    partsa = square_parts(*tie((ga, gb_in), grads[0]), 0, GA)
    sqa = square(partsa)
    dq, dk, dv = attend_back(after(q, *partsa), *args, 4, 16, grads)
    linea = line_parts(tie(sqa, dq))
    lna = line(linea)
    ha, hb = weights_back(after(dq, *linea), dk, dv, normed, wt, rows, vec_g, upb_g)
    suma = line_total(tie(lna, ha))
    alla = line_spread(suma)
    hb_in = swap(after(hb, suma), 1)
    partsb = square_parts(ha, hb_in, 0, GB)
    sqb = square(partsb)
    dn0, dnx, dnb = rows_back(after(dq, *partsb), dk, dv, wt)
    lineb = line_parts(tie(sqb, dn0))
    lnb = line(lineb)
    neara = jnp.concatenate(tie(alla, *lineb))
    fara = swap(neara, 0, 1)
    core = swap(after(dnb, neara), 1)
    d_sum = total([dnx, core[1]])
    across = swap(d_sum, 2)
    sumb = line_total(tie(lnb, d_sum))
    allb = line_spread(sumb)
    grad_tok = finish(quarters, tok, rows, after(dn0, sumb), core, across, d_mid)
    nearb = jnp.concatenate(tie(allb, grad_tok))
    farb = swap(nearb, 0, 1)
    g_down, g_up, g_out = place_call(
        place_a_kernel, (after(neara, nearb), fara), ((D, D), (D, D), (OW, D)), GA
    )
    g_qkv, six, g_bias, g_upb = place_call(
        place_b_kernel, (nearb, after(farb, g_down)), ((QW, D), (8, OW), (1, QW), (1, D)), GB
    )

    return (
        out[None], grad_tok[None], g_qkv.T, g_bias[0], g_out.T, six[0], six[1], six[2], six[3], six[4],
        g_up, g_upb[0], g_down, six[5],
    )


def solution(mesh):
    rows, vector = P("dp", "seq", None), P("seq")
    columns = P(None, "seq")
    return jax.shard_map(
        functools.partial(local, n_dp=mesh.shape["dp"]),
        mesh=mesh,
        in_specs=(rows, rows, P("dp", None), columns, vector, columns, vector, vector, vector, vector, vector,
                  columns, vector, P("seq", None), vector),
        out_specs=(rows, rows, columns, vector, columns, vector, vector, vector, vector, vector,
                   columns, vector, P("seq", None), vector),
        check_vma=False,
    )
```

```python
import functools
import math

import jax
import jax.numpy as jnp
import numpy as np
from jax import lax
from jax.experimental import pallas as pl
from jax.experimental.pallas import tpu as pltpu
from jax.sharding import PartitionSpec as P

HEADS = 20
HEAD_DIM = 32
HALF = 16
D = 640
FF = 2560
ROWS = 512
SEG = 256
QW = 480
OW = 160
EPS = 1e-05
SCALE = 1.0 / math.sqrt(HEAD_DIM)
SCALE2 = SCALE * math.log2(math.e)

bf16 = jnp.bfloat16
f32 = jnp.float32

NN = (((1,), (0,)), ((), ()))
NT = (((1,), (1,)), ((), ()))
TN = (((0,), (0,)), ((), ()))
TT = (((0,), (1,)), ((), ()))

VMEM = pl.BlockSpec(memory_space=pltpu.VMEM)
SMEM = pl.BlockSpec(memory_space=pltpu.SMEM)
ANY = pl.BlockSpec(memory_space=pl.ANY)
SHORT = pl.CostEstimate(flops=10**6, bytes_accessed=10**5, transcendentals=0)


def vmem(mebibytes):
    return pltpu.CompilerParams(vmem_limit_bytes=mebibytes * 2**20)


def dot(a, b, dims):
    return lax.dot_general(a, b, dims, preferred_element_type=f32)


def normalize(x):
    center = x - jnp.mean(x, axis=-1, keepdims=True)
    spread = jnp.mean(center * center, axis=-1, keepdims=True)
    rstd = lax.rsqrt(spread + EPS)
    return center * rstd, rstd


def first_row(quarters):
    start = jnp.int32(0)
    before = jnp.int32(0)
    for c in range(4):
        size = quarters[0, c]
        start = jnp.where(size == SEG, before, start)
        before = before + size
    return start


def rolled(ref, start):
    return pltpu.roll(ref[...].astype(f32), ROWS - start, 0)


def tables_kernel(quarters, freqs, cos, sin, mask):
    pos = lax.axis_index("seq")
    start = first_row(quarters)

    def crops(shape, dim, first):
        row = (lax.broadcasted_iota(jnp.int32, shape, dim) + (first + start)) % ROWS
        end = jnp.int32(0)
        crop = jnp.zeros(shape, jnp.int32)
        offset, length = crop, crop
        for c in range(4):
            size = quarters[0, c]
            begin, end = end, end + size
            crop = crop + (row >= end).astype(jnp.int32)
            inside = jnp.logical_and(row >= begin, row < end)
            offset = jnp.where(inside, begin, offset)
            length = jnp.where(inside, size, length)
        return crop, row - offset, length

    _, place, length = crops((HALF, ROWS), 1, 0)
    for p in range(4):
        angles = ((pos ^ p) * length + place).astype(f32) * freqs[...][:, 0:1]
        cos[p] = jnp.cos(angles)
        sin[p] = jnp.sin(angles)
    down = crops((SEG, SEG), 0, SEG)[0]
    along = crops((SEG, SEG), 1, SEG)[0]
    mask[...] = jnp.where(down == along, 0.0, -1e30)


def tables(quarters):
    freqs = np.float32(10000.0) ** (-np.arange(0, HEAD_DIM, 2).astype(np.float32) / np.float32(HEAD_DIM))
    table = jax.ShapeDtypeStruct((4, HALF, ROWS), f32)
    return pl.pallas_call(
        tables_kernel,
        in_specs=[SMEM, VMEM],
        out_specs=[VMEM] * 3,
        out_shape=[table, table, jax.ShapeDtypeStruct((SEG, SEG), f32)],
        compiler_params=vmem(60),
    )(quarters, jnp.asarray(np.repeat(freqs[:, None], 128, axis=1)))


def project_rows(p, x, wt, column, gain, shift, cos, sin, q_out, k_out, v_out, n_out):
    xhat, _ = normalize(x)
    normed = (xhat * gain + shift).astype(bf16)
    n_out[p] = normed
    for part in range(0 if q_out is not None else 1, 3):
        rows = slice(D * part, D * part + D)
        y = dot(wt[rows, :], normed, NT) + column[rows]
        if part == 2:
            v_out[p] = y.astype(bf16)
            continue
        c, s = cos[p], sin[p]
        for h in range(HEADS):
            a = y[32 * h : 32 * h + 16]
            b = y[32 * h + 16 : 32 * h + 32]
            r = jnp.concatenate([a * c - b * s, b * c + a * s], axis=0).astype(bf16)
            if part == 0:
                q_out[32 * h : 32 * h + 32, :] = r
            else:
                k_out[p, 32 * h : 32 * h + 32, :] = r


WPART = 512
PART = WPART // 4
PACK = WPART + ROWS


def pack_kernel(*refs):
    w, tok, out, part = refs[0], refs[1], refs[10], refs[11]
    out[0:QW, :] = w[...]
    out[WPART:PACK, :] = tok[...]
    rows = []
    for v in refs[2:10]:
        n = v.shape[0]
        row = v[...].astype(f32).reshape(1, n)
        rows.append(row if n == D else jnp.concatenate([row, jnp.zeros((1, D - n), f32)], axis=1))
    rows.append(jnp.zeros((WPART - QW - 8, D), f32))
    out[QW:WPART, :] = jnp.concatenate(rows, axis=0).astype(bf16)
    which = lax.axis_index("dp") & 3
    part[...] = out[pl.ds(pl.multiple_of(which * PART, PART), PART), :]


def pack(w, tok, vectors):
    return pl.pallas_call(
        pack_kernel,
        in_specs=[VMEM] * 10,
        out_specs=[VMEM] * 2,
        out_shape=[jax.ShapeDtypeStruct((PACK, D), bf16), jax.ShapeDtypeStruct((PART, D), bf16)],
        compiler_params=vmem(60),
        cost_estimate=SHORT,
    )(w, tok, *vectors)


def project_kernel(
    quarters, own, near, tok_far, tok_last, far0, far1, far2, last0, last1, last2, cos, sin,
    q_out, k_out, v_out, n_out, wt, rows_out, upb_out, vt, col, w_far, w_last,
):
    pos = lax.axis_index("seq")
    which = lax.axis_index("dp") & 3
    start = first_row(quarters)
    for whole, p0, p1, p2 in ((w_far, far0, far1, far2), (w_last, last0, last1, last2)):
        pieces = (p0[...], p1[...], p2[0:PART, :], p2[PART : 2 * PART, :])
        for i, piece in enumerate(pieces):
            whole[pl.ds(pl.multiple_of((which ^ i) * PART, PART), PART), :] = piece
    for p, m in enumerate((own, near, w_far, w_last)):
        wt[pl.ds(QW * (pos ^ p), QW), :] = m[0:QW, :]
        v = m[QW : QW + 16, :].astype(f32)[0:8]
        t = v.T
        col[pl.ds(QW * (pos ^ p), QW), :] = t[0:QW]
        vt[pl.ds(OW * (pos ^ p), OW), :] = t[0:OW]
        upb_out[p : p + 1, :] = v[7:8, :]
    rows = vt[...].T
    rows_out[...] = rows
    column = col[:, 0:1]
    gain, shift = rows[2:3], rows[3:4]
    toks = (own.at[pl.ds(WPART, ROWS), :], near.at[pl.ds(WPART, ROWS), :], tok_far, tok_last)
    for p, tok in enumerate(toks):
        project_rows(
            p, rolled(tok, start), wt, column, gain, shift, cos, sin,
            q_out if p == 0 else None, k_out, v_out, n_out,
        )


def project(quarters, parts, cos, sin):
    sds = jax.ShapeDtypeStruct
    kv = sds((4, D, ROWS), bf16)
    return pl.pallas_call(
        project_kernel,
        in_specs=[SMEM] + [VMEM] * 12,
        out_specs=[VMEM] * 7,
        out_shape=[
            sds((D, ROWS), bf16), kv, kv, sds((4, ROWS, D), bf16), sds((3 * D, D), bf16),
            sds((8, D), f32), sds((4, D), f32),
        ],
        scratch_shapes=[
            pltpu.VMEM((D, 8), f32), pltpu.VMEM((3 * D, 8), f32),
            pltpu.VMEM((WPART, D), bf16), pltpu.VMEM((WPART, D), bf16),
        ],
        compiler_params=vmem(60),
        cost_estimate=SHORT,
    )(quarters, *parts, cos, sin)


def attend_kernel(q_ref, k_ref, v_ref, mask_ref, o_ref, l_ref, *, heads):
    ones = jnp.ones((HALF, SEG), bf16)
    for h in range(heads):
        hs = slice(32 * h, 32 * h + 32)
        for seg in range(2):
            cs = slice(SEG * seg, SEG * seg + SEG)
            q = q_ref[hs, cs].T
            scores = []
            for p in range(4):
                s = dot(q, k_ref[p, hs, cs], NN)
                if seg == 1:
                    s = s + mask_ref[...]
                scores.append(s)
            top = scores[0]
            for s in scores[1:]:
                top = jnp.maximum(top, s)
            top = top.max(1, keepdims=True)
            acc = None
            for p in range(4):
                e = jnp.exp2((scores[p] - top) * SCALE2).astype(bf16)
                t = dot(e, jnp.concatenate([v_ref[p, hs, cs], ones], axis=0), NT)
                acc = t if acc is None else acc + t
            total = acc[:, HEAD_DIM : HEAD_DIM + 1]
            o_ref[hs, cs] = (acc[:, 0:HEAD_DIM] / total).T
            log_total = top * SCALE2 + jnp.log2(total)
            l_ref[h, :, cs] = jnp.broadcast_to(log_total, (SEG, 128)).T[0:1]


def attend(q, k, v, mask):
    heads = 5
    row = pl.BlockSpec((32 * heads, ROWS), lambda h: (h, 0))
    four = pl.BlockSpec((4, 32 * heads, ROWS), lambda h: (0, h, 0))
    return pl.pallas_call(
        functools.partial(attend_kernel, heads=heads),
        grid=(HEADS // heads,),
        in_specs=[row, four, four, pl.BlockSpec((SEG, SEG), lambda h: (0, 0))],
        out_specs=[row, pl.BlockSpec((heads, 1, ROWS), lambda h: (h, 0, 0))],
        out_shape=[
            jax.ShapeDtypeStruct((D, ROWS), f32),
            jax.ShapeDtypeStruct((HEADS, 1, ROWS), f32),
        ],
        compiler_params=vmem(60),
        cost_estimate=SHORT,
    )(q, k, v, mask)


GA = 1472
HD = 320


def middle_kernel(
    quarters, ctx_ref, tok, cot, wo0, wo1, wo2, wo3, vec, upb,
    up0, up1, up2, up3, dn0, dn1, dn2, dn3, dq2, dq3,
    out_ref, dmid_ref, dctx_ref, delta_ref, vecg_ref, upbg_ref, ga, gb,
    up_s, dn_s, wo_s, mid_s, n2_s, n2t_s, cot_s, acc_s, dn2_s, g_s, go_s, sems,
):
    pos = lax.axis_index("seq")
    start = first_row(quarters)
    copies = []
    half = lax.axis_index("dp") & 1
    for p, (u, d) in enumerate(((up0, dn0), (up1, dn1), (up2, dn2), (up3, dn3))):
        copies.append(pltpu.make_async_copy(u, up_s.at[p], sems.at[3 * p]))
        if p < 2:
            copies.append(pltpu.make_async_copy(d, dn_s.at[p], sems.at[3 * p + 1]))
            continue
        for i, h in enumerate((d, (dq2, dq3)[p - 2])):
            to = dn_s.at[p, pl.ds(pl.multiple_of(HD * (half ^ i), HD), HD), :]
            copies.append(pltpu.make_async_copy(h, to, sems.at[3 * p + 1 + i]))
    for c in copies:
        c.start()
    for p, wo in enumerate((wo0, wo1, wo2, wo3)):
        wo_s[pl.ds(OW * (pos ^ p), OW), :] = wo[...]
    ctx_low = ctx_ref[...].astype(bf16)
    out_bias, gain, shift, down_bias = (vec[i : i + 1, :] for i in (1, 4, 5, 6))
    mid = rolled(tok, start) + dot(wo_s[...], ctx_low, NN).T + out_bias
    mid_s[...] = mid
    xhat, rstd = normalize(mid)
    normed2 = (xhat * gain + shift).astype(bf16)
    n2_s[...] = normed2
    n2t_s[...] = normed2.T
    cot_s[...] = rolled(cot, start).astype(bf16)
    acc_s[...] = mid + down_bias
    dn2_s[...] = jnp.zeros_like(dn2_s)
    for c in copies:
        c.wait()

    def piece(p, carry):
        pre = dot(n2_s[...], up_s[p], NN) + upb[pl.ds(p, 1), :]
        d_act = dot(cot_s[...], dn_s[p], NT)
        cdf = 0.5 + 0.5 * lax.erf(pre * (1.0 / math.sqrt(2.0)))
        pdf = jnp.exp(-0.5 * pre * pre) * (1.0 / math.sqrt(2.0 * math.pi))
        act = (pre * cdf).astype(bf16)
        d_pre = (d_act * (cdf + pre * pdf)).astype(bf16)
        acc_s[...] += dot(act, dn_s[p], NN)
        dn2_s[...] += dot(d_pre, up_s[p], NT)
        g_s[p, 0:D, :] = dot(act, cot_s[...], TN).astype(bf16)
        g_s[p, D : 2 * D, :] = dot(n2t_s[...], d_pre, NN).astype(bf16)
        upbg_ref[pl.ds(p, 1), :] = jnp.sum(d_pre.astype(f32), axis=0, keepdims=True)
        return carry

    lax.fori_loop(0, 4, piece, 0)
    out_ref[...] = pltpu.roll(acc_s[...], start, 0).astype(bf16)
    xhat, rstd = normalize(mid_s[...])
    d_n2 = dn2_s[...]
    e = d_n2 * gain
    d_cot = cot_s[...].astype(f32)
    d_mid = d_cot + rstd * (
        e - jnp.mean(e, axis=-1, keepdims=True) - xhat * jnp.mean(e * xhat, axis=-1, keepdims=True)
    )
    dmid_ref[...] = d_mid
    d_attn = d_mid.astype(bf16)
    vecg_ref[0:1, :] = jnp.sum(d_attn.astype(f32), axis=0, keepdims=True)
    vecg_ref[1:3, :] = jnp.zeros((2, D), f32)
    vecg_ref[3:4, :] = jnp.sum(d_n2 * xhat, axis=0, keepdims=True)
    vecg_ref[4:5, :] = jnp.sum(d_n2, axis=0, keepdims=True)
    vecg_ref[5:6, :] = jnp.sum(d_cot, axis=0, keepdims=True)
    vecg_ref[6:8, :] = jnp.zeros((2, D), f32)
    d_attn_t = d_attn.T
    go_s[...] = dot(d_attn_t, ctx_ref[...].astype(bf16), NT).astype(bf16)
    for p in range(4):
        out = (ga, gb)[p % 2]
        out[p // 2, 0 : 2 * D, :] = g_s[p]
        out[p // 2, 2 * D : 2 * D + OW, :] = go_s[pl.ds(OW * (pos ^ p), OW), :]
        out[p // 2, 2 * D + OW : GA, :] = jnp.zeros((GA - 2 * D - OW, D), bf16)
    d_ctx = dot(wo_s[...], d_attn_t, TN).astype(bf16)
    dctx_ref[...] = d_ctx
    product = d_ctx.astype(f32) * ctx_ref[...]
    for h in range(HEADS):
        delta_ref[h] = jnp.sum(product[32 * h : 32 * h + 32], axis=0, keepdims=True)


def middle(quarters, ctx, tok, cot, wos, vec, upb, ups, downs):
    sds = jax.ShapeDtypeStruct
    big = sds((2, GA, D), bf16)
    return pl.pallas_call(
        middle_kernel,
        in_specs=[SMEM] + [VMEM] * 9 + [ANY] * 10,
        out_specs=[VMEM] * 8,
        out_shape=[
            sds((ROWS, D), bf16), sds((ROWS, D), f32), sds((D, ROWS), bf16), sds((HEADS, 1, ROWS), f32),
            sds((8, D), f32), sds((4, D), f32), big, big,
        ],
        scratch_shapes=[
            pltpu.VMEM((4, D, D), bf16), pltpu.VMEM((4, D, D), bf16), pltpu.VMEM((D, D), bf16),
            pltpu.VMEM((ROWS, D), f32), pltpu.VMEM((ROWS, D), bf16), pltpu.VMEM((D, ROWS), bf16),
            pltpu.VMEM((ROWS, D), bf16), pltpu.VMEM((ROWS, D), f32), pltpu.VMEM((ROWS, D), f32),
            pltpu.VMEM((4, 2 * D, D), bf16), pltpu.VMEM((D, D), bf16),
            pltpu.SemaphoreType.DMA((12,)),
        ],
        compiler_params=vmem(58),
        cost_estimate=SHORT,
    )(quarters, ctx, tok, cot, *wos, vec, upb, *ups, *downs)


BLOCK = 5
WIDE = 32 * BLOCK


def attend_back_step(q_ref, k_ref, v_ref, do_ref, l_ref, dl_ref, mask_ref, cos_ref, sin_ref, dq_ref, dk_ref, dv_ref):
    def back(g, c, s):
        a, b = g[0:HALF], g[HALF : 2 * HALF]
        return jnp.concatenate([a * c + b * s, b * c - a * s], axis=0).astype(bf16)

    for h in range(BLOCK):
        hs = slice(32 * h, 32 * h + 32)
        for seg in range(2):
            cs = slice(SEG * seg, SEG * seg + SEG)
            q, d_o = q_ref[hs, cs], do_ref[hs, cs]
            log_total, delta = l_ref[h, :, cs], dl_ref[h, :, cs]
            d_q = None
            for p in range(4):
                k = k_ref[p, hs, cs]
                v = v_ref[p, hs, cs]
                s = dot(k, q, TN)
                if seg == 1:
                    s = s + mask_ref[...]
                e = jnp.exp2(s * SCALE2 - log_total)
                d_s = (e * (dot(v, d_o, TN) - delta)).astype(bf16)
                dv_ref[p, hs, cs] = dot(d_o, e.astype(bf16), NT).astype(bf16)
                d_k = dot(q, d_s, NT) * SCALE
                dk_ref[p, hs, cs] = back(d_k, cos_ref[p, :, cs], sin_ref[p, :, cs])
                t = dot(k, d_s, NN)
                d_q = t if d_q is None else d_q + t
            dq_ref[hs, cs] = back(d_q * SCALE, cos_ref[0, :, cs], sin_ref[0, :, cs])


def back_specs(block):
    row = pl.BlockSpec((WIDE, ROWS), lambda h: (block(h), 0))
    four = pl.BlockSpec((4, WIDE, ROWS), lambda h: (0, block(h), 0))
    stat = pl.BlockSpec((BLOCK, 1, ROWS), lambda h: (block(h), 0, 0))
    table = pl.BlockSpec((4, HALF, ROWS), lambda h: (0, 0, 0))
    mask = pl.BlockSpec((SEG, SEG), lambda h: (0, 0))
    return [row, four, four, row, stat, stat, mask, table, table]


def result_specs(block):
    row = pl.BlockSpec((WIDE, ROWS), lambda h: (block(h), 0))
    four = pl.BlockSpec((4, WIDE, ROWS), lambda h: (0, block(h), 0))
    return [row, four, four]


def attend_back_part(operands, first, count):
    four = jax.ShapeDtypeStruct((4, WIDE * count, ROWS), bf16)
    return pl.pallas_call(
        attend_back_step,
        grid=(count,),
        in_specs=back_specs(lambda h: h + first),
        out_specs=result_specs(lambda h: h),
        out_shape=[jax.ShapeDtypeStruct((WIDE * count, ROWS), bf16), four, four],
        compiler_params=vmem(60),
        cost_estimate=SHORT,
    )(*operands)


GB = 512


def attend_back_kernel(*refs):
    ins, first, second, (normed, wt, rows, vec_g, upb_g) = refs[0:9], refs[9:12], refs[12:15], refs[15:20]
    dq_ref, dk_ref, dv_ref, ga, gb = refs[20:25]
    g_s, b_s, v_s, o_s = refs[25:]
    step = pl.program_id(0)
    last = HEADS // BLOCK - 1
    outs = (dq_ref, dk_ref, dv_ref)

    @pl.when(step == 0)
    def _():
        for out, part in zip(outs, first):
            out[...] = part[...]

    @pl.when(jnp.logical_and(step > 0, step < last))
    def _():
        for out, part in zip(outs, second):
            out[...] = part[...]

    @pl.when(step == last)
    def _():
        attend_back_step(*ins, *outs)

    row = pl.multiple_of(step * WIDE, WIDE)
    g_s[pl.ds(row, WIDE), :] = dot(dq_ref[...], normed[0], NN)
    total = jnp.sum(dq_ref[...].astype(f32), axis=1, keepdims=True)
    b_s[pl.ds(row, WIDE), :] = jnp.broadcast_to(total, (WIDE, 8))
    for part, ref in ((1, dk_ref), (2, dv_ref)):
        g = b = None
        for p in range(4):
            t = dot(ref[p], normed[p], NN)
            u = ref[p].astype(f32)
            g = t if g is None else g + t
            b = u if b is None else b + u
        g_s[pl.ds(D * part + row, WIDE), :] = g
        total = jnp.sum(b, axis=1, keepdims=True)
        b_s[pl.ds(D * part + row, WIDE), :] = jnp.broadcast_to(total, (WIDE, 8))

    @pl.when(step == last)
    def _():
        pos = lax.axis_index("seq")
        w = wt[...].astype(f32)
        both = jnp.sum(w * g_s[...], axis=0, keepdims=True)
        shift_g = jnp.sum(w * b_s[:, 0:1], axis=0, keepdims=True)
        gain_g = (both - rows[3:4, :] * shift_g) / rows[2:3, :]
        v_s[...] = jnp.concatenate([vec_g[0:1, :], gain_g, shift_g, vec_g[3:8, :]], axis=0).T
        o_s[...] = jnp.zeros_like(o_s)
        for p in range(4):
            out = (ga, gb)[p % 2]
            own = pos ^ p
            out[p // 2, 0:QW, :] = g_s[pl.ds(QW * own, QW), :].astype(bf16)
            o_s[0:8, 0:OW] = v_s[pl.ds(OW * own, OW), :].T
            o_s[8:16, 0:QW] = b_s[pl.ds(QW * own, QW), :].T
            o_s[16:24, :] = jnp.broadcast_to(upb_g[p : p + 1, :], (8, D))
            out[p // 2, QW:GB, :] = o_s[...].astype(bf16)


def attend_back(operands, first, second, normed, wt, rows, vec_g, upb_g):
    steps = HEADS // BLOCK

    def whole(*shape):
        return pl.BlockSpec(shape, lambda h: (0,) * len(shape))

    four = jax.ShapeDtypeStruct((4, D, ROWS), bf16)
    block = jax.ShapeDtypeStruct((2, GB, D), bf16)
    return pl.pallas_call(
        attend_back_kernel,
        grid=(steps,),
        in_specs=back_specs(lambda h: steps - 1)
        + result_specs(lambda h: 0)
        + result_specs(lambda h: jnp.clip(h - 1, 0, steps - 3))
        + [whole(4, ROWS, D), whole(3 * D, D), whole(8, D), whole(8, D), whole(4, D)],
        out_specs=result_specs(lambda h: h) + [whole(2, GB, D), whole(2, GB, D)],
        out_shape=[jax.ShapeDtypeStruct((D, ROWS), bf16), four, four, block, block],
        scratch_shapes=[
            pltpu.VMEM((3 * D, D), f32), pltpu.VMEM((3 * D, 8), f32), pltpu.VMEM((D, 8), f32), pltpu.VMEM((32, D), f32),
        ],
        compiler_params=vmem(60),
        cost_estimate=SHORT,
    )(*operands, *first, *second, normed, wt, rows, vec_g, upb_g)


def rows_back_kernel(dq, dk, dv, wt, dn0, dnx, dnb):
    for p, out in ((1, dnb.at[0]), (3, dnb.at[1]), (2, dnx), (0, dn0)):
        d_n = dot(dk[p], wt[D : 2 * D, :], TN) + dot(dv[p], wt[2 * D : 3 * D, :], TN)
        if p == 0:
            d_n = d_n + dot(dq[...], wt[0:D, :], TN)
        out[...] = d_n.astype(bf16)


def rows_back(dq, dk, dv, wt):
    rows = jax.ShapeDtypeStruct((ROWS, D), bf16)
    return pl.pallas_call(
        rows_back_kernel,
        in_specs=[VMEM] * 4,
        out_specs=[VMEM] * 3,
        out_shape=[rows, rows, jax.ShapeDtypeStruct((2, ROWS, D), bf16)],
        compiler_params=vmem(60),
        cost_estimate=SHORT,
    )(dq, dk, dv, wt)


def finish_kernel(quarters, tok, rows, own, core, across, d_mid, out):
    start = first_row(quarters)
    xhat, rstd = normalize(rolled(tok, start))
    d_n = own[...].astype(f32) + core[0].astype(f32) + across[...].astype(f32)
    e = d_n * rows[2:3, :]
    grad = d_mid[...] + rstd * (
        e - jnp.mean(e, axis=-1, keepdims=True) - xhat * jnp.mean(e * xhat, axis=-1, keepdims=True)
    )
    out[...] = pltpu.roll(grad, start, 0)


def finish(quarters, tok, rows, own, core, across, d_mid):
    return pl.pallas_call(
        finish_kernel,
        in_specs=[SMEM] + [VMEM] * 6,
        out_specs=VMEM,
        out_shape=jax.ShapeDtypeStruct((ROWS, D), f32),
        compiler_params=vmem(16),
        cost_estimate=SHORT,
    )(quarters, tok, rows, own, core, across, d_mid)


def place(parts, total):
    group = lax.axis_index("dp")
    y, z = group & 1, (group >> 1) & 1
    for (my, mz), part in parts:
        n = part.shape[0]
        row = ((y ^ my) * 2 + (z ^ mz)) * n
        total[pl.ds(pl.multiple_of(row, 8), n), :] = part.astype(f32)


def place_a_kernel(*refs):
    down, up, out, total = refs[4:]
    place([((m & 1, m >> 1), ref[...]) for m, ref in enumerate(refs[:4])], total)
    down[...] = total[0:D, :]
    up[...] = total[D : 2 * D, :]
    out[...] = total[2 * D : 2 * D + OW, :]


def place_b_kernel(*refs):
    qkv, six, bias, upb, total = refs[4:]
    place([((m & 1, m >> 1), ref[...]) for m, ref in enumerate(refs[:4])], total)
    qkv[...] = total[0:QW, :]
    six[...] = total[QW : QW + 8, 0:OW]
    bias[...] = total[QW + 8 : QW + 9, 0:QW]
    upb[...] = total[QW + 16 : QW + 17, :]


def place_call(kernel, parts, shapes, rows):
    return pl.pallas_call(
        kernel,
        in_specs=[VMEM] * len(parts),
        out_specs=[VMEM] * len(shapes),
        out_shape=[jax.ShapeDtypeStruct(s, f32) for s in shapes],
        scratch_shapes=[pltpu.VMEM((rows, D), f32)],
        compiler_params=vmem(24),
        cost_estimate=SHORT,
    )(*parts)


def tie(terms, *others):
    return lax.optimization_barrier((tuple(terms),) + others)[0]


def after(x, *others):
    return lax.optimization_barrier((x,) + others)[0]


def local(
    tokens, cotangent, quarters, qkv_weight, qkv_bias, out_weight, out_bias, attn_gain, attn_shift,
    ffn_gain, ffn_shift, up_weight, up_bias, down_weight, down_bias, *, n_dp,
):
    group = lax.axis_index("dp")

    def swap(x, seq_mask, dp_mask=0):
        pairs = []
        for s in range(4):
            for d in range(n_dp):
                pairs.append((s * n_dp + d, (s ^ seq_mask) * n_dp + (d ^ dp_mask)))
        return lax.ppermute(x, ("seq", "dp"), pairs)

    tok, cot = tokens[0], cotangent[0]
    vectors = (qkv_bias, out_bias, attn_gain, attn_shift, ffn_gain, ffn_shift, down_bias, up_bias)
    own, part = pack(qkv_weight.T, tok, vectors)
    far0 = swap(part, 2)
    near = swap(own, 1)
    tok_far = swap(after(tok, far0), 2)
    far1 = swap(far0, 0, 1)
    cos, sin, mask = tables(after(quarters, far0))
    far2 = swap(jnp.concatenate([after(far0, mask), far1]), 0, 2)
    last = [swap(x, 1) for x in (far0, far1, far2)]
    tok_last = swap(tok_far, 1)
    q, k, v, normed, wt, rows, upb = project(
        quarters, (own, near, tok_far, tok_last, far0, far1, far2, *last), cos, sin
    )
    half = lax.dynamic_slice_in_dim(down_weight, (group & 1) * HD, HD)
    wo, half = tie((out_weight.T, half), tok_far)
    wo_far, wo_near = swap(wo, 2), swap(wo, 1)
    dn_far, dn_near = swap(half, 2), swap(down_weight, 1)
    wo_far, dn_far = tie((wo_far, dn_far), q)
    wo_last, dn_last = swap(wo_far, 1), swap(dn_far, 1)
    dn_far2 = swap(dn_far, 0, 1)
    up_far, up_near = swap(after(up_weight, wo_far), 2), swap(up_weight, 1)
    ctx, log_total = attend(after(q, wo_far, dn_far), k, v, mask)
    up_far, dn_far2 = tie((up_far, dn_far2), log_total)
    up_last, dn_last2 = swap(up_far, 1), swap(dn_far2, 1)
    out, d_mid, d_ctx, delta, vec_g, upb_g, ga, gb = middle(
        quarters, ctx, tok, cot, (out_weight.T, wo_near, wo_far, wo_last), rows, upb,
        (up_weight, up_near, up_far, up_last),
        (down_weight, dn_near, dn_far, dn_last, dn_far2, dn_last2),
    )

    bits = n_dp.bit_length() - 1
    y, z = group & 1, (group >> 1) & 1

    def total(terms):
        s = terms[0].astype(f32)
        for t in terms[1:]:
            s = s + t.astype(f32)
        return s.astype(bf16)

    def cube_parts(a, b):
        n = a.shape[1] // 4

        def part(m):
            quarter = (y ^ ((m >> 1) & 1)) * 2 + (z ^ (m >> 2))
            return total([lax.dynamic_slice(t, (m & 1, quarter * n, 0), (1, n, D))[0] for t in (a, b)])

        return tuple(part(m) for m in range(8))

    def crossing(parts, which):
        return tuple(swap(part, 2 * (m & 1), m >> 1) for part, m in zip(parts, which))

    def square_parts(a, b):
        h = a.shape[1] // 2

        def part(m):
            first = (y ^ (m >> 1)) * h
            return total([lax.dynamic_slice(t, (m & 1, first, 0), (1, h, D))[0] for t in (a, b)])

        return tuple(part(m) for m in range(4))

    def half_parts(terms):
        n = terms[0].shape[0] // 2
        return tuple(total([lax.dynamic_slice(t, ((z ^ m) * n, 0), (n, D)) for t in terms]) for m in (0, 1))

    def rest(s):
        for b in range(3, bits):
            s = total([s, swap(s, 0, 1 << b)])
        return s

    args = (k, v, d_ctx, log_total, delta, mask, cos, sin)
    gb_in = swap(gb, 1)
    first = attend_back_part((q,) + args, 0, 1)
    partsa = cube_parts(*tie((ga, gb_in), first[0]))
    one = crossing([partsa[m] for m in (1, 2, 4, 7)], (1, 2, 4, 7))
    second = attend_back_part((after(q, *partsa),) + args, 1, 2)
    one = tie(one, second[0])
    later = tie([partsa[m] for m in (3, 5, 6)], *one)
    two = crossing(later, (3, 5, 6))
    dq, dk, dv, ha, hb = attend_back(
        (after(q, *later),) + args, first, second, normed, wt, rows, vec_g, upb_g
    )
    parta = total((partsa[0],) + one + tie(two, dq))
    parta_in = swap(parta, 0, 4)
    hb_in = swap(after(hb, parta), 1)
    partsb = square_parts(ha, hb_in)
    squareb = partsb[0:1] + crossing(partsb[1:], (1, 2, 3))
    dn0, dnx, dnb = rows_back(after(dq, *partsb), dk, dv, wt)
    keepb, sendb = half_parts(tie(squareb, dn0))
    sendb_in = swap(sendb, 0, 2)
    suma = rest(total([parta, after(parta_in, sendb)]))
    alla = (suma,) + tuple(swap(suma, 0, m) for m in (1, 2, 3))
    core = swap(after(dnb, suma), 1)
    d_sum = total([dnx, core[1]])
    across = swap(d_sum, 2)
    partb = total([keepb, after(sendb_in, d_sum)])
    partb_in = swap(partb, 0, 4)
    sumb = rest(total([partb, partb_in]))
    alla = tie(alla, sumb)
    sumb = after(sumb, *alla)
    allb = (sumb,) + tuple(swap(sumb, 0, m) for m in (1, 2, 3))
    g_down, g_up, g_out = place_call(place_a_kernel, alla, ((D, D), (D, D), (OW, D)), GA)
    grad_tok = finish(quarters, tok, rows, after(dn0, g_down), core, across, d_mid)
    g_qkv, six, g_bias, g_upb = place_call(
        place_b_kernel, tie(allb, grad_tok), ((QW, D), (8, OW), (1, QW), (1, D)), GB
    )

    return (
        out[None], grad_tok[None], g_qkv.T, g_bias[0], g_out.T, six[0], six[1], six[2], six[3], six[4],
        g_up, g_upb[0], g_down, six[5],
    )


def solution(mesh):
    rows, vector = P("dp", "seq", None), P("seq")
    columns = P(None, "seq")
    return jax.shard_map(
        functools.partial(local, n_dp=mesh.shape["dp"]),
        mesh=mesh,
        in_specs=(rows, rows, P("dp", None), columns, vector, columns, vector, vector, vector, vector, vector,
                  columns, vector, P("seq", None), vector),
        out_specs=(rows, rows, columns, vector, columns, vector, vector, vector, vector, vector,
                   columns, vector, P("seq", None), vector),
        check_vma=False,
    )
```

```python
import functools
import math

import jax
import jax.numpy as jnp
import numpy as np
from jax import lax
from jax.experimental import pallas as pl
from jax.experimental.pallas import tpu as pltpu
from jax.sharding import PartitionSpec as P

HEADS = 20
HEAD_DIM = 32
HALF = 16
D = 640
FF = 2560
ROWS = 512
SEG = 256
QW = 480
OW = 160
EPS = 1e-05
SCALE = 1.0 / math.sqrt(HEAD_DIM)
SCALE2 = SCALE * math.log2(math.e)

bf16 = jnp.bfloat16
f32 = jnp.float32

NN = (((1,), (0,)), ((), ()))
NT = (((1,), (1,)), ((), ()))
TN = (((0,), (0,)), ((), ()))
TT = (((0,), (1,)), ((), ()))

VMEM = pl.BlockSpec(memory_space=pltpu.VMEM)
SMEM = pl.BlockSpec(memory_space=pltpu.SMEM)
ANY = pl.BlockSpec(memory_space=pl.ANY)
SHORT = pl.CostEstimate(flops=10**6, bytes_accessed=10**5, transcendentals=0)


def vmem(mebibytes):
    return pltpu.CompilerParams(vmem_limit_bytes=mebibytes * 2**20)


def dot(a, b, dims):
    return lax.dot_general(a, b, dims, preferred_element_type=f32)


def normalize(x):
    center = x - jnp.mean(x, axis=-1, keepdims=True)
    spread = jnp.mean(center * center, axis=-1, keepdims=True)
    rstd = lax.rsqrt(spread + EPS)
    return center * rstd, rstd


def first_row(quarters):
    start = jnp.int32(0)
    before = jnp.int32(0)
    for c in range(4):
        size = quarters[0, c]
        start = jnp.where(size == SEG, before, start)
        before = before + size
    return start


def rolled(ref, start):
    return pltpu.roll(ref[...].astype(f32), ROWS - start, 0)


def tables_kernel(quarters, freqs, cos, sin, mask):
    pos = lax.axis_index("seq")
    start = first_row(quarters)

    def crops(shape, dim, first):
        row = (lax.broadcasted_iota(jnp.int32, shape, dim) + (first + start)) % ROWS
        end = jnp.int32(0)
        crop = jnp.zeros(shape, jnp.int32)
        offset, length = crop, crop
        for c in range(4):
            size = quarters[0, c]
            begin, end = end, end + size
            crop = crop + (row >= end).astype(jnp.int32)
            inside = jnp.logical_and(row >= begin, row < end)
            offset = jnp.where(inside, begin, offset)
            length = jnp.where(inside, size, length)
        return crop, row - offset, length

    _, place, length = crops((HALF, ROWS), 1, 0)
    for p in range(4):
        angles = ((pos ^ p) * length + place).astype(f32) * freqs[...][:, 0:1]
        cos[p] = jnp.cos(angles)
        sin[p] = jnp.sin(angles)
    down = crops((SEG, SEG), 0, SEG)[0]
    along = crops((SEG, SEG), 1, SEG)[0]
    mask[...] = jnp.where(down == along, 0.0, -1e30)


def tables(quarters):
    freqs = np.float32(10000.0) ** (-np.arange(0, HEAD_DIM, 2).astype(np.float32) / np.float32(HEAD_DIM))
    table = jax.ShapeDtypeStruct((4, HALF, ROWS), f32)
    return pl.pallas_call(
        tables_kernel,
        in_specs=[SMEM, VMEM],
        out_specs=[VMEM] * 3,
        out_shape=[table, table, jax.ShapeDtypeStruct((SEG, SEG), f32)],
        compiler_params=vmem(60),
    )(quarters, jnp.asarray(np.repeat(freqs[:, None], 128, axis=1)))


def project_rows(p, x, wt, column, gain, shift, cos, sin, q_out, k_out, v_out, n_out):
    xhat, _ = normalize(x)
    normed = (xhat * gain + shift).astype(bf16)
    n_out[p] = normed
    for part in range(0 if q_out is not None else 1, 3):
        rows = slice(D * part, D * part + D)
        y = dot(wt[rows, :], normed, NT) + column[rows]
        if part == 2:
            v_out[p] = y.astype(bf16)
            continue
        c, s = cos[p], sin[p]
        for h in range(HEADS):
            a = y[32 * h : 32 * h + 16]
            b = y[32 * h + 16 : 32 * h + 32]
            r = jnp.concatenate([a * c - b * s, b * c + a * s], axis=0).astype(bf16)
            if part == 0:
                q_out[32 * h : 32 * h + 32, :] = r
            else:
                k_out[p, 32 * h : 32 * h + 32, :] = r


WPART = 512
PART = WPART // 4
PACK = WPART + ROWS


def pack_kernel(*refs):
    w, tok, out, part = refs[0], refs[1], refs[10], refs[11]
    out[0:QW, :] = w[...]
    out[WPART:PACK, :] = tok[...]
    rows = []
    for v in refs[2:10]:
        n = v.shape[0]
        row = v[...].astype(f32).reshape(1, n)
        rows.append(row if n == D else jnp.concatenate([row, jnp.zeros((1, D - n), f32)], axis=1))
    rows.append(jnp.zeros((WPART - QW - 8, D), f32))
    out[QW:WPART, :] = jnp.concatenate(rows, axis=0).astype(bf16)
    which = lax.axis_index("dp") & 3
    part[...] = out[pl.ds(pl.multiple_of(which * PART, PART), PART), :]


def pack(w, tok, vectors):
    return pl.pallas_call(
        pack_kernel,
        in_specs=[VMEM] * 10,
        out_specs=[VMEM] * 2,
        out_shape=[jax.ShapeDtypeStruct((PACK, D), bf16), jax.ShapeDtypeStruct((PART, D), bf16)],
        compiler_params=vmem(60),
        cost_estimate=SHORT,
    )(w, tok, *vectors)


def project_kernel(
    quarters, own, near, tok_far, tok_last, far0, far1, far2, last0, last1, last2, cos, sin,
    q_to, k_to, v_to, n_to, wt_to, rows_out, upb_out,
    q_out, k_out, v_out, n_out, wt, vt, col, w_far, w_last, sems,
):
    pos = lax.axis_index("seq")
    which = lax.axis_index("dp") & 3
    start = first_row(quarters)
    for whole, p0, p1, p2 in ((w_far, far0, far1, far2), (w_last, last0, last1, last2)):
        pieces = (p0[...], p1[...], p2[0:PART, :], p2[PART : 2 * PART, :])
        for i, piece in enumerate(pieces):
            whole[pl.ds(pl.multiple_of((which ^ i) * PART, PART), PART), :] = piece
    for p, m in enumerate((own, near, w_far, w_last)):
        wt[pl.ds(QW * (pos ^ p), QW), :] = m[0:QW, :]
        v = m[QW : QW + 16, :].astype(f32)[0:8]
        t = v.T
        col[pl.ds(QW * (pos ^ p), QW), :] = t[0:QW]
        vt[pl.ds(OW * (pos ^ p), OW), :] = t[0:OW]
        upb_out[p : p + 1, :] = v[7:8, :]
    sends = []

    def send(source, to):
        copy = pltpu.make_async_copy(source, to, sems.at[len(sends)])
        copy.start()
        sends.append(copy)

    send(wt, wt_to)
    rows = vt[...].T
    rows_out[...] = rows
    column = col[:, 0:1]
    gain, shift = rows[2:3], rows[3:4]
    toks = (own.at[pl.ds(WPART, ROWS), :], near.at[pl.ds(WPART, ROWS), :], tok_far, tok_last)
    for p, tok in enumerate(toks):
        project_rows(
            p, rolled(tok, start), wt, column, gain, shift, cos, sin,
            q_out if p == 0 else None, k_out, v_out, n_out,
        )
        if p == 0:
            send(q_out, q_to)
        for source, to in ((k_out, k_to), (v_out, v_to), (n_out, n_to)):
            send(source.at[p], to.at[p])
    for copy in sends:
        copy.wait()


def project(quarters, parts, cos, sin):
    sds = jax.ShapeDtypeStruct
    kv = sds((4, D, ROWS), bf16)
    return pl.pallas_call(
        project_kernel,
        in_specs=[SMEM] + [VMEM] * 12,
        out_specs=[ANY] * 5 + [VMEM] * 2,
        out_shape=[
            sds((D, ROWS), bf16), kv, kv, sds((4, ROWS, D), bf16), sds((3 * D, D), bf16),
            sds((8, D), f32), sds((4, D), f32),
        ],
        scratch_shapes=[
            pltpu.VMEM((D, ROWS), bf16), pltpu.VMEM((4, D, ROWS), bf16), pltpu.VMEM((4, D, ROWS), bf16),
            pltpu.VMEM((4, ROWS, D), bf16), pltpu.VMEM((3 * D, D), bf16),
            pltpu.VMEM((D, 8), f32), pltpu.VMEM((3 * D, 8), f32),
            pltpu.VMEM((WPART, D), bf16), pltpu.VMEM((WPART, D), bf16), pltpu.SemaphoreType.DMA((14,)),
        ],
        compiler_params=vmem(60),
        cost_estimate=SHORT,
    )(quarters, *parts, cos, sin)


def attend_kernel(q_ref, k_ref, v_ref, mask_ref, o_ref, l_ref, *, heads):
    ones = jnp.ones((HALF, SEG), bf16)
    for h in range(heads):
        hs = slice(32 * h, 32 * h + 32)
        for seg in range(2):
            cs = slice(SEG * seg, SEG * seg + SEG)
            q = q_ref[hs, cs].T
            scores = []
            for p in range(4):
                s = dot(q, k_ref[p, hs, cs], NN)
                if seg == 1:
                    s = s + mask_ref[...]
                scores.append(s)
            top = scores[0]
            for s in scores[1:]:
                top = jnp.maximum(top, s)
            top = top.max(1, keepdims=True)
            acc = None
            for p in range(4):
                e = jnp.exp2((scores[p] - top) * SCALE2).astype(bf16)
                t = dot(e, jnp.concatenate([v_ref[p, hs, cs], ones], axis=0), NT)
                acc = t if acc is None else acc + t
            total = acc[:, HEAD_DIM : HEAD_DIM + 1]
            o_ref[hs, cs] = (acc[:, 0:HEAD_DIM] / total).T
            log_total = top * SCALE2 + jnp.log2(total)
            l_ref[h, :, cs] = jnp.broadcast_to(log_total, (SEG, 128)).T[0:1]


def attend(q, k, v, mask):
    heads = 5
    row = pl.BlockSpec((32 * heads, ROWS), lambda h: (h, 0))
    four = pl.BlockSpec((4, 32 * heads, ROWS), lambda h: (0, h, 0))
    return pl.pallas_call(
        functools.partial(attend_kernel, heads=heads),
        grid=(HEADS // heads,),
        in_specs=[row, four, four, pl.BlockSpec((SEG, SEG), lambda h: (0, 0))],
        out_specs=[row, pl.BlockSpec((heads, 1, ROWS), lambda h: (h, 0, 0))],
        out_shape=[
            jax.ShapeDtypeStruct((D, ROWS), f32),
            jax.ShapeDtypeStruct((HEADS, 1, ROWS), f32),
        ],
        compiler_params=vmem(60),
        cost_estimate=SHORT,
    )(q, k, v, mask)


GA = 1472
HD = 320


def middle_kernel(
    quarters, ctx_ref, tok, cot, wo0, wo1, wo2, wo3, vec, upb,
    up0, up1, up2, up3, dn0, dn1, dn2, dn3, dq2, dq3,
    out_ref, dmid_ref, dctx_ref, delta_ref, vecg_ref, upbg_ref, ga, gb,
    up_s, dn_s, wo_s, mid_s, n2_s, n2t_s, cot_s, acc_s, dn2_s, g_s, go_s, goo_s, sems, out_sems,
):
    pos = lax.axis_index("seq")
    start = first_row(quarters)
    copies = []
    half = lax.axis_index("dp") & 1
    for p, (u, d) in enumerate(((up0, dn0), (up1, dn1), (up2, dn2), (up3, dn3))):
        copies.append(pltpu.make_async_copy(u, up_s.at[p], sems.at[3 * p]))
        if p < 2:
            copies.append(pltpu.make_async_copy(d, dn_s.at[p], sems.at[3 * p + 1]))
            continue
        for i, h in enumerate((d, (dq2, dq3)[p - 2])):
            to = dn_s.at[p, pl.ds(pl.multiple_of(HD * (half ^ i), HD), HD), :]
            copies.append(pltpu.make_async_copy(h, to, sems.at[3 * p + 1 + i]))
    for c in copies:
        c.start()
    for p, wo in enumerate((wo0, wo1, wo2, wo3)):
        wo_s[pl.ds(OW * (pos ^ p), OW), :] = wo[...]
    ctx_low = ctx_ref[...].astype(bf16)
    out_bias, gain, shift, down_bias = (vec[i : i + 1, :] for i in (1, 4, 5, 6))
    mid = rolled(tok, start) + dot(wo_s[...], ctx_low, NN).T + out_bias
    mid_s[...] = mid
    xhat, rstd = normalize(mid)
    normed2 = (xhat * gain + shift).astype(bf16)
    n2_s[...] = normed2
    n2t_s[...] = normed2.T
    cot_s[...] = rolled(cot, start).astype(bf16)
    acc_s[...] = mid + down_bias
    dn2_s[...] = jnp.zeros_like(dn2_s)
    for c in copies:
        c.wait()

    sends = []

    def send(p, source, first, count, slot):
        to = (ga, gb)[p % 2].at[p // 2, pl.ds(first, count), :]
        copy = pltpu.make_async_copy(source, to, out_sems.at[slot])
        copy.start()
        sends.append(copy)

    def piece(p, carry):
        pre = dot(n2_s[...], up_s[p], NN) + upb[pl.ds(p, 1), :]
        d_act = dot(cot_s[...], dn_s[p], NT)
        cdf = 0.5 + 0.5 * lax.erf(pre * (1.0 / math.sqrt(2.0)))
        pdf = jnp.exp(-0.5 * pre * pre) * (1.0 / math.sqrt(2.0 * math.pi))
        act = (pre * cdf).astype(bf16)
        d_pre = (d_act * (cdf + pre * pdf)).astype(bf16)
        acc_s[...] += dot(act, dn_s[p], NN)
        dn2_s[...] += dot(d_pre, up_s[p], NT)
        g_s[p, 0:D, :] = dot(act, cot_s[...], TN).astype(bf16)
        g_s[p, D : 2 * D, :] = dot(n2t_s[...], d_pre, NN).astype(bf16)
        upbg_ref[pl.ds(p, 1), :] = jnp.sum(d_pre.astype(f32), axis=0, keepdims=True)
        return carry

    lax.fori_loop(0, 4, piece, 0)
    for p in range(4):
        send(p, g_s.at[p], 0, 2 * D, p)

    out_ref[...] = pltpu.roll(acc_s[...], start, 0).astype(bf16)
    xhat, rstd = normalize(mid_s[...])
    d_n2 = dn2_s[...]
    e = d_n2 * gain
    d_cot = cot_s[...].astype(f32)
    d_mid = d_cot + rstd * (
        e - jnp.mean(e, axis=-1, keepdims=True) - xhat * jnp.mean(e * xhat, axis=-1, keepdims=True)
    )
    dmid_ref[...] = d_mid
    d_attn = d_mid.astype(bf16)
    vecg_ref[0:1, :] = jnp.sum(d_attn.astype(f32), axis=0, keepdims=True)
    vecg_ref[1:3, :] = jnp.zeros((2, D), f32)
    vecg_ref[3:4, :] = jnp.sum(d_n2 * xhat, axis=0, keepdims=True)
    vecg_ref[4:5, :] = jnp.sum(d_n2, axis=0, keepdims=True)
    vecg_ref[5:6, :] = jnp.sum(d_cot, axis=0, keepdims=True)
    vecg_ref[6:8, :] = jnp.zeros((2, D), f32)
    d_attn_t = d_attn.T
    go_s[...] = dot(d_attn_t, ctx_ref[...].astype(bf16), NT).astype(bf16)
    for p in range(4):
        goo_s[p, 0:OW, :] = go_s[pl.ds(OW * (pos ^ p), OW), :]
        goo_s[p, OW:, :] = jnp.zeros((GA - 2 * D - OW, D), bf16)
        send(p, goo_s.at[p], 2 * D, GA - 2 * D, 4 + p)
    d_ctx = dot(wo_s[...], d_attn_t, TN).astype(bf16)
    dctx_ref[...] = d_ctx
    product = d_ctx.astype(f32) * ctx_ref[...]
    for h in range(HEADS):
        delta_ref[h] = jnp.sum(product[32 * h : 32 * h + 32], axis=0, keepdims=True)
    for copy in sends:
        copy.wait()


def middle(quarters, ctx, tok, cot, wos, vec, upb, ups, downs):
    sds = jax.ShapeDtypeStruct
    big = sds((2, GA, D), bf16)
    return pl.pallas_call(
        middle_kernel,
        in_specs=[SMEM] + [VMEM] * 9 + [ANY] * 10,
        out_specs=[VMEM] * 6 + [ANY] * 2,
        out_shape=[
            sds((ROWS, D), bf16), sds((ROWS, D), f32), sds((D, ROWS), bf16), sds((HEADS, 1, ROWS), f32),
            sds((8, D), f32), sds((4, D), f32), big, big,
        ],
        scratch_shapes=[
            pltpu.VMEM((4, D, D), bf16), pltpu.VMEM((4, D, D), bf16), pltpu.VMEM((D, D), bf16),
            pltpu.VMEM((ROWS, D), f32), pltpu.VMEM((ROWS, D), bf16), pltpu.VMEM((D, ROWS), bf16),
            pltpu.VMEM((ROWS, D), bf16), pltpu.VMEM((ROWS, D), f32), pltpu.VMEM((ROWS, D), f32),
            pltpu.VMEM((4, 2 * D, D), bf16), pltpu.VMEM((D, D), bf16),
            pltpu.VMEM((4, GA - 2 * D, D), bf16),
            pltpu.SemaphoreType.DMA((12,)), pltpu.SemaphoreType.DMA((8,)),
        ],
        compiler_params=vmem(58),
        cost_estimate=SHORT,
    )(quarters, ctx, tok, cot, *wos, vec, upb, *ups, *downs)


BLOCK = 5
WIDE = 32 * BLOCK


def attend_back_step(q_ref, k_ref, v_ref, do_ref, l_ref, dl_ref, mask_ref, cos_ref, sin_ref, dq_ref, dk_ref, dv_ref):
    def back(g, c, s):
        a, b = g[0:HALF], g[HALF : 2 * HALF]
        return jnp.concatenate([a * c + b * s, b * c - a * s], axis=0).astype(bf16)

    for h in range(BLOCK):
        hs = slice(32 * h, 32 * h + 32)
        for seg in range(2):
            cs = slice(SEG * seg, SEG * seg + SEG)
            q, d_o = q_ref[hs, cs], do_ref[hs, cs]
            log_total, delta = l_ref[h, :, cs], dl_ref[h, :, cs]
            d_q = None
            for p in range(4):
                k = k_ref[p, hs, cs]
                v = v_ref[p, hs, cs]
                s = dot(k, q, TN)
                if seg == 1:
                    s = s + mask_ref[...]
                e = jnp.exp2(s * SCALE2 - log_total)
                d_s = (e * (dot(v, d_o, TN) - delta)).astype(bf16)
                dv_ref[p, hs, cs] = dot(d_o, e.astype(bf16), NT).astype(bf16)
                d_k = dot(q, d_s, NT) * SCALE
                dk_ref[p, hs, cs] = back(d_k, cos_ref[p, :, cs], sin_ref[p, :, cs])
                t = dot(k, d_s, NN)
                d_q = t if d_q is None else d_q + t
            dq_ref[hs, cs] = back(d_q * SCALE, cos_ref[0, :, cs], sin_ref[0, :, cs])


def back_specs(block):
    row = pl.BlockSpec((WIDE, ROWS), lambda h: (block(h), 0))
    four = pl.BlockSpec((4, WIDE, ROWS), lambda h: (0, block(h), 0))
    stat = pl.BlockSpec((BLOCK, 1, ROWS), lambda h: (block(h), 0, 0))
    table = pl.BlockSpec((4, HALF, ROWS), lambda h: (0, 0, 0))
    mask = pl.BlockSpec((SEG, SEG), lambda h: (0, 0))
    return [row, four, four, row, stat, stat, mask, table, table]


def result_specs(block):
    row = pl.BlockSpec((WIDE, ROWS), lambda h: (block(h), 0))
    four = pl.BlockSpec((4, WIDE, ROWS), lambda h: (0, block(h), 0))
    return [row, four, four]


def attend_back_part(operands, first, count):
    four = jax.ShapeDtypeStruct((4, WIDE * count, ROWS), bf16)
    return pl.pallas_call(
        attend_back_step,
        grid=(count,),
        in_specs=back_specs(lambda h: h + first),
        out_specs=result_specs(lambda h: h),
        out_shape=[jax.ShapeDtypeStruct((WIDE * count, ROWS), bf16), four, four],
        compiler_params=vmem(60),
        cost_estimate=SHORT,
    )(*operands)


GB = 512


def attend_back_kernel(*refs):
    ins, first, second, (normed, wt, rows, vec_g, upb_g) = refs[0:9], refs[9:12], refs[12:15], refs[15:20]
    dq_ref, dk_ref, dv_ref, ga, gb = refs[20:25]
    g_s, b_s, v_s, o_s = refs[25:]
    step = pl.program_id(0)
    last = HEADS // BLOCK - 1
    outs = (dq_ref, dk_ref, dv_ref)

    @pl.when(step == 0)
    def _():
        for out, part in zip(outs, first):
            out[...] = part[...]

    @pl.when(jnp.logical_and(step > 0, step < last))
    def _():
        for out, part in zip(outs, second):
            out[...] = part[...]

    @pl.when(step == last)
    def _():
        attend_back_step(*ins, *outs)

    row = pl.multiple_of(step * WIDE, WIDE)
    g_s[pl.ds(row, WIDE), :] = dot(dq_ref[...], normed[0], NN)
    total = jnp.sum(dq_ref[...].astype(f32), axis=1, keepdims=True)
    b_s[pl.ds(row, WIDE), :] = jnp.broadcast_to(total, (WIDE, 8))
    for part, ref in ((1, dk_ref), (2, dv_ref)):
        g = b = None
        for p in range(4):
            t = dot(ref[p], normed[p], NN)
            u = ref[p].astype(f32)
            g = t if g is None else g + t
            b = u if b is None else b + u
        g_s[pl.ds(D * part + row, WIDE), :] = g
        total = jnp.sum(b, axis=1, keepdims=True)
        b_s[pl.ds(D * part + row, WIDE), :] = jnp.broadcast_to(total, (WIDE, 8))

    @pl.when(step == last)
    def _():
        pos = lax.axis_index("seq")
        w = wt[...].astype(f32)
        both = jnp.sum(w * g_s[...], axis=0, keepdims=True)
        shift_g = jnp.sum(w * b_s[:, 0:1], axis=0, keepdims=True)
        gain_g = (both - rows[3:4, :] * shift_g) / rows[2:3, :]
        v_s[...] = jnp.concatenate([vec_g[0:1, :], gain_g, shift_g, vec_g[3:8, :]], axis=0).T
        o_s[...] = jnp.zeros_like(o_s)
        for p in range(4):
            out = (ga, gb)[p % 2]
            own = pos ^ p
            out[p // 2, 0:QW, :] = g_s[pl.ds(QW * own, QW), :].astype(bf16)
            o_s[0:8, 0:OW] = v_s[pl.ds(OW * own, OW), :].T
            o_s[8:16, 0:QW] = b_s[pl.ds(QW * own, QW), :].T
            o_s[16:24, :] = jnp.broadcast_to(upb_g[p : p + 1, :], (8, D))
            out[p // 2, QW:GB, :] = o_s[...].astype(bf16)


def attend_back(operands, first, second, normed, wt, rows, vec_g, upb_g):
    steps = HEADS // BLOCK

    def whole(*shape):
        return pl.BlockSpec(shape, lambda h: (0,) * len(shape))

    four = jax.ShapeDtypeStruct((4, D, ROWS), bf16)
    block = jax.ShapeDtypeStruct((2, GB, D), bf16)
    return pl.pallas_call(
        attend_back_kernel,
        grid=(steps,),
        in_specs=back_specs(lambda h: steps - 1)
        + result_specs(lambda h: 0)
        + result_specs(lambda h: jnp.clip(h - 1, 0, steps - 3))
        + [whole(4, ROWS, D), whole(3 * D, D), whole(8, D), whole(8, D), whole(4, D)],
        out_specs=result_specs(lambda h: h) + [whole(2, GB, D), whole(2, GB, D)],
        out_shape=[jax.ShapeDtypeStruct((D, ROWS), bf16), four, four, block, block],
        scratch_shapes=[
            pltpu.VMEM((3 * D, D), f32), pltpu.VMEM((3 * D, 8), f32), pltpu.VMEM((D, 8), f32), pltpu.VMEM((32, D), f32),
        ],
        compiler_params=vmem(60),
        cost_estimate=SHORT,
    )(*operands, *first, *second, normed, wt, rows, vec_g, upb_g)


def rows_back_kernel(dq, dk, dv, wt, dn0, dnx, dnb):
    for p, out in ((1, dnb.at[0]), (3, dnb.at[1]), (2, dnx), (0, dn0)):
        d_n = dot(dk[p], wt[D : 2 * D, :], TN) + dot(dv[p], wt[2 * D : 3 * D, :], TN)
        if p == 0:
            d_n = d_n + dot(dq[...], wt[0:D, :], TN)
        out[...] = d_n.astype(bf16)


def rows_back(dq, dk, dv, wt):
    rows = jax.ShapeDtypeStruct((ROWS, D), bf16)
    return pl.pallas_call(
        rows_back_kernel,
        in_specs=[VMEM] * 4,
        out_specs=[VMEM] * 3,
        out_shape=[rows, rows, jax.ShapeDtypeStruct((2, ROWS, D), bf16)],
        compiler_params=vmem(60),
        cost_estimate=SHORT,
    )(dq, dk, dv, wt)


def finish_kernel(quarters, tok, rows, own, core, across, d_mid, out):
    start = first_row(quarters)
    xhat, rstd = normalize(rolled(tok, start))
    d_n = own[...].astype(f32) + core[0].astype(f32) + across[...].astype(f32)
    e = d_n * rows[2:3, :]
    grad = d_mid[...] + rstd * (
        e - jnp.mean(e, axis=-1, keepdims=True) - xhat * jnp.mean(e * xhat, axis=-1, keepdims=True)
    )
    out[...] = pltpu.roll(grad, start, 0)


def finish(quarters, tok, rows, own, core, across, d_mid):
    return pl.pallas_call(
        finish_kernel,
        in_specs=[SMEM] + [VMEM] * 6,
        out_specs=VMEM,
        out_shape=jax.ShapeDtypeStruct((ROWS, D), f32),
        compiler_params=vmem(16),
        cost_estimate=SHORT,
    )(quarters, tok, rows, own, core, across, d_mid)


def place(parts, total):
    group = lax.axis_index("dp")
    y, z = group & 1, (group >> 1) & 1
    for (my, mz), part in parts:
        n = part.shape[0]
        row = ((y ^ my) * 2 + (z ^ mz)) * n
        total[pl.ds(pl.multiple_of(row, 8), n), :] = part.astype(f32)


def place_a_kernel(*refs):
    down, up, out, total = refs[4:]
    place([((m & 1, m >> 1), ref[...]) for m, ref in enumerate(refs[:4])], total)
    down[...] = total[0:D, :]
    up[...] = total[D : 2 * D, :]
    out[...] = total[2 * D : 2 * D + OW, :]


def place_b_kernel(*refs):
    qkv, bias, upb, total = refs[4], refs[5], refs[6], refs[13]
    place([((m & 1, m >> 1), ref[...]) for m, ref in enumerate(refs[:4])], total)
    qkv[...] = total[0:QW, :]
    bias[...] = total[QW + 8, 0:QW]
    upb[...] = total[QW + 16, :]
    for i in range(6):
        refs[7 + i][...] = total[QW + i, 0:OW]


def place_call(kernel, parts, shapes, rows):
    return pl.pallas_call(
        kernel,
        in_specs=[VMEM] * len(parts),
        out_specs=[VMEM] * len(shapes),
        out_shape=[jax.ShapeDtypeStruct(s, f32) for s in shapes],
        scratch_shapes=[pltpu.VMEM((rows, D), f32)],
        compiler_params=vmem(24),
        cost_estimate=SHORT,
    )(*parts)


def tie(terms, *others):
    return lax.optimization_barrier((tuple(terms),) + others)[0]


def after(x, *others):
    return lax.optimization_barrier((x,) + others)[0]


def local(
    tokens, cotangent, quarters, qkv_weight, qkv_bias, out_weight, out_bias, attn_gain, attn_shift,
    ffn_gain, ffn_shift, up_weight, up_bias, down_weight, down_bias, *, n_dp,
):
    group = lax.axis_index("dp")

    def swap(x, seq_mask, dp_mask=0):
        pairs = []
        for s in range(4):
            for d in range(n_dp):
                pairs.append((s * n_dp + d, (s ^ seq_mask) * n_dp + (d ^ dp_mask)))
        return lax.ppermute(x, ("seq", "dp"), pairs)

    tok, cot = tokens[0], cotangent[0]
    vectors = (qkv_bias, out_bias, attn_gain, attn_shift, ffn_gain, ffn_shift, down_bias, up_bias)
    own, part = pack(qkv_weight.T, tok, vectors)
    far0 = swap(part, 2)
    near = swap(own, 1)
    tok_far = swap(after(tok, far0), 2)
    far1 = swap(far0, 0, 1)
    cos, sin, mask = tables(after(quarters, far0))
    far2 = swap(jnp.concatenate([after(far0, mask), far1]), 0, 2)
    last = [swap(x, 1) for x in (far0, far1, far2)]
    tok_last = swap(tok_far, 1)
    q, k, v, normed, wt, rows, upb = project(
        quarters, (own, near, tok_far, tok_last, far0, far1, far2, *last), cos, sin
    )
    half = lax.dynamic_slice_in_dim(down_weight, (group & 1) * HD, HD)
    wo, half = tie((out_weight.T, half), tok_far)
    wo_far, wo_near = swap(wo, 2), swap(wo, 1)
    dn_far, dn_near = swap(half, 2), swap(down_weight, 1)
    wo_far, dn_far = tie((wo_far, dn_far), q)
    wo_last, dn_last = swap(wo_far, 1), swap(dn_far, 1)
    dn_far2 = swap(dn_far, 0, 1)
    up_far, up_near = swap(after(up_weight, wo_far), 2), swap(up_weight, 1)
    ctx, log_total = attend(after(q, wo_far, dn_far), k, v, mask)
    up_far, dn_far2 = tie((up_far, dn_far2), log_total)
    up_last, dn_last2 = swap(up_far, 1), swap(dn_far2, 1)
    out, d_mid, d_ctx, delta, vec_g, upb_g, ga, gb = middle(
        quarters, ctx, tok, cot, (out_weight.T, wo_near, wo_far, wo_last), rows, upb,
        (up_weight, up_near, up_far, up_last),
        (down_weight, dn_near, dn_far, dn_last, dn_far2, dn_last2),
    )

    bits = n_dp.bit_length() - 1
    y, z = group & 1, (group >> 1) & 1

    def total(terms):
        s = terms[0].astype(f32)
        for t in terms[1:]:
            s = s + t.astype(f32)
        return s.astype(bf16)

    def cube_parts(a, b):
        n = a.shape[1] // 4

        def part(m):
            quarter = (y ^ ((m >> 1) & 1)) * 2 + (z ^ (m >> 2))
            return total([lax.dynamic_slice(t, (m & 1, quarter * n, 0), (1, n, D))[0] for t in (a, b)])

        return tuple(part(m) for m in range(8))

    def crossing(parts, which):
        return tuple(swap(part, 2 * (m & 1), m >> 1) for part, m in zip(parts, which))

    def square_parts(a, b):
        h = a.shape[1] // 2

        def part(m):
            first = (y ^ (m >> 1)) * h
            return total([lax.dynamic_slice(t, (m & 1, first, 0), (1, h, D))[0] for t in (a, b)])

        return tuple(part(m) for m in range(4))

    def half_parts(terms):
        n = terms[0].shape[0] // 2
        return tuple(total([lax.dynamic_slice(t, ((z ^ m) * n, 0), (n, D)) for t in terms]) for m in (0, 1))

    def rest(s):
        for b in range(3, bits):
            s = total([s, swap(s, 0, 1 << b)])
        return s

    args = (k, v, d_ctx, log_total, delta, mask, cos, sin)
    gb_in = swap(gb, 1)
    first = attend_back_part((q,) + args, 0, 1)
    partsa = cube_parts(*tie((ga, gb_in), first[0]))
    one = crossing([partsa[m] for m in (1, 2, 4, 7)], (1, 2, 4, 7))
    second = attend_back_part((after(q, *partsa),) + args, 1, 2)
    one = tie(one, second[0])
    later = tie([partsa[m] for m in (3, 5, 6)], *one)
    two = crossing(later, (3, 5, 6))
    dq, dk, dv, ha, hb = attend_back(
        (after(q, *later),) + args, first, second, normed, wt, rows, vec_g, upb_g
    )
    parta = total((partsa[0],) + one + tie(two, dq))
    parta_in = swap(parta, 0, 4)
    hb_in = swap(after(hb, parta), 1)
    partsb = square_parts(ha, hb_in)
    squareb = partsb[0:1] + crossing(partsb[1:], (1, 2, 3))
    dn0, dnx, dnb = rows_back(after(dq, *partsb), dk, dv, wt)
    keepb, sendb = half_parts(tie(squareb, dn0))
    sendb_in = swap(sendb, 0, 2)
    suma = rest(total([parta, after(parta_in, sendb)]))
    alla = (suma,) + tuple(swap(suma, 0, m) for m in (1, 2, 3))
    core = swap(after(dnb, suma), 1)
    d_sum = total([dnx, core[1]])
    across = swap(d_sum, 2)
    partb = total([keepb, after(sendb_in, d_sum)])
    partb_in = swap(partb, 0, 4)
    sumb = rest(total([partb, partb_in]))
    alla = tie(alla, sumb)
    sumb = after(sumb, *alla)
    allb = (sumb,) + tuple(swap(sumb, 0, m) for m in (1, 2, 3))
    g_down, g_up, g_out = place_call(place_a_kernel, alla, ((D, D), (D, D), (OW, D)), GA)
    grad_tok = finish(quarters, tok, rows, after(dn0, g_down), core, across, d_mid)
    g_qkv, g_bias, g_upb, *six = place_call(
        place_b_kernel, tie(allb, grad_tok), ((QW, D), (QW,), (D,)) + ((OW,),) * 6, GB
    )

    return (
        out[None], grad_tok[None], g_qkv.T, g_bias, g_out.T, six[0], six[1], six[2], six[3], six[4],
        g_up, g_upb, g_down, six[5],
    )


def solution(mesh):
    rows, vector = P("dp", "seq", None), P("seq")
    columns = P(None, "seq")
    return jax.shard_map(
        functools.partial(local, n_dp=mesh.shape["dp"]),
        mesh=mesh,
        in_specs=(rows, rows, P("dp", None), columns, vector, columns, vector, vector, vector, vector, vector,
                  columns, vector, P("seq", None), vector),
        out_specs=(rows, rows, columns, vector, columns, vector, vector, vector, vector, vector,
                   columns, vector, P("seq", None), vector),
        check_vma=False,
    )
```

```python
import functools
import math

import jax
import jax.numpy as jnp
import numpy as np
from jax import lax
from jax.experimental import pallas as pl
from jax.experimental.pallas import tpu as pltpu
from jax.sharding import PartitionSpec as P

HEADS = 20
HEAD_DIM = 32
HALF = 16
D = 640
FF = 2560
ROWS = 512
SEG = 256
QW = 480
OW = 160
EPS = 1e-05
SCALE = 1.0 / math.sqrt(HEAD_DIM)
SCALE2 = SCALE * math.log2(math.e)

bf16 = jnp.bfloat16
f32 = jnp.float32

NN = (((1,), (0,)), ((), ()))
NT = (((1,), (1,)), ((), ()))
TN = (((0,), (0,)), ((), ()))
TT = (((0,), (1,)), ((), ()))

VMEM = pl.BlockSpec(memory_space=pltpu.VMEM)
SMEM = pl.BlockSpec(memory_space=pltpu.SMEM)
ANY = pl.BlockSpec(memory_space=pl.ANY)
SHORT = pl.CostEstimate(flops=10**6, bytes_accessed=10**5, transcendentals=0)


def vmem(mebibytes):
    return pltpu.CompilerParams(vmem_limit_bytes=mebibytes * 2**20)


def dot(a, b, dims):
    return lax.dot_general(a, b, dims, preferred_element_type=f32)


def normalize(x):
    center = x - jnp.mean(x, axis=-1, keepdims=True)
    spread = jnp.mean(center * center, axis=-1, keepdims=True)
    rstd = lax.rsqrt(spread + EPS)
    return center * rstd, rstd


def first_row(quarters):
    start = jnp.int32(0)
    before = jnp.int32(0)
    for c in range(4):
        size = quarters[0, c]
        start = jnp.where(size == SEG, before, start)
        before = before + size
    return start


def rolled(ref, start):
    return pltpu.roll(ref[...].astype(f32), ROWS - start, 0)


def tables_kernel(quarters, freqs, cos, sin, mask):
    pos = lax.axis_index("seq")
    start = first_row(quarters)

    def crops(shape, dim, first):
        row = (lax.broadcasted_iota(jnp.int32, shape, dim) + (first + start)) % ROWS
        end = jnp.int32(0)
        crop = jnp.zeros(shape, jnp.int32)
        offset, length = crop, crop
        for c in range(4):
            size = quarters[0, c]
            begin, end = end, end + size
            crop = crop + (row >= end).astype(jnp.int32)
            inside = jnp.logical_and(row >= begin, row < end)
            offset = jnp.where(inside, begin, offset)
            length = jnp.where(inside, size, length)
        return crop, row - offset, length

    _, place, length = crops((HALF, ROWS), 1, 0)
    for p in range(4):
        angles = ((pos ^ p) * length + place).astype(f32) * freqs[...][:, 0:1]
        cos[p] = jnp.cos(angles)
        sin[p] = jnp.sin(angles)
    down = crops((SEG, SEG), 0, SEG)[0]
    along = crops((SEG, SEG), 1, SEG)[0]
    mask[...] = jnp.where(down == along, 0.0, -1e30)


def tables(quarters):
    freqs = np.float32(10000.0) ** (-np.arange(0, HEAD_DIM, 2).astype(np.float32) / np.float32(HEAD_DIM))
    table = jax.ShapeDtypeStruct((4, HALF, ROWS), f32)
    return pl.pallas_call(
        tables_kernel,
        in_specs=[SMEM, VMEM],
        out_specs=[VMEM] * 3,
        out_shape=[table, table, jax.ShapeDtypeStruct((SEG, SEG), f32)],
        compiler_params=vmem(60),
    )(quarters, jnp.asarray(np.repeat(freqs[:, None], 128, axis=1)))


def project_rows(p, x, wt, column, gain, shift, cos, sin, q_out, k_out, v_out, n_out):
    xhat, _ = normalize(x)
    normed = (xhat * gain + shift).astype(bf16)
    n_out[p] = normed
    for part in range(0 if q_out is not None else 1, 3):
        rows = slice(D * part, D * part + D)
        y = dot(wt[rows, :], normed, NT) + column[rows]
        if part == 2:
            v_out[p] = y.astype(bf16)
            continue
        c, s = cos[p], sin[p]
        for h in range(HEADS):
            a = y[32 * h : 32 * h + 16]
            b = y[32 * h + 16 : 32 * h + 32]
            r = jnp.concatenate([a * c - b * s, b * c + a * s], axis=0).astype(bf16)
            if part == 0:
                q_out[32 * h : 32 * h + 32, :] = r
            else:
                k_out[p, 32 * h : 32 * h + 32, :] = r


WPART = 512
PART = WPART // 4
PACK = WPART + ROWS


def pack_kernel(*refs):
    w, tok, out, part = refs[0], refs[1], refs[10], refs[11]
    out[0:QW, :] = w[...]
    out[WPART:PACK, :] = tok[...]
    rows = []
    for v in refs[2:10]:
        n = v.shape[0]
        row = v[...].astype(f32).reshape(1, n)
        rows.append(row if n == D else jnp.concatenate([row, jnp.zeros((1, D - n), f32)], axis=1))
    rows.append(jnp.zeros((WPART - QW - 8, D), f32))
    out[QW:WPART, :] = jnp.concatenate(rows, axis=0).astype(bf16)
    which = lax.axis_index("dp") & 3
    part[...] = out[pl.ds(pl.multiple_of(which * PART, PART), PART), :]


def pack(w, tok, vectors):
    return pl.pallas_call(
        pack_kernel,
        in_specs=[VMEM] * 10,
        out_specs=[VMEM] * 2,
        out_shape=[jax.ShapeDtypeStruct((PACK, D), bf16), jax.ShapeDtypeStruct((PART, D), bf16)],
        compiler_params=vmem(60),
        cost_estimate=SHORT,
    )(w, tok, *vectors)


def project_kernel(
    quarters, own, near, tok_far, tok_last, far0, far1, far2, last0, last1, last2, cos, sin,
    q_to, k_to, v_to, n_to, wt_to, rows_out, upb_out,
    q_out, k_out, v_out, n_out, wt, vt, col, w_far, w_last, sems,
):
    pos = lax.axis_index("seq")
    which = lax.axis_index("dp") & 3
    start = first_row(quarters)
    for whole, p0, p1, p2 in ((w_far, far0, far1, far2), (w_last, last0, last1, last2)):
        pieces = (p0[...], p1[...], p2[0:PART, :], p2[PART : 2 * PART, :])
        for i, piece in enumerate(pieces):
            whole[pl.ds(pl.multiple_of((which ^ i) * PART, PART), PART), :] = piece
    for p, m in enumerate((own, near, w_far, w_last)):
        wt[pl.ds(QW * (pos ^ p), QW), :] = m[0:QW, :]
        v = m[QW : QW + 16, :].astype(f32)[0:8]
        t = v.T
        col[pl.ds(QW * (pos ^ p), QW), :] = t[0:QW]
        vt[pl.ds(OW * (pos ^ p), OW), :] = t[0:OW]
        upb_out[p : p + 1, :] = v[7:8, :]
    sends = []

    def send(source, to):
        copy = pltpu.make_async_copy(source, to, sems.at[len(sends)])
        copy.start()
        sends.append(copy)

    send(wt, wt_to)
    rows = vt[...].T
    rows_out[...] = rows
    column = col[:, 0:1]
    gain, shift = rows[2:3], rows[3:4]
    toks = (own.at[pl.ds(WPART, ROWS), :], near.at[pl.ds(WPART, ROWS), :], tok_far, tok_last)
    for p, tok in enumerate(toks):
        project_rows(
            p, rolled(tok, start), wt, column, gain, shift, cos, sin,
            q_out if p == 0 else None, k_out, v_out, n_out,
        )
        if p == 0:
            send(q_out, q_to)
        for source, to in ((k_out, k_to), (v_out, v_to), (n_out, n_to)):
            send(source.at[p], to.at[p])
    for copy in sends:
        copy.wait()


def project(quarters, parts, cos, sin):
    sds = jax.ShapeDtypeStruct
    kv = sds((4, D, ROWS), bf16)
    return pl.pallas_call(
        project_kernel,
        in_specs=[SMEM] + [VMEM] * 12,
        out_specs=[ANY] * 5 + [VMEM] * 2,
        out_shape=[
            sds((D, ROWS), bf16), kv, kv, sds((4, ROWS, D), bf16), sds((3 * D, D), bf16),
            sds((8, D), f32), sds((4, D), f32),
        ],
        scratch_shapes=[
            pltpu.VMEM((D, ROWS), bf16), pltpu.VMEM((4, D, ROWS), bf16), pltpu.VMEM((4, D, ROWS), bf16),
            pltpu.VMEM((4, ROWS, D), bf16), pltpu.VMEM((3 * D, D), bf16),
            pltpu.VMEM((D, 8), f32), pltpu.VMEM((3 * D, 8), f32),
            pltpu.VMEM((WPART, D), bf16), pltpu.VMEM((WPART, D), bf16), pltpu.SemaphoreType.DMA((14,)),
        ],
        compiler_params=vmem(60),
        cost_estimate=SHORT,
    )(quarters, *parts, cos, sin)


def attend_kernel(q_ref, k_ref, v_ref, mask_ref, o_ref, l_ref, *, heads):
    ones = jnp.ones((HALF, SEG), bf16)
    for h in range(heads):
        hs = slice(32 * h, 32 * h + 32)
        for seg in range(2):
            cs = slice(SEG * seg, SEG * seg + SEG)
            q = q_ref[hs, cs].T
            scores = []
            for p in range(4):
                s = dot(q, k_ref[p, hs, cs], NN)
                if seg == 1:
                    s = s + mask_ref[...]
                scores.append(s)
            top = scores[0]
            for s in scores[1:]:
                top = jnp.maximum(top, s)
            top = top.max(1, keepdims=True)
            acc = None
            for p in range(4):
                e = jnp.exp2((scores[p] - top) * SCALE2).astype(bf16)
                t = dot(e, jnp.concatenate([v_ref[p, hs, cs], ones], axis=0), NT)
                acc = t if acc is None else acc + t
            total = acc[:, HEAD_DIM : HEAD_DIM + 1]
            o_ref[hs, cs] = (acc[:, 0:HEAD_DIM] / total).T
            log_total = top * SCALE2 + jnp.log2(total)
            l_ref[h, :, cs] = jnp.broadcast_to(log_total, (SEG, 128)).T[0:1]


def attend(q, k, v, mask):
    heads = 5
    row = pl.BlockSpec((32 * heads, ROWS), lambda h: (h, 0))
    four = pl.BlockSpec((4, 32 * heads, ROWS), lambda h: (0, h, 0))
    return pl.pallas_call(
        functools.partial(attend_kernel, heads=heads),
        grid=(HEADS // heads,),
        in_specs=[row, four, four, pl.BlockSpec((SEG, SEG), lambda h: (0, 0))],
        out_specs=[row, pl.BlockSpec((heads, 1, ROWS), lambda h: (h, 0, 0))],
        out_shape=[
            jax.ShapeDtypeStruct((D, ROWS), f32),
            jax.ShapeDtypeStruct((HEADS, 1, ROWS), f32),
        ],
        compiler_params=vmem(60),
        cost_estimate=SHORT,
    )(q, k, v, mask)


GA = 1472
HD = 320


def middle_kernel(
    quarters, ctx_ref, tok, cot, wo0, wo1, wo2, wo3, vec, upb,
    up0, up1, up2, up3, dn0, dn1, dn2, dn3, dq2, dq3,
    dmid_ref, dctx_ref, delta_ref, vecg_ref, upbg_ref, act_to, mid_to, ga, gb,
    up_s, dn_s, wo_s, mid_s, n2_s, n2t_s, cot_s, act_s, dn2_s, g_s, go_s, goo_s, sems, out_sems,
):
    pos = lax.axis_index("seq")
    start = first_row(quarters)
    copies = []
    half = lax.axis_index("dp") & 1
    for p, (u, d) in enumerate(((up0, dn0), (up1, dn1), (up2, dn2), (up3, dn3))):
        copies.append(pltpu.make_async_copy(u, up_s.at[p], sems.at[3 * p]))
        if p < 2:
            copies.append(pltpu.make_async_copy(d, dn_s.at[p], sems.at[3 * p + 1]))
            continue
        for i, h in enumerate((d, (dq2, dq3)[p - 2])):
            to = dn_s.at[p, pl.ds(pl.multiple_of(HD * (half ^ i), HD), HD), :]
            copies.append(pltpu.make_async_copy(h, to, sems.at[3 * p + 1 + i]))
    for c in copies:
        c.start()
    for p, wo in enumerate((wo0, wo1, wo2, wo3)):
        wo_s[pl.ds(OW * (pos ^ p), OW), :] = wo[...]
    ctx_low = ctx_ref[...].astype(bf16)
    out_bias, gain, shift = (vec[i : i + 1, :] for i in (1, 4, 5))
    mid = rolled(tok, start) + dot(wo_s[...], ctx_low, NN).T + out_bias
    mid_s[...] = mid
    kept = [pltpu.make_async_copy(mid_s, mid_to, out_sems.at[8])]
    kept[0].start()
    xhat, rstd = normalize(mid)
    normed2 = (xhat * gain + shift).astype(bf16)
    n2_s[...] = normed2
    n2t_s[...] = normed2.T
    cot_s[...] = rolled(cot, start).astype(bf16)
    dn2_s[...] = jnp.zeros_like(dn2_s)
    for c in copies:
        c.wait()

    sends = []

    def send(p, source, first, count, slot):
        to = (ga, gb)[p % 2].at[p // 2, pl.ds(first, count), :]
        copy = pltpu.make_async_copy(source, to, out_sems.at[slot])
        copy.start()
        sends.append(copy)

    def piece(p, carry):
        pre = dot(n2_s[...], up_s[p], NN) + upb[pl.ds(p, 1), :]
        d_act = dot(cot_s[...], dn_s[p], NT)
        cdf = 0.5 + 0.5 * lax.erf(pre * (1.0 / math.sqrt(2.0)))
        pdf = jnp.exp(-0.5 * pre * pre) * (1.0 / math.sqrt(2.0 * math.pi))
        act = (pre * cdf).astype(bf16)
        d_pre = (d_act * (cdf + pre * pdf)).astype(bf16)
        act_s[p] = act
        dn2_s[...] += dot(d_pre, up_s[p], NT)
        g_s[p, 0:D, :] = dot(act, cot_s[...], TN).astype(bf16)
        g_s[p, D : 2 * D, :] = dot(n2t_s[...], d_pre, NN).astype(bf16)
        upbg_ref[pl.ds(p, 1), :] = jnp.sum(d_pre.astype(f32), axis=0, keepdims=True)
        return carry

    lax.fori_loop(0, 4, piece, 0)
    for p in range(4):
        send(p, g_s.at[p], 0, 2 * D, p)

    kept.append(pltpu.make_async_copy(act_s, act_to, out_sems.at[9]))
    kept[1].start()
    xhat, rstd = normalize(mid_s[...])
    d_n2 = dn2_s[...]
    e = d_n2 * gain
    d_cot = cot_s[...].astype(f32)
    d_mid = d_cot + rstd * (
        e - jnp.mean(e, axis=-1, keepdims=True) - xhat * jnp.mean(e * xhat, axis=-1, keepdims=True)
    )
    dmid_ref[...] = d_mid
    d_attn = d_mid.astype(bf16)
    vecg_ref[0:1, :] = jnp.sum(d_attn.astype(f32), axis=0, keepdims=True)
    vecg_ref[1:3, :] = jnp.zeros((2, D), f32)
    vecg_ref[3:4, :] = jnp.sum(d_n2 * xhat, axis=0, keepdims=True)
    vecg_ref[4:5, :] = jnp.sum(d_n2, axis=0, keepdims=True)
    vecg_ref[5:6, :] = jnp.sum(d_cot, axis=0, keepdims=True)
    vecg_ref[6:8, :] = jnp.zeros((2, D), f32)
    d_attn_t = d_attn.T
    go_s[...] = dot(d_attn_t, ctx_ref[...].astype(bf16), NT).astype(bf16)
    for p in range(4):
        goo_s[p, 0:OW, :] = go_s[pl.ds(OW * (pos ^ p), OW), :]
        goo_s[p, OW:, :] = jnp.zeros((GA - 2 * D - OW, D), bf16)
        send(p, goo_s.at[p], 2 * D, GA - 2 * D, 4 + p)
    d_ctx = dot(wo_s[...], d_attn_t, TN).astype(bf16)
    dctx_ref[...] = d_ctx
    product = d_ctx.astype(f32) * ctx_ref[...]
    for h in range(HEADS):
        delta_ref[h] = jnp.sum(product[32 * h : 32 * h + 32], axis=0, keepdims=True)
    for copy in sends + kept:
        copy.wait()


def middle(quarters, ctx, tok, cot, wos, vec, upb, ups, downs):
    sds = jax.ShapeDtypeStruct
    big = sds((2, GA, D), bf16)
    return pl.pallas_call(
        middle_kernel,
        in_specs=[SMEM] + [VMEM] * 9 + [ANY] * 10,
        out_specs=[VMEM] * 5 + [ANY] * 4,
        out_shape=[
            sds((ROWS, D), f32), sds((D, ROWS), bf16), sds((HEADS, 1, ROWS), f32),
            sds((8, D), f32), sds((4, D), f32), sds((4, ROWS, D), bf16), sds((ROWS, D), f32), big, big,
        ],
        scratch_shapes=[
            pltpu.VMEM((4, D, D), bf16), pltpu.VMEM((4, D, D), bf16), pltpu.VMEM((D, D), bf16),
            pltpu.VMEM((ROWS, D), f32), pltpu.VMEM((ROWS, D), bf16), pltpu.VMEM((D, ROWS), bf16),
            pltpu.VMEM((ROWS, D), bf16), pltpu.VMEM((4, ROWS, D), bf16), pltpu.VMEM((ROWS, D), f32),
            pltpu.VMEM((4, 2 * D, D), bf16), pltpu.VMEM((D, D), bf16),
            pltpu.VMEM((4, GA - 2 * D, D), bf16),
            pltpu.SemaphoreType.DMA((12,)), pltpu.SemaphoreType.DMA((10,)),
        ],
        compiler_params=vmem(58),
        cost_estimate=SHORT,
    )(quarters, ctx, tok, cot, *wos, vec, upb, *ups, *downs)


def output_kernel(quarters, act, mid, vec, dn0, dn1, dn2, dn3, dq2, dq3, out, dn_s, sems):
    half = lax.axis_index("dp") & 1
    copies = []
    for p, d in enumerate((dn0, dn1)):
        copies.append(pltpu.make_async_copy(d, dn_s.at[p], sems.at[p]))
    for p, pair in ((2, (dn2, dq2)), (3, (dn3, dq3))):
        for i, h in enumerate(pair):
            to = dn_s.at[p, pl.ds(pl.multiple_of(HD * (half ^ i), HD), HD), :]
            copies.append(pltpu.make_async_copy(h, to, sems.at[2 * p - 2 + i]))
    for c in copies:
        c.start()
    for c in copies:
        c.wait()
    total = mid[...] + vec[6:7, :]
    for p in range(4):
        total = total + dot(act[p], dn_s[p], NN)
    out[...] = pltpu.roll(total, first_row(quarters), 0).astype(bf16)


def output(quarters, act, mid, vec, downs):
    return pl.pallas_call(
        output_kernel,
        in_specs=[SMEM] + [VMEM] * 3 + [ANY] * 6,
        out_specs=VMEM,
        out_shape=jax.ShapeDtypeStruct((ROWS, D), bf16),
        scratch_shapes=[pltpu.VMEM((4, D, D), bf16), pltpu.SemaphoreType.DMA((6,))],
        compiler_params=vmem(60),
        cost_estimate=SHORT,
    )(quarters, act, mid, vec, *downs)


BLOCK = 5
WIDE = 32 * BLOCK


def attend_back_step(q_ref, k_ref, v_ref, do_ref, l_ref, dl_ref, mask_ref, cos_ref, sin_ref, dq_ref, dk_ref, dv_ref):
    def back(g, c, s):
        a, b = g[0:HALF], g[HALF : 2 * HALF]
        return jnp.concatenate([a * c + b * s, b * c - a * s], axis=0).astype(bf16)

    for h in range(BLOCK):
        hs = slice(32 * h, 32 * h + 32)
        for seg in range(2):
            cs = slice(SEG * seg, SEG * seg + SEG)
            q, d_o = q_ref[hs, cs], do_ref[hs, cs]
            log_total, delta = l_ref[h, :, cs], dl_ref[h, :, cs]
            d_q = None
            for p in range(4):
                k = k_ref[p, hs, cs]
                v = v_ref[p, hs, cs]
                s = dot(k, q, TN)
                if seg == 1:
                    s = s + mask_ref[...]
                e = jnp.exp2(s * SCALE2 - log_total)
                d_s = (e * (dot(v, d_o, TN) - delta)).astype(bf16)
                dv_ref[p, hs, cs] = dot(d_o, e.astype(bf16), NT).astype(bf16)
                d_k = dot(q, d_s, NT) * SCALE
                dk_ref[p, hs, cs] = back(d_k, cos_ref[p, :, cs], sin_ref[p, :, cs])
                t = dot(k, d_s, NN)
                d_q = t if d_q is None else d_q + t
            dq_ref[hs, cs] = back(d_q * SCALE, cos_ref[0, :, cs], sin_ref[0, :, cs])


def back_specs(block):
    row = pl.BlockSpec((WIDE, ROWS), lambda h: (block(h), 0))
    four = pl.BlockSpec((4, WIDE, ROWS), lambda h: (0, block(h), 0))
    stat = pl.BlockSpec((BLOCK, 1, ROWS), lambda h: (block(h), 0, 0))
    table = pl.BlockSpec((4, HALF, ROWS), lambda h: (0, 0, 0))
    mask = pl.BlockSpec((SEG, SEG), lambda h: (0, 0))
    return [row, four, four, row, stat, stat, mask, table, table]


def result_specs(block):
    row = pl.BlockSpec((WIDE, ROWS), lambda h: (block(h), 0))
    four = pl.BlockSpec((4, WIDE, ROWS), lambda h: (0, block(h), 0))
    return [row, four, four]


def attend_back_part(operands, first, count):
    four = jax.ShapeDtypeStruct((4, WIDE * count, ROWS), bf16)
    return pl.pallas_call(
        attend_back_step,
        grid=(count,),
        in_specs=back_specs(lambda h: h + first),
        out_specs=result_specs(lambda h: h),
        out_shape=[jax.ShapeDtypeStruct((WIDE * count, ROWS), bf16), four, four],
        compiler_params=vmem(60),
        cost_estimate=SHORT,
    )(*operands)


GB = 512


def attend_back_kernel(*refs):
    ins, first, second, (normed, wt, rows, vec_g, upb_g) = refs[0:9], refs[9:12], refs[12:15], refs[15:20]
    dq_ref, dk_ref, dv_ref, ga, gb = refs[20:25]
    g_s, b_s, v_s, o_s = refs[25:]
    step = pl.program_id(0)
    last = HEADS // BLOCK - 1
    outs = (dq_ref, dk_ref, dv_ref)

    @pl.when(step == 0)
    def _():
        for out, part in zip(outs, first):
            out[...] = part[...]

    @pl.when(jnp.logical_and(step > 0, step < last))
    def _():
        for out, part in zip(outs, second):
            out[...] = part[...]

    @pl.when(step == last)
    def _():
        attend_back_step(*ins, *outs)

    row = pl.multiple_of(step * WIDE, WIDE)
    g_s[pl.ds(row, WIDE), :] = dot(dq_ref[...], normed[0], NN)
    total = jnp.sum(dq_ref[...].astype(f32), axis=1, keepdims=True)
    b_s[pl.ds(row, WIDE), :] = jnp.broadcast_to(total, (WIDE, 8))
    for part, ref in ((1, dk_ref), (2, dv_ref)):
        g = b = None
        for p in range(4):
            t = dot(ref[p], normed[p], NN)
            u = ref[p].astype(f32)
            g = t if g is None else g + t
            b = u if b is None else b + u
        g_s[pl.ds(D * part + row, WIDE), :] = g
        total = jnp.sum(b, axis=1, keepdims=True)
        b_s[pl.ds(D * part + row, WIDE), :] = jnp.broadcast_to(total, (WIDE, 8))

    @pl.when(step == last)
    def _():
        pos = lax.axis_index("seq")
        w = wt[...].astype(f32)
        both = jnp.sum(w * g_s[...], axis=0, keepdims=True)
        shift_g = jnp.sum(w * b_s[:, 0:1], axis=0, keepdims=True)
        gain_g = (both - rows[3:4, :] * shift_g) / rows[2:3, :]
        v_s[...] = jnp.concatenate([vec_g[0:1, :], gain_g, shift_g, vec_g[3:8, :]], axis=0).T
        o_s[...] = jnp.zeros_like(o_s)
        for p in range(4):
            out = (ga, gb)[p % 2]
            own = pos ^ p
            out[p // 2, 0:QW, :] = g_s[pl.ds(QW * own, QW), :].astype(bf16)
            o_s[0:8, 0:OW] = v_s[pl.ds(OW * own, OW), :].T
            o_s[8:16, 0:QW] = b_s[pl.ds(QW * own, QW), :].T
            o_s[16:24, :] = jnp.broadcast_to(upb_g[p : p + 1, :], (8, D))
            out[p // 2, QW:GB, :] = o_s[...].astype(bf16)


def attend_back(operands, first, second, normed, wt, rows, vec_g, upb_g):
    steps = HEADS // BLOCK

    def whole(*shape):
        return pl.BlockSpec(shape, lambda h: (0,) * len(shape))

    four = jax.ShapeDtypeStruct((4, D, ROWS), bf16)
    block = jax.ShapeDtypeStruct((2, GB, D), bf16)
    return pl.pallas_call(
        attend_back_kernel,
        grid=(steps,),
        in_specs=back_specs(lambda h: steps - 1)
        + result_specs(lambda h: 0)
        + result_specs(lambda h: jnp.clip(h - 1, 0, steps - 3))
        + [whole(4, ROWS, D), whole(3 * D, D), whole(8, D), whole(8, D), whole(4, D)],
        out_specs=result_specs(lambda h: h) + [whole(2, GB, D), whole(2, GB, D)],
        out_shape=[jax.ShapeDtypeStruct((D, ROWS), bf16), four, four, block, block],
        scratch_shapes=[
            pltpu.VMEM((3 * D, D), f32), pltpu.VMEM((3 * D, 8), f32), pltpu.VMEM((D, 8), f32), pltpu.VMEM((32, D), f32),
        ],
        compiler_params=vmem(60),
        cost_estimate=SHORT,
    )(*operands, *first, *second, normed, wt, rows, vec_g, upb_g)


def rows_back_kernel(dq, dk, dv, wt, dn0, dnx, dnb):
    for p, out in ((1, dnb.at[0]), (3, dnb.at[1]), (2, dnx), (0, dn0)):
        d_n = dot(dk[p], wt[D : 2 * D, :], TN) + dot(dv[p], wt[2 * D : 3 * D, :], TN)
        if p == 0:
            d_n = d_n + dot(dq[...], wt[0:D, :], TN)
        out[...] = d_n.astype(bf16)


def rows_back(dq, dk, dv, wt):
    rows = jax.ShapeDtypeStruct((ROWS, D), bf16)
    return pl.pallas_call(
        rows_back_kernel,
        in_specs=[VMEM] * 4,
        out_specs=[VMEM] * 3,
        out_shape=[rows, rows, jax.ShapeDtypeStruct((2, ROWS, D), bf16)],
        compiler_params=vmem(60),
        cost_estimate=SHORT,
    )(dq, dk, dv, wt)


def finish_kernel(quarters, tok, rows, own, core, across, d_mid, out):
    start = first_row(quarters)
    xhat, rstd = normalize(rolled(tok, start))
    d_n = own[...].astype(f32) + core[0].astype(f32) + across[...].astype(f32)
    e = d_n * rows[2:3, :]
    grad = d_mid[...] + rstd * (
        e - jnp.mean(e, axis=-1, keepdims=True) - xhat * jnp.mean(e * xhat, axis=-1, keepdims=True)
    )
    out[...] = pltpu.roll(grad, start, 0)


def finish(quarters, tok, rows, own, core, across, d_mid):
    return pl.pallas_call(
        finish_kernel,
        in_specs=[SMEM] + [VMEM] * 6,
        out_specs=VMEM,
        out_shape=jax.ShapeDtypeStruct((ROWS, D), f32),
        compiler_params=vmem(16),
        cost_estimate=SHORT,
    )(quarters, tok, rows, own, core, across, d_mid)


def place(parts, total):
    group = lax.axis_index("dp")
    y, z = group & 1, (group >> 1) & 1
    for (my, mz), part in parts:
        n = part.shape[0]
        row = ((y ^ my) * 2 + (z ^ mz)) * n
        total[pl.ds(pl.multiple_of(row, 8), n), :] = part.astype(f32)


def place_a_kernel(*refs):
    down, up, out, total = refs[4:]
    place([((m & 1, m >> 1), ref[...]) for m, ref in enumerate(refs[:4])], total)
    down[...] = total[0:D, :]
    up[...] = total[D : 2 * D, :]
    out[...] = total[2 * D : 2 * D + OW, :]


def place_b_kernel(*refs):
    qkv, bias, upb, total = refs[4], refs[5], refs[6], refs[13]
    place([((m & 1, m >> 1), ref[...]) for m, ref in enumerate(refs[:4])], total)
    qkv[...] = total[0:QW, :]
    bias[...] = total[QW + 8, 0:QW]
    upb[...] = total[QW + 16, :]
    for i in range(6):
        refs[7 + i][...] = total[QW + i, 0:OW]


def place_call(kernel, parts, shapes, rows):
    return pl.pallas_call(
        kernel,
        in_specs=[VMEM] * len(parts),
        out_specs=[VMEM] * len(shapes),
        out_shape=[jax.ShapeDtypeStruct(s, f32) for s in shapes],
        scratch_shapes=[pltpu.VMEM((rows, D), f32)],
        compiler_params=vmem(24),
        cost_estimate=SHORT,
    )(*parts)


def tie(terms, *others):
    return lax.optimization_barrier((tuple(terms),) + others)[0]


def after(x, *others):
    return lax.optimization_barrier((x,) + others)[0]


def local(
    tokens, cotangent, quarters, qkv_weight, qkv_bias, out_weight, out_bias, attn_gain, attn_shift,
    ffn_gain, ffn_shift, up_weight, up_bias, down_weight, down_bias, *, n_dp,
):
    group = lax.axis_index("dp")

    def swap(x, seq_mask, dp_mask=0):
        pairs = []
        for s in range(4):
            for d in range(n_dp):
                pairs.append((s * n_dp + d, (s ^ seq_mask) * n_dp + (d ^ dp_mask)))
        return lax.ppermute(x, ("seq", "dp"), pairs)

    tok, cot = tokens[0], cotangent[0]
    vectors = (qkv_bias, out_bias, attn_gain, attn_shift, ffn_gain, ffn_shift, down_bias, up_bias)
    own, part = pack(qkv_weight.T, tok, vectors)
    far0 = swap(part, 2)
    near = swap(own, 1)
    tok_far = swap(after(tok, far0), 2)
    far1 = swap(far0, 0, 1)
    cos, sin, mask = tables(after(quarters, far0))
    far2 = swap(jnp.concatenate([after(far0, mask), far1]), 0, 2)
    last = [swap(x, 1) for x in (far0, far1, far2)]
    tok_last = swap(tok_far, 1)
    q, k, v, normed, wt, rows, upb = project(
        quarters, (own, near, tok_far, tok_last, far0, far1, far2, *last), cos, sin
    )
    half = lax.dynamic_slice_in_dim(down_weight, (group & 1) * HD, HD)
    wo, half = tie((out_weight.T, half), tok_far)
    wo_far, wo_near = swap(wo, 2), swap(wo, 1)
    dn_far, dn_near = swap(half, 2), swap(down_weight, 1)
    wo_far, dn_far = tie((wo_far, dn_far), q)
    wo_last, dn_last = swap(wo_far, 1), swap(dn_far, 1)
    dn_far2 = swap(dn_far, 0, 1)
    up_far, up_near = swap(after(up_weight, wo_far), 2), swap(up_weight, 1)
    ctx, log_total = attend(after(q, wo_far, dn_far), k, v, mask)
    up_far, dn_far2 = tie((up_far, dn_far2), log_total)
    up_last, dn_last2 = swap(up_far, 1), swap(dn_far2, 1)
    downs = (down_weight, dn_near, dn_far, dn_last, dn_far2, dn_last2)
    d_mid, d_ctx, delta, vec_g, upb_g, act, mid, ga, gb = middle(
        quarters, ctx, tok, cot, (out_weight.T, wo_near, wo_far, wo_last), rows, upb,
        (up_weight, up_near, up_far, up_last), downs,
    )

    bits = n_dp.bit_length() - 1
    y, z = group & 1, (group >> 1) & 1

    def total(terms):
        s = terms[0].astype(f32)
        for t in terms[1:]:
            s = s + t.astype(f32)
        return s.astype(bf16)

    def cube_parts(a, b):
        n = a.shape[1] // 4

        def part(m):
            quarter = (y ^ ((m >> 1) & 1)) * 2 + (z ^ (m >> 2))
            return total([lax.dynamic_slice(t, (m & 1, quarter * n, 0), (1, n, D))[0] for t in (a, b)])

        return tuple(part(m) for m in range(8))

    def crossing(parts, which):
        return tuple(swap(part, 2 * (m & 1), m >> 1) for part, m in zip(parts, which))

    def square_parts(a, b):
        h = a.shape[1] // 2

        def part(m):
            first = (y ^ (m >> 1)) * h
            return total([lax.dynamic_slice(t, (m & 1, first, 0), (1, h, D))[0] for t in (a, b)])

        return tuple(part(m) for m in range(4))

    def half_parts(terms):
        n = terms[0].shape[0] // 2
        return tuple(total([lax.dynamic_slice(t, ((z ^ m) * n, 0), (n, D)) for t in terms]) for m in (0, 1))

    def rest(s):
        for b in range(3, bits):
            s = total([s, swap(s, 0, 1 << b)])
        return s

    args = (k, v, d_ctx, log_total, delta, mask, cos, sin)
    gb_in = swap(gb, 1)
    first = attend_back_part((q,) + args, 0, 1)
    partsa = cube_parts(*tie((ga, gb_in), first[0]))
    one = crossing([partsa[m] for m in (1, 2, 4, 7)], (1, 2, 4, 7))
    second = attend_back_part((after(q, *partsa),) + args, 1, 2)
    one = tie(one, second[0])
    later = tie([partsa[m] for m in (3, 5, 6)], *one)
    two = crossing(later, (3, 5, 6))
    dq, dk, dv, ha, hb = attend_back(
        (after(q, *later),) + args, first, second, normed, wt, rows, vec_g, upb_g
    )
    parta = total((partsa[0],) + one + tie(two, dq))
    parta_in = swap(parta, 0, 4)
    hb_in = swap(after(hb, parta), 1)
    partsb = square_parts(ha, hb_in)
    squareb = partsb[0:1] + crossing(partsb[1:], (1, 2, 3))
    dn0, dnx, dnb = rows_back(after(dq, *partsb), dk, dv, wt)
    keepb, sendb = half_parts(tie(squareb, dn0))
    sendb_in = swap(sendb, 0, 2)
    suma = rest(total([parta, after(parta_in, sendb)]))
    alla = (suma,) + tuple(swap(suma, 0, m) for m in (1, 2, 3))
    core = swap(after(dnb, suma), 1)
    d_sum = total([dnx, core[1]])
    across = swap(d_sum, 2)
    partb = total([keepb, after(sendb_in, d_sum)])
    partb_in = swap(partb, 0, 4)
    out = output(quarters, after(act, partb), mid, rows, downs)
    sumb = rest(total([partb, after(partb_in, out)]))
    alla = tie(alla, sumb)
    sumb = after(sumb, *alla)
    allb = (sumb,) + tuple(swap(sumb, 0, m) for m in (1, 2, 3))
    g_down, g_up, g_out = place_call(place_a_kernel, alla, ((D, D), (D, D), (OW, D)), GA)
    grad_tok = finish(quarters, tok, rows, after(dn0, g_down), core, across, d_mid)
    g_qkv, g_bias, g_upb, *six = place_call(
        place_b_kernel, tie(allb, grad_tok), ((QW, D), (QW,), (D,)) + ((OW,),) * 6, GB
    )

    return (
        out[None], grad_tok[None], g_qkv.T, g_bias, g_out.T, six[0], six[1], six[2], six[3], six[4],
        g_up, g_upb, g_down, six[5],
    )


def solution(mesh):
    rows, vector = P("dp", "seq", None), P("seq")
    columns = P(None, "seq")
    return jax.shard_map(
        functools.partial(local, n_dp=mesh.shape["dp"]),
        mesh=mesh,
        in_specs=(rows, rows, P("dp", None), columns, vector, columns, vector, vector, vector, vector, vector,
                  columns, vector, P("seq", None), vector),
        out_specs=(rows, rows, columns, vector, columns, vector, vector, vector, vector, vector,
                   columns, vector, P("seq", None), vector),
        check_vma=False,
    )
```

```python
import functools
import math

import jax
import jax.numpy as jnp
import numpy as np
from jax import lax
from jax.experimental import pallas as pl
from jax.experimental.pallas import tpu as pltpu
from jax.sharding import PartitionSpec as P

HEADS = 20
HEAD_DIM = 32
HALF = 16
D = 640
FF = 2560
ROWS = 512
SEG = 256
QW = 480
OW = 160
EPS = 1e-05
SCALE = 1.0 / math.sqrt(HEAD_DIM)
SCALE2 = SCALE * math.log2(math.e)

bf16 = jnp.bfloat16
f32 = jnp.float32

NN = (((1,), (0,)), ((), ()))
NT = (((1,), (1,)), ((), ()))
TN = (((0,), (0,)), ((), ()))
TT = (((0,), (1,)), ((), ()))

VMEM = pl.BlockSpec(memory_space=pltpu.VMEM)
SMEM = pl.BlockSpec(memory_space=pltpu.SMEM)
ANY = pl.BlockSpec(memory_space=pl.ANY)
SHORT = pl.CostEstimate(flops=10**6, bytes_accessed=10**5, transcendentals=0)


def vmem(mebibytes):
    return pltpu.CompilerParams(vmem_limit_bytes=mebibytes * 2**20)


def dot(a, b, dims):
    return lax.dot_general(a, b, dims, preferred_element_type=f32)


def normalize(x):
    center = x - jnp.mean(x, axis=-1, keepdims=True)
    spread = jnp.mean(center * center, axis=-1, keepdims=True)
    rstd = lax.rsqrt(spread + EPS)
    return center * rstd, rstd


def first_row(quarters):
    start = jnp.int32(0)
    before = jnp.int32(0)
    for c in range(4):
        size = quarters[0, c]
        start = jnp.where(size == SEG, before, start)
        before = before + size
    return start


def rolled(ref, start):
    return pltpu.roll(ref[...].astype(f32), ROWS - start, 0)


def tables_kernel(quarters, freqs, cos, sin, mask):
    pos = lax.axis_index("seq")
    start = first_row(quarters)

    def crops(shape, dim, first):
        row = (lax.broadcasted_iota(jnp.int32, shape, dim) + (first + start)) % ROWS
        end = jnp.int32(0)
        crop = jnp.zeros(shape, jnp.int32)
        offset, length = crop, crop
        for c in range(4):
            size = quarters[0, c]
            begin, end = end, end + size
            crop = crop + (row >= end).astype(jnp.int32)
            inside = jnp.logical_and(row >= begin, row < end)
            offset = jnp.where(inside, begin, offset)
            length = jnp.where(inside, size, length)
        return crop, row - offset, length

    _, place, length = crops((HALF, ROWS), 1, 0)
    for p in range(4):
        angles = ((pos ^ p) * length + place).astype(f32) * freqs[...][:, 0:1]
        cos[p] = jnp.cos(angles)
        sin[p] = jnp.sin(angles)
    down = crops((SEG, SEG), 0, SEG)[0]
    along = crops((SEG, SEG), 1, SEG)[0]
    mask[...] = jnp.where(down == along, 0.0, -1e30)


def tables(quarters):
    freqs = np.float32(10000.0) ** (-np.arange(0, HEAD_DIM, 2).astype(np.float32) / np.float32(HEAD_DIM))
    table = jax.ShapeDtypeStruct((4, HALF, ROWS), f32)
    return pl.pallas_call(
        tables_kernel,
        in_specs=[SMEM, VMEM],
        out_specs=[VMEM] * 3,
        out_shape=[table, table, jax.ShapeDtypeStruct((SEG, SEG), f32)],
        compiler_params=vmem(60),
    )(quarters, jnp.asarray(np.repeat(freqs[:, None], 128, axis=1)))


def project_rows(p, x, wt, column, gain, shift, cos, sin, q_out, k_out, v_out, n_out):
    xhat, _ = normalize(x)
    normed = (xhat * gain + shift).astype(bf16)
    n_out[p] = normed
    for part in range(0 if q_out is not None else 1, 3):
        rows = slice(D * part, D * part + D)
        y = dot(wt[rows, :], normed, NT) + column[rows]
        if part == 2:
            v_out[p] = y.astype(bf16)
            continue
        c, s = cos[p], sin[p]
        for h in range(HEADS):
            a = y[32 * h : 32 * h + 16]
            b = y[32 * h + 16 : 32 * h + 32]
            r = jnp.concatenate([a * c - b * s, b * c + a * s], axis=0).astype(bf16)
            if part == 0:
                q_out[32 * h : 32 * h + 32, :] = r
            else:
                k_out[p, 32 * h : 32 * h + 32, :] = r


WPART = 512
PART = WPART // 4
PACK = WPART + ROWS


def pack_kernel(*refs):
    w, tok, out, part = refs[0], refs[1], refs[10], refs[11]
    out[0:QW, :] = w[...]
    out[WPART:PACK, :] = tok[...]
    rows = []
    for v in refs[2:10]:
        n = v.shape[0]
        row = v[...].astype(f32).reshape(1, n)
        rows.append(row if n == D else jnp.concatenate([row, jnp.zeros((1, D - n), f32)], axis=1))
    rows.append(jnp.zeros((WPART - QW - 8, D), f32))
    out[QW:WPART, :] = jnp.concatenate(rows, axis=0).astype(bf16)
    which = lax.axis_index("dp") & 3
    part[...] = out[pl.ds(pl.multiple_of(which * PART, PART), PART), :]


def pack(w, tok, vectors):
    return pl.pallas_call(
        pack_kernel,
        in_specs=[VMEM] * 10,
        out_specs=[VMEM] * 2,
        out_shape=[jax.ShapeDtypeStruct((PACK, D), bf16), jax.ShapeDtypeStruct((PART, D), bf16)],
        compiler_params=vmem(60),
        cost_estimate=SHORT,
    )(w, tok, *vectors)


def project_kernel(
    quarters, own, near, tok_far, tok_last, far0, far1, far2, last0, last1, last2, cos, sin,
    q_to, k_to, v_to, n_to, wt_to, rows_out, upb_out,
    q_out, k_out, v_out, n_out, wt, vt, col, w_far, w_last, sems,
):
    pos = lax.axis_index("seq")
    which = lax.axis_index("dp") & 3
    start = first_row(quarters)
    for whole, p0, p1, p2 in ((w_far, far0, far1, far2), (w_last, last0, last1, last2)):
        pieces = (p0[...], p1[...], p2[0:PART, :], p2[PART : 2 * PART, :])
        for i, piece in enumerate(pieces):
            whole[pl.ds(pl.multiple_of((which ^ i) * PART, PART), PART), :] = piece
    for p, m in enumerate((own, near, w_far, w_last)):
        wt[pl.ds(QW * (pos ^ p), QW), :] = m[0:QW, :]
        v = m[QW : QW + 16, :].astype(f32)[0:8]
        t = v.T
        col[pl.ds(QW * (pos ^ p), QW), :] = t[0:QW]
        vt[pl.ds(OW * (pos ^ p), OW), :] = t[0:OW]
        upb_out[p : p + 1, :] = v[7:8, :]
    sends = []

    def send(source, to):
        copy = pltpu.make_async_copy(source, to, sems.at[len(sends)])
        copy.start()
        sends.append(copy)

    send(wt, wt_to)
    rows = vt[...].T
    rows_out[...] = rows
    column = col[:, 0:1]
    gain, shift = rows[2:3], rows[3:4]
    toks = (own.at[pl.ds(WPART, ROWS), :], near.at[pl.ds(WPART, ROWS), :], tok_far, tok_last)
    for p, tok in enumerate(toks):
        project_rows(
            p, rolled(tok, start), wt, column, gain, shift, cos, sin,
            q_out if p == 0 else None, k_out, v_out, n_out,
        )
        if p == 0:
            send(q_out, q_to)
        for source, to in ((k_out, k_to), (v_out, v_to), (n_out, n_to)):
            send(source.at[p], to.at[p])
    for copy in sends:
        copy.wait()


def project(quarters, parts, cos, sin):
    sds = jax.ShapeDtypeStruct
    kv = sds((4, D, ROWS), bf16)
    return pl.pallas_call(
        project_kernel,
        in_specs=[SMEM] + [VMEM] * 12,
        out_specs=[ANY] * 5 + [VMEM] * 2,
        out_shape=[
            sds((D, ROWS), bf16), kv, kv, sds((4, ROWS, D), bf16), sds((3 * D, D), bf16),
            sds((8, D), f32), sds((4, D), f32),
        ],
        scratch_shapes=[
            pltpu.VMEM((D, ROWS), bf16), pltpu.VMEM((4, D, ROWS), bf16), pltpu.VMEM((4, D, ROWS), bf16),
            pltpu.VMEM((4, ROWS, D), bf16), pltpu.VMEM((3 * D, D), bf16),
            pltpu.VMEM((D, 8), f32), pltpu.VMEM((3 * D, 8), f32),
            pltpu.VMEM((WPART, D), bf16), pltpu.VMEM((WPART, D), bf16), pltpu.SemaphoreType.DMA((14,)),
        ],
        compiler_params=vmem(60),
        cost_estimate=SHORT,
    )(quarters, *parts, cos, sin)


def attend_kernel(q_ref, k_ref, v_ref, mask_ref, o_ref, l_ref, *, heads):
    ones = jnp.ones((HALF, SEG), bf16)
    for h in range(heads):
        hs = slice(32 * h, 32 * h + 32)
        for seg in range(2):
            cs = slice(SEG * seg, SEG * seg + SEG)
            q = q_ref[hs, cs].T
            scores = []
            for p in range(4):
                s = dot(q, k_ref[p, hs, cs], NN)
                if seg == 1:
                    s = s + mask_ref[...]
                scores.append(s)
            top = scores[0]
            for s in scores[1:]:
                top = jnp.maximum(top, s)
            top = top.max(1, keepdims=True)
            acc = None
            for p in range(4):
                e = jnp.exp2((scores[p] - top) * SCALE2).astype(bf16)
                t = dot(e, jnp.concatenate([v_ref[p, hs, cs], ones], axis=0), NT)
                acc = t if acc is None else acc + t
            total = acc[:, HEAD_DIM : HEAD_DIM + 1]
            o_ref[hs, cs] = (acc[:, 0:HEAD_DIM] / total).T
            log_total = top * SCALE2 + jnp.log2(total)
            l_ref[h, :, cs] = jnp.broadcast_to(log_total, (SEG, 128)).T[0:1]


def attend(q, k, v, mask):
    heads = 5
    row = pl.BlockSpec((32 * heads, ROWS), lambda h: (h, 0))
    four = pl.BlockSpec((4, 32 * heads, ROWS), lambda h: (0, h, 0))
    return pl.pallas_call(
        functools.partial(attend_kernel, heads=heads),
        grid=(HEADS // heads,),
        in_specs=[row, four, four, pl.BlockSpec((SEG, SEG), lambda h: (0, 0))],
        out_specs=[row, pl.BlockSpec((heads, 1, ROWS), lambda h: (h, 0, 0))],
        out_shape=[
            jax.ShapeDtypeStruct((D, ROWS), f32),
            jax.ShapeDtypeStruct((HEADS, 1, ROWS), f32),
        ],
        compiler_params=vmem(60),
        cost_estimate=SHORT,
    )(q, k, v, mask)


GA = 1472
HD = 320


def middle_kernel(
    quarters, ctx_ref, tok, cot, wo0, wo1, wo2, wo3, vec, upb,
    up0, up1, up2, up3, dn0, dn1, dn2, dn3, dq2, dq3,
    dmid_ref, dctx_ref, delta_ref, vecg_ref, upbg_ref, act_to, mid_to, ga, gb,
    up_s, dn_s, wo_s, mid_s, n2_s, n2t_s, cot_s, act_s, dn2_s, g_s, go_s, goo_s, sems, out_sems,
):
    pos = lax.axis_index("seq")
    start = first_row(quarters)
    copies = []
    half = lax.axis_index("dp") & 1
    for p, (u, d) in enumerate(((up0, dn0), (up1, dn1), (up2, dn2), (up3, dn3))):
        copies.append(pltpu.make_async_copy(u, up_s.at[p], sems.at[3 * p]))
        if p < 2:
            copies.append(pltpu.make_async_copy(d, dn_s.at[p], sems.at[3 * p + 1]))
            continue
        for i, h in enumerate((d, (dq2, dq3)[p - 2])):
            to = dn_s.at[p, pl.ds(pl.multiple_of(HD * (half ^ i), HD), HD), :]
            copies.append(pltpu.make_async_copy(h, to, sems.at[3 * p + 1 + i]))
    for c in copies:
        c.start()
    for p, wo in enumerate((wo0, wo1, wo2, wo3)):
        wo_s[pl.ds(OW * (pos ^ p), OW), :] = wo[...]
    ctx_low = ctx_ref[...].astype(bf16)
    out_bias, gain, shift = (vec[i : i + 1, :] for i in (1, 4, 5))
    mid = rolled(tok, start) + dot(wo_s[...], ctx_low, NN).T + out_bias
    mid_s[...] = mid
    kept = [pltpu.make_async_copy(mid_s, mid_to, out_sems.at[8])]
    kept[0].start()
    xhat, rstd = normalize(mid)
    normed2 = (xhat * gain + shift).astype(bf16)
    n2_s[...] = normed2
    n2t_s[...] = normed2.T
    cot_s[...] = rolled(cot, start).astype(bf16)
    dn2_s[...] = jnp.zeros_like(dn2_s)
    for c in copies:
        c.wait()

    sends = []

    def send(p, source, first, count, slot):
        to = (ga, gb)[p % 2].at[p // 2, pl.ds(first, count), :]
        copy = pltpu.make_async_copy(source, to, out_sems.at[slot])
        copy.start()
        sends.append(copy)

    def piece(p, carry):
        pre = dot(n2_s[...], up_s[p], NN) + upb[pl.ds(p, 1), :]
        d_act = dot(cot_s[...], dn_s[p], NT)
        cdf = 0.5 + 0.5 * lax.erf(pre * (1.0 / math.sqrt(2.0)))
        pdf = jnp.exp(-0.5 * pre * pre) * (1.0 / math.sqrt(2.0 * math.pi))
        act = (pre * cdf).astype(bf16)
        d_pre = (d_act * (cdf + pre * pdf)).astype(bf16)
        act_s[p] = act
        dn2_s[...] += dot(d_pre, up_s[p], NT)
        g_s[p, 0:D, :] = dot(act, cot_s[...], TN).astype(bf16)
        g_s[p, D : 2 * D, :] = dot(n2t_s[...], d_pre, NN).astype(bf16)
        upbg_ref[pl.ds(p, 1), :] = jnp.sum(d_pre.astype(f32), axis=0, keepdims=True)
        return carry

    lax.fori_loop(0, 4, piece, 0)
    for p in range(4):
        send(p, g_s.at[p], 0, 2 * D, p)

    kept.append(pltpu.make_async_copy(act_s, act_to, out_sems.at[9]))
    kept[1].start()
    xhat, rstd = normalize(mid_s[...])
    d_n2 = dn2_s[...]
    e = d_n2 * gain
    d_cot = cot_s[...].astype(f32)
    d_mid = d_cot + rstd * (
        e - jnp.mean(e, axis=-1, keepdims=True) - xhat * jnp.mean(e * xhat, axis=-1, keepdims=True)
    )
    dmid_ref[...] = d_mid
    d_attn = d_mid.astype(bf16)
    vecg_ref[0:1, :] = jnp.sum(d_attn.astype(f32), axis=0, keepdims=True)
    vecg_ref[1:3, :] = jnp.zeros((2, D), f32)
    vecg_ref[3:4, :] = jnp.sum(d_n2 * xhat, axis=0, keepdims=True)
    vecg_ref[4:5, :] = jnp.sum(d_n2, axis=0, keepdims=True)
    vecg_ref[5:6, :] = jnp.sum(d_cot, axis=0, keepdims=True)
    vecg_ref[6:8, :] = jnp.zeros((2, D), f32)
    d_attn_t = d_attn.T
    go_s[...] = dot(d_attn_t, ctx_ref[...].astype(bf16), NT).astype(bf16)
    for p in range(4):
        goo_s[p, 0:OW, :] = go_s[pl.ds(OW * (pos ^ p), OW), :]
        goo_s[p, OW:, :] = jnp.zeros((GA - 2 * D - OW, D), bf16)
        send(p, goo_s.at[p], 2 * D, GA - 2 * D, 4 + p)
    d_ctx = dot(wo_s[...], d_attn_t, TN).astype(bf16)
    dctx_ref[...] = d_ctx
    product = d_ctx.astype(f32) * ctx_ref[...]
    for h in range(HEADS):
        delta_ref[h] = jnp.sum(product[32 * h : 32 * h + 32], axis=0, keepdims=True)
    for copy in sends + kept:
        copy.wait()


def middle(quarters, ctx, tok, cot, wos, vec, upb, ups, downs):
    sds = jax.ShapeDtypeStruct
    big = sds((2, GA, D), bf16)
    return pl.pallas_call(
        middle_kernel,
        in_specs=[SMEM] + [VMEM] * 9 + [ANY] * 10,
        out_specs=[VMEM] * 5 + [ANY] * 4,
        out_shape=[
            sds((ROWS, D), f32), sds((D, ROWS), bf16), sds((HEADS, 1, ROWS), f32),
            sds((8, D), f32), sds((4, D), f32), sds((4, ROWS, D), bf16), sds((ROWS, D), f32), big, big,
        ],
        scratch_shapes=[
            pltpu.VMEM((4, D, D), bf16), pltpu.VMEM((4, D, D), bf16), pltpu.VMEM((D, D), bf16),
            pltpu.VMEM((ROWS, D), f32), pltpu.VMEM((ROWS, D), bf16), pltpu.VMEM((D, ROWS), bf16),
            pltpu.VMEM((ROWS, D), bf16), pltpu.VMEM((4, ROWS, D), bf16), pltpu.VMEM((ROWS, D), f32),
            pltpu.VMEM((4, 2 * D, D), bf16), pltpu.VMEM((D, D), bf16),
            pltpu.VMEM((4, GA - 2 * D, D), bf16),
            pltpu.SemaphoreType.DMA((12,)), pltpu.SemaphoreType.DMA((10,)),
        ],
        compiler_params=vmem(58),
        cost_estimate=SHORT,
    )(quarters, ctx, tok, cot, *wos, vec, upb, *ups, *downs)


def output_kernel(quarters, act, mid, vec, dn0, dn1, dn2, dn3, dq2, dq3, out, dn_s, sems):
    half = lax.axis_index("dp") & 1
    copies = []
    for p, d in enumerate((dn0, dn1)):
        copies.append(pltpu.make_async_copy(d, dn_s.at[p], sems.at[p]))
    for p, pair in ((2, (dn2, dq2)), (3, (dn3, dq3))):
        for i, h in enumerate(pair):
            to = dn_s.at[p, pl.ds(pl.multiple_of(HD * (half ^ i), HD), HD), :]
            copies.append(pltpu.make_async_copy(h, to, sems.at[2 * p - 2 + i]))
    for c in copies:
        c.start()
    for c in copies:
        c.wait()
    total = mid[...] + vec[6:7, :]
    for p in range(4):
        total = total + dot(act[p], dn_s[p], NN)
    out[...] = pltpu.roll(total, first_row(quarters), 0).astype(bf16)


def output(quarters, act, mid, vec, downs):
    return pl.pallas_call(
        output_kernel,
        in_specs=[SMEM] + [VMEM] * 3 + [ANY] * 6,
        out_specs=VMEM,
        out_shape=jax.ShapeDtypeStruct((ROWS, D), bf16),
        scratch_shapes=[pltpu.VMEM((4, D, D), bf16), pltpu.SemaphoreType.DMA((6,))],
        compiler_params=vmem(60),
        cost_estimate=SHORT,
    )(quarters, act, mid, vec, *downs)


BLOCK = 5
WIDE = 32 * BLOCK


def attend_back_step(q_ref, k_ref, v_ref, do_ref, l_ref, dl_ref, mask_ref, cos_ref, sin_ref, dq_ref, dk_ref, dv_ref):
    def back(g, c, s):
        a, b = g[0:HALF], g[HALF : 2 * HALF]
        return jnp.concatenate([a * c + b * s, b * c - a * s], axis=0).astype(bf16)

    for h in range(BLOCK):
        hs = slice(32 * h, 32 * h + 32)
        for seg in range(2):
            cs = slice(SEG * seg, SEG * seg + SEG)
            q, d_o = q_ref[hs, cs], do_ref[hs, cs]
            log_total, delta = l_ref[h, :, cs], dl_ref[h, :, cs]
            d_q = None
            for p in range(4):
                k = k_ref[p, hs, cs]
                v = v_ref[p, hs, cs]
                s = dot(k, q, TN)
                if seg == 1:
                    s = s + mask_ref[...]
                e = jnp.exp2(s * SCALE2 - log_total)
                d_s = (e * (dot(v, d_o, TN) - delta)).astype(bf16)
                dv_ref[p, hs, cs] = dot(d_o, e.astype(bf16), NT).astype(bf16)
                d_k = dot(q, d_s, NT) * SCALE
                dk_ref[p, hs, cs] = back(d_k, cos_ref[p, :, cs], sin_ref[p, :, cs])
                t = dot(k, d_s, NN)
                d_q = t if d_q is None else d_q + t
            dq_ref[hs, cs] = back(d_q * SCALE, cos_ref[0, :, cs], sin_ref[0, :, cs])


def back_specs(block):
    row = pl.BlockSpec((WIDE, ROWS), lambda h: (block(h), 0))
    four = pl.BlockSpec((4, WIDE, ROWS), lambda h: (0, block(h), 0))
    stat = pl.BlockSpec((BLOCK, 1, ROWS), lambda h: (block(h), 0, 0))
    table = pl.BlockSpec((4, HALF, ROWS), lambda h: (0, 0, 0))
    mask = pl.BlockSpec((SEG, SEG), lambda h: (0, 0))
    return [row, four, four, row, stat, stat, mask, table, table]


def result_specs(block):
    row = pl.BlockSpec((WIDE, ROWS), lambda h: (block(h), 0))
    four = pl.BlockSpec((4, WIDE, ROWS), lambda h: (0, block(h), 0))
    return [row, four, four]


def attend_back_part(operands, first, count):
    four = jax.ShapeDtypeStruct((4, WIDE * count, ROWS), bf16)
    return pl.pallas_call(
        attend_back_step,
        grid=(count,),
        in_specs=back_specs(lambda h: h + first),
        out_specs=result_specs(lambda h: h),
        out_shape=[jax.ShapeDtypeStruct((WIDE * count, ROWS), bf16), four, four],
        compiler_params=vmem(60),
        cost_estimate=SHORT,
    )(*operands)


GB = 512


def attend_back_kernel(*refs):
    ins, first, second, (normed, wt, rows, vec_g, upb_g) = refs[0:9], refs[9:12], refs[12:15], refs[15:20]
    dq_ref, dk_ref, dv_ref, ga, gb = refs[20:25]
    g_s, b_s, v_s, o_s = refs[25:]
    step = pl.program_id(0)
    last = HEADS // BLOCK - 1
    outs = (dq_ref, dk_ref, dv_ref)

    @pl.when(step == 0)
    def _():
        for out, part in zip(outs, first):
            out[...] = part[...]

    @pl.when(jnp.logical_and(step > 0, step < last))
    def _():
        for out, part in zip(outs, second):
            out[...] = part[...]

    @pl.when(step == last)
    def _():
        attend_back_step(*ins, *outs)

    row = pl.multiple_of(step * WIDE, WIDE)
    g_s[pl.ds(row, WIDE), :] = dot(dq_ref[...], normed[0], NN)
    total = jnp.sum(dq_ref[...].astype(f32), axis=1, keepdims=True)
    b_s[pl.ds(row, WIDE), :] = jnp.broadcast_to(total, (WIDE, 8))
    for part, ref in ((1, dk_ref), (2, dv_ref)):
        g = b = None
        for p in range(4):
            t = dot(ref[p], normed[p], NN)
            u = ref[p].astype(f32)
            g = t if g is None else g + t
            b = u if b is None else b + u
        g_s[pl.ds(D * part + row, WIDE), :] = g
        total = jnp.sum(b, axis=1, keepdims=True)
        b_s[pl.ds(D * part + row, WIDE), :] = jnp.broadcast_to(total, (WIDE, 8))

    @pl.when(step == last)
    def _():
        pos = lax.axis_index("seq")
        w = wt[...].astype(f32)
        both = jnp.sum(w * g_s[...], axis=0, keepdims=True)
        shift_g = jnp.sum(w * b_s[:, 0:1], axis=0, keepdims=True)
        gain_g = (both - rows[3:4, :] * shift_g) / rows[2:3, :]
        v_s[...] = jnp.concatenate([vec_g[0:1, :], gain_g, shift_g, vec_g[3:8, :]], axis=0).T
        o_s[...] = jnp.zeros_like(o_s)
        for p in range(4):
            out = (ga, gb)[p % 2]
            own = pos ^ p
            out[p // 2, 0:QW, :] = g_s[pl.ds(QW * own, QW), :].astype(bf16)
            o_s[0:8, 0:OW] = v_s[pl.ds(OW * own, OW), :].T
            o_s[8:16, 0:QW] = b_s[pl.ds(QW * own, QW), :].T
            o_s[16:24, :] = jnp.broadcast_to(upb_g[p : p + 1, :], (8, D))
            out[p // 2, QW:GB, :] = o_s[...].astype(bf16)


def attend_back(operands, first, second, normed, wt, rows, vec_g, upb_g):
    steps = HEADS // BLOCK

    def whole(*shape):
        return pl.BlockSpec(shape, lambda h: (0,) * len(shape))

    four = jax.ShapeDtypeStruct((4, D, ROWS), bf16)
    block = jax.ShapeDtypeStruct((2, GB, D), bf16)
    return pl.pallas_call(
        attend_back_kernel,
        grid=(steps,),
        in_specs=back_specs(lambda h: steps - 1)
        + result_specs(lambda h: 0)
        + result_specs(lambda h: jnp.clip(h - 1, 0, steps - 3))
        + [whole(4, ROWS, D), whole(3 * D, D), whole(8, D), whole(8, D), whole(4, D)],
        out_specs=result_specs(lambda h: h) + [whole(2, GB, D), whole(2, GB, D)],
        out_shape=[jax.ShapeDtypeStruct((D, ROWS), bf16), four, four, block, block],
        scratch_shapes=[
            pltpu.VMEM((3 * D, D), f32), pltpu.VMEM((3 * D, 8), f32), pltpu.VMEM((D, 8), f32), pltpu.VMEM((32, D), f32),
        ],
        compiler_params=vmem(60),
        cost_estimate=SHORT,
    )(*operands, *first, *second, normed, wt, rows, vec_g, upb_g)


def rows_back_kernel(dq, dk, dv, wt, dn0, dnx, dnb):
    for p, out in ((1, dnb.at[0]), (3, dnb.at[1]), (2, dnx), (0, dn0)):
        d_n = dot(dk[p], wt[D : 2 * D, :], TN) + dot(dv[p], wt[2 * D : 3 * D, :], TN)
        if p == 0:
            d_n = d_n + dot(dq[...], wt[0:D, :], TN)
        out[...] = d_n.astype(bf16)


def rows_back(dq, dk, dv, wt):
    rows = jax.ShapeDtypeStruct((ROWS, D), bf16)
    return pl.pallas_call(
        rows_back_kernel,
        in_specs=[VMEM] * 4,
        out_specs=[VMEM] * 3,
        out_shape=[rows, rows, jax.ShapeDtypeStruct((2, ROWS, D), bf16)],
        compiler_params=vmem(60),
        cost_estimate=SHORT,
    )(dq, dk, dv, wt)


def finish_kernel(quarters, tok, rows, own, core, across, d_mid, out):
    start = first_row(quarters)
    xhat, rstd = normalize(rolled(tok, start))
    d_n = own[...].astype(f32) + core[0].astype(f32) + across[...].astype(f32)
    e = d_n * rows[2:3, :]
    grad = d_mid[...] + rstd * (
        e - jnp.mean(e, axis=-1, keepdims=True) - xhat * jnp.mean(e * xhat, axis=-1, keepdims=True)
    )
    out[...] = pltpu.roll(grad, start, 0)


def finish(quarters, tok, rows, own, core, across, d_mid):
    return pl.pallas_call(
        finish_kernel,
        in_specs=[SMEM] + [VMEM] * 6,
        out_specs=VMEM,
        out_shape=jax.ShapeDtypeStruct((ROWS, D), f32),
        compiler_params=vmem(16),
        cost_estimate=SHORT,
    )(quarters, tok, rows, own, core, across, d_mid)


def place(parts, total):
    group = lax.axis_index("dp")
    y, z = group & 1, (group >> 1) & 1
    for (my, mz), part in parts:
        n = part.shape[0]
        row = ((y ^ my) * 2 + (z ^ mz)) * n
        total[pl.ds(pl.multiple_of(row, 8), n), :] = part.astype(f32)


def place_a_kernel(*refs):
    down, up, out, total = refs[4:]
    place([((m & 1, m >> 1), ref[...]) for m, ref in enumerate(refs[:4])], total)
    down[...] = total[0:D, :]
    up[...] = total[D : 2 * D, :]
    out[...] = total[2 * D : 2 * D + OW, :]


def place_b_kernel(*refs):
    qkv, bias, upb, total = refs[4], refs[5], refs[6], refs[13]
    place([((m & 1, m >> 1), ref[...]) for m, ref in enumerate(refs[:4])], total)
    qkv[...] = total[0:QW, :]
    bias[...] = total[QW + 8, 0:QW]
    upb[...] = total[QW + 16, :]
    for i in range(6):
        refs[7 + i][...] = total[QW + i, 0:OW]


def place_call(kernel, parts, shapes, rows):
    return pl.pallas_call(
        kernel,
        in_specs=[VMEM] * len(parts),
        out_specs=[VMEM] * len(shapes),
        out_shape=[jax.ShapeDtypeStruct(s, f32) for s in shapes],
        scratch_shapes=[pltpu.VMEM((rows, D), f32)],
        compiler_params=vmem(24),
        cost_estimate=SHORT,
    )(*parts)


def tie(terms, *others):
    return lax.optimization_barrier((tuple(terms),) + others)[0]


def after(x, *others):
    return lax.optimization_barrier((x,) + others)[0]


def local(
    tokens, cotangent, quarters, qkv_weight, qkv_bias, out_weight, out_bias, attn_gain, attn_shift,
    ffn_gain, ffn_shift, up_weight, up_bias, down_weight, down_bias, *, n_dp,
):
    group = lax.axis_index("dp")

    def swap(x, seq_mask, dp_mask=0):
        pairs = []
        for s in range(4):
            for d in range(n_dp):
                pairs.append((s * n_dp + d, (s ^ seq_mask) * n_dp + (d ^ dp_mask)))
        return lax.ppermute(x, ("seq", "dp"), pairs)

    tok, cot = tokens[0], cotangent[0]
    vectors = (qkv_bias, out_bias, attn_gain, attn_shift, ffn_gain, ffn_shift, down_bias, up_bias)
    own, part = pack(qkv_weight.T, tok, vectors)
    far0 = swap(part, 2)
    near = swap(own, 1)
    tok_far = swap(after(tok, far0), 2)
    far1 = swap(far0, 0, 1)
    cos, sin, mask = tables(after(quarters, far0))
    far2 = swap(jnp.concatenate([after(far0, mask), far1]), 0, 2)
    last = [swap(x, 1) for x in (far0, far1, far2)]
    tok_last = swap(tok_far, 1)
    q, k, v, normed, wt, rows, upb = project(
        quarters, (own, near, tok_far, tok_last, far0, far1, far2, *last), cos, sin
    )
    half = lax.dynamic_slice_in_dim(down_weight, (group & 1) * HD, HD)
    wo, half = tie((out_weight.T, half), tok_far)
    wo_far, wo_near = swap(wo, 2), swap(wo, 1)
    dn_far, dn_near = swap(half, 2), swap(down_weight, 1)
    wo_far, dn_far = tie((wo_far, dn_far), q)
    wo_last, dn_last = swap(wo_far, 1), swap(dn_far, 1)
    dn_far2 = swap(dn_far, 0, 1)
    up_far, up_near = swap(after(up_weight, wo_far), 2), swap(up_weight, 1)
    ctx, log_total = attend(after(q, wo_far, dn_far), k, v, mask)
    up_far, dn_far2 = tie((up_far, dn_far2), log_total)
    up_last, dn_last2 = swap(up_far, 1), swap(dn_far2, 1)
    downs = (down_weight, dn_near, dn_far, dn_last, dn_far2, dn_last2)
    d_mid, d_ctx, delta, vec_g, upb_g, act, mid, ga, gb = middle(
        quarters, ctx, tok, cot, (out_weight.T, wo_near, wo_far, wo_last), rows, upb,
        (up_weight, up_near, up_far, up_last), downs,
    )

    bits = n_dp.bit_length() - 1
    y, z = group & 1, (group >> 1) & 1

    def total(terms):
        s = terms[0].astype(f32)
        for t in terms[1:]:
            s = s + t.astype(f32)
        return s.astype(bf16)

    def cube_parts(a, b):
        n = a.shape[1] // 4

        def part(m):
            quarter = (y ^ ((m >> 1) & 1)) * 2 + (z ^ (m >> 2))
            return total([lax.dynamic_slice(t, (m & 1, quarter * n, 0), (1, n, D))[0] for t in (a, b)])

        return tuple(part(m) for m in range(8))

    def crossing(parts, which):
        return tuple(swap(part, 2 * (m & 1), m >> 1) for part, m in zip(parts, which))

    def square_parts(a, b):
        h = a.shape[1] // 2

        def part(m):
            first = (y ^ (m >> 1)) * h
            return total([lax.dynamic_slice(t, (m & 1, first, 0), (1, h, D))[0] for t in (a, b)])

        return tuple(part(m) for m in range(4))

    def half_parts(terms):
        n = terms[0].shape[0] // 2
        return tuple(total([lax.dynamic_slice(t, ((z ^ m) * n, 0), (n, D)) for t in terms]) for m in (0, 1))

    def rest(s):
        for b in range(3, bits):
            s = total([s, swap(s, 0, 1 << b)])
        return s

    args = (k, v, d_ctx, log_total, delta, mask, cos, sin)
    gb_in = swap(gb, 1)
    first = attend_back_part((q,) + args, 0, 1)
    partsa = cube_parts(*tie((ga, gb_in), first[0]))
    one = crossing([partsa[m] for m in (1, 2, 4, 7)], (1, 2, 4, 7))
    second = attend_back_part((after(q, *partsa),) + args, 1, 2)
    one = tie(one, second[0])
    later = tie([partsa[m] for m in (3, 5, 6)], *one)
    two = crossing(later, (3, 5, 6))
    dq, dk, dv, ha, hb = attend_back(
        (after(q, *later),) + args, first, second, normed, wt, rows, vec_g, upb_g
    )
    parta = total((partsa[0],) + one + tie(two, dq))
    parta_in = swap(parta, 0, 4)
    hb_in = swap(after(hb, parta), 1)
    partsb = square_parts(ha, hb_in)
    squareb = partsb[0:1] + crossing(partsb[1:], (1, 2, 3))
    dn0, dnx, dnb = rows_back(after(dq, *partsb), dk, dv, wt)
    keepb, sendb = half_parts(tie(squareb, dn0))
    sendb_in = swap(sendb, 0, 2)
    suma = rest(total([parta, after(parta_in, sendb)]))
    alla = (suma,) + tuple(swap(suma, 0, m) for m in (1, 2, 3))
    core = swap(after(dnb, suma), 1)
    d_sum = total([dnx, core[1]])
    across = swap(d_sum, 2)
    partb = total([keepb, after(sendb_in, d_sum)])
    partb_in = swap(partb, 0, 4)
    out = output(quarters, after(act, partb), mid, rows, downs)
    sumb = rest(total([partb, after(partb_in, out)]))
    alla = tie(alla, sumb)
    sumb = after(sumb, across)
    allb = (sumb,) + tuple(swap(sumb, 0, m) for m in (1, 2, 3))
    g_down, g_up, g_out = place_call(place_a_kernel, alla, ((D, D), (D, D), (OW, D)), GA)
    grad_tok = finish(quarters, tok, rows, after(dn0, g_down), core, across, d_mid)
    g_qkv, g_bias, g_upb, *six = place_call(
        place_b_kernel, tie(allb, grad_tok), ((QW, D), (QW,), (D,)) + ((OW,),) * 6, GB
    )

    return (
        out[None], grad_tok[None], g_qkv.T, g_bias, g_out.T, six[0], six[1], six[2], six[3], six[4],
        g_up, g_upb, g_down, six[5],
    )


def solution(mesh):
    rows, vector = P("dp", "seq", None), P("seq")
    columns = P(None, "seq")
    return jax.shard_map(
        functools.partial(local, n_dp=mesh.shape["dp"]),
        mesh=mesh,
        in_specs=(rows, rows, P("dp", None), columns, vector, columns, vector, vector, vector, vector, vector,
                  columns, vector, P("seq", None), vector),
        out_specs=(rows, rows, columns, vector, columns, vector, vector, vector, vector, vector,
                   columns, vector, P("seq", None), vector),
        check_vma=False,
    )
```
